32 devices in a mesh: dp: 4 (over z), col: 8 (over y, x, core).
Axes of the slice: x: 2, y: 2, z: 4, core: 2. Of those that a mesh axis runs over, the one named last changes fastest.
Arguments:
- inputs: bfloat16 [4096, 768], P(('dp', 'col')), may hold values from -6 to 6
- gain_one: float32 [768], replicated, may hold values from 0.5 to 1.5
- shift_one: float32 [768], replicated, may hold values from -1.25 to 1.25
- w_qkv: bfloat16 [768, 2304], replicated, may hold values from -0.21875 to 0.21875
- bias_q: float32 [768], replicated, may hold values from -1.25 to 1.25
- bias_v: float32 [768], replicated, may hold values from -0.1875 to 0.1875
- w_out: bfloat16 [768, 768], replicated, may hold values from -3 to 3
- bias_out: float32 [768], replicated, may hold values from -1.25 to 1.25
- gain_two: float32 [768], replicated, may hold values from 0.5 to 1.5
- shift_two: float32 [768], replicated, may hold values from -1.25 to 1.25
- w_up: bfloat16 [768, 3072], replicated, may hold values from -0.21875 to 0.21875
- bias_up: float32 [3072], replicated, may hold values from -1.25 to 1.25
- w_down: bfloat16 [3072, 768], replicated, may hold values from -0.109375 to 0.109375
- bias_down: float32 [768], replicated, may hold values from -1.25 to 1.25
- lengths: int32 [4, 4], P('dp'), may hold values from 1 to 960, 1024 in all within a row
- cotangent: bfloat16 [4096, 768], P(('dp', 'col')), may hold values from -6 to 6
Outputs:
- layer_out: bfloat16 [4096, 768], P(('dp', 'col'))
- grad_inputs: bfloat16 [4096, 768], P(('dp', 'col'))
- grad_gain_one: float32 [768], P('col')
- grad_shift_one: float32 [768], P('col')
- grad_w_qkv: float32 [768, 2304], P('col')
- grad_bias_q: float32 [768], P('col')
- grad_bias_v: float32 [768], P('col')
- grad_w_out: float32 [768, 768], P('col')
- grad_bias_out: float32 [768], P('col')
- grad_gain_two: float32 [768], P('col')
- grad_shift_two: float32 [768], P('col')
- grad_w_up: float32 [768, 3072], P('col')
- grad_bias_up: float32 [3072], P('col')
- grad_w_down: float32 [3072, 768], P('col')
- grad_bias_down: float32 [768], P('col')
The draws below stay inside these ranges and needn't reach their ends.
Inputs may be any that keep to these rules, and one draw needn't show every extreme that they name: In each row the 4 lengths sum to 1024, and the longest is exactly 960.
All inputs are finite; a program needn't handle non-finite values.
Results may differ from the reference program's by a relative error of at most 0.022.
Values may be sent and summed in bfloat16 or wider, within the bound.
A program may use at most 256 MiB of HBM per device.

```python
import math
import jax
import jax.numpy as jnp
import numpy as np
from jax import lax

H = 12
HEAD = 64
D = 768
FF = 3072
TOK_DEV = 128
DOCS = 4
ROW_LEN = 1024
TOKENS = 4096
N_DP = 4


def strengthened(entries, stream_key, source, target, shards_of, factor):
    def block_of(dim):
        return (jnp.arange(entries.shape[dim]) // (entries.shape[dim] // shards_of)).reshape((-1,) + (1,) * (entries.ndim - 1 - dim))

    one_side = jax.random.permutation(stream_key, shards_of)[block_of(target)]
    other_side = (block_of(target) + shards_of // 2) % shards_of
    return jnp.where((block_of(source) == one_side) | (block_of(source) == other_side), factor * entries, entries)


def steps_of(key, extent, split, smallest, top_value):
    level, own = 1.0, jax.random.fold_in(key, 6)
    for axis_at, blocks in split:
        draws = jnp.exp(jax.random.uniform(jax.random.fold_in(own, axis_at), (blocks,), jnp.float32, smallest / len(split), top_value / len(split)))
        level = level * jnp.repeat(draws, extent[axis_at] // blocks).reshape([-1 if axis == axis_at else 1 for axis in range(len(extent))])
    return level


def profile(number_of, total, bound, slope):
    portions = [(1 << 20) // math.isqrt(rank ** slope) + 1 for rank in range(2, number_of + 1)]
    spare, given = total - bound - (number_of - 1), [1] * (number_of - 1)
    while spare > 0:
        free = [i for i in range(number_of - 1) if given[i] < bound]
        mass, left = sum([portions[i] for i in free]), spare
        for i in free:
            extra = min(bound - given[i], max(1, left * portions[i] // mass), spare)
            given[i] = given[i] + extra
            spare = spare - extra
    return np.array([bound] + given)


def uneven(key, count, total, reach, slope):
    if count == 2:
        one = jax.random.randint(key, (), max(1, total - reach), min(reach, total - 1) + 1)
        return jnp.stack([one, total - one])
    tallies = jnp.asarray(profile(count, total, reach, slope), jnp.int32)
    twos = (count - 1) // 2
    source_of, sink = tallies[1:1 + 2 * twos:2], tallies[2:2 + 2 * twos:2]
    room = jnp.minimum(source_of - 1, reach - sink)
    passed = jax.random.randint(jax.random.fold_in(key, 1), (twos,), 0, 1 << 20) % (room + 1)
    tallies = tallies.at[1:1 + 2 * twos:2].set(source_of - passed).at[2:2 + 2 * twos:2].set(sink + passed)
    return tallies[jax.random.permutation(jax.random.fold_in(key, 2), count)]


def gaussian(own_key, extent, deviation, most, shards=(), held_as=jnp.bfloat16):
    entries = jax.random.normal(own_key, extent, jnp.float32) * deviation
    if len(shards) > 0:
        entries = steps_of(own_key, extent, shards, -0.22, 0.18) * entries
    return jnp.clip(entries, min=-most, max=most).astype(held_as)


def gaussian_with(rng, shape, width, limit, split, heavy, held_as=jnp.bfloat16):
    drawn = width * jax.random.normal(rng, shape, jnp.float32)
    if split:
        drawn = drawn * steps_of(rng, shape, split, -0.22, 0.18)
    return jnp.clip(strengthened(drawn, jax.random.fold_in(rng, 3), *heavy), -limit, limit).astype(held_as)


def setup_inputs(seed: int = 0) -> dict:
    keys = jax.random.split(jax.random.key(seed), 17)
    inputs = gaussian(keys[0], (TOKENS, D), 1.0, 6.0, ((0, 32),))
    gain_one = jnp.clip(1.0 + 0.1 * jax.random.normal(keys[1], (D,), jnp.float32), 0.5, 1.5)
    shift_one = gaussian(keys[2], (D,), 0.2, 1.25, (), jnp.float32)
    w_qkv = gaussian(keys[3], (D, 3 * D), D ** -0.5, 0.21875)
    bias_q = gaussian(keys[4], (D,), 0.2, 1.25, (), jnp.float32)
    bias_v = gaussian(keys[5], (D,), 0.03, 0.1875, (), jnp.float32)
    w_out = gaussian(keys[6], (D, D), (4 * D // ROW_LEN + 1) ** -0.5, 3.0)
    bias_out = gaussian(keys[7], (D,), 0.2, 1.25, (), jnp.float32)
    gain_two = jnp.clip(1.0 + 0.1 * jax.random.normal(keys[8], (D,), jnp.float32), 0.5, 1.5)
    shift_two = gaussian(keys[9], (D,), 0.2, 1.25, (), jnp.float32)
    w_up = gaussian(keys[10], (D, FF), D ** -0.5, 0.21875)
    bias_up = gaussian(keys[11], (FF,), 0.2, 1.25, (), jnp.float32)
    w_down = gaussian(keys[12], (FF, D), FF ** -0.5, 0.109375)
    bias_down = gaussian(keys[13], (D,), 0.2, 1.25, (), jnp.float32)
    lengths = jax.vmap(lambda own: uneven(own, DOCS, ROW_LEN, ROW_LEN - TOK_DEV // 2, 0))(jax.random.split(keys[14], N_DP)).reshape((N_DP, DOCS)).astype(jnp.int32)
    cotangent = gaussian_with(keys[15], (TOKENS, D), 1.0, 6.0, ((0, 32),), (0, 1, 32, 2.75))
    return dict(inputs=inputs, gain_one=gain_one, shift_one=shift_one, w_qkv=w_qkv, bias_q=bias_q, bias_v=bias_v, w_out=w_out, bias_out=bias_out, gain_two=gain_two, shift_two=shift_two, w_up=w_up, bias_up=bias_up, w_down=w_down, bias_down=bias_down, lengths=lengths, cotangent=cotangent)


@jax.custom_vjp
def low(v):
    return lax.optimization_barrier(v.astype(jnp.bfloat16)).astype(jnp.float32)

@jax.custom_vjp
def low_back(v):
    return v

def low_keep(v):
    return (low(v), None)

def low_pass(kept, grad):
    return (grad,)

def back_keep(v):
    return (v, None)

def back_low(kept, grad):
    return (low(grad),)
low.defvjp(low_keep, low_pass)
low_back.defvjp(back_keep, back_low)
precise = lax.Precision.HIGHEST
epsilon = 1e-05

def layer_norm(values, scales, offset):
    average = lax.optimization_barrier(jnp.mean(values, axis=-1, keepdims=True))
    centered = values - average
    spread = lax.optimization_barrier(jnp.mean(centered * centered, axis=-1, keepdims=True))
    return centered * lax.rsqrt(spread + epsilon) * scales + offset

def documents(places, row_lengths):
    finish = jnp.cumsum(row_lengths).astype(jnp.int32)
    begins = (finish - row_lengths).astype(jnp.int32)
    inside = (places[:, None] >= begins[None, :]) & (places[:, None] < finish[None, :])
    numbers = jnp.arange(row_lengths.shape[0], dtype=jnp.int32)
    doc_index = lax.optimization_barrier(jnp.sum(jnp.where(inside, numbers[None, :], 0), axis=1)).astype(jnp.int32)
    first_place = lax.optimization_barrier(jnp.sum(jnp.where(inside, begins[None, :], 0), axis=1)).astype(jnp.int32)
    return (doc_index, first_place == places)

def attend_row(packed):
    queries, key_rows, value_rows, row_lengths = packed
    row_len = queries.shape[0]
    places = jnp.arange(row_len, dtype=jnp.int32)
    doc_index, first_flag = documents(places, row_lengths)
    block_rows = min(512, row_len)
    block_count = row_len // block_rows

    def one_block(carried, inputs_block):
        q_block, q_doc, q_places = inputs_block
        scores = low_back(jnp.einsum('qhd,khd->hqk', q_block, key_rows, precision=precise) * 0.125)
        allowed = (places[None, :] <= q_places[:, None]) & (doc_index[None, :] == q_doc[:, None])
        chosen = allowed & (places[None, :] < q_places[:, None]) & jnp.logical_not(first_flag)[None, :]
        picked = jnp.where(chosen, jax.nn.softplus(scores[0]), 0.0) / row_len
        forgot = carried[None, :] + jnp.cumsum(picked, axis=0) - picked
        logits = jnp.where(allowed[None], scores - forgot[None], -jnp.inf)
        row_top = lax.optimization_barrier(jnp.max(logits, axis=2, keepdims=True))
        raised = jnp.exp(logits - row_top)
        weights = raised / lax.optimization_barrier(jnp.sum(raised, axis=2, keepdims=True))
        mixed_rows = jnp.einsum('hqk,khd->qhd', low(weights), value_rows, precision=precise)
        return (carried + lax.optimization_barrier(jnp.sum(picked, axis=0)), mixed_rows)
    blocks = (queries.reshape(block_count, block_rows, H, HEAD), doc_index.reshape(block_count, block_rows), places.reshape(block_count, block_rows))
    unused, mixed_rows = lax.scan(jax.checkpoint(one_block), jnp.zeros((row_len,), jnp.float32), blocks)
    return mixed_rows.reshape(row_len, H * HEAD)

def forward(inputs, gain_one, shift_one, w_qkv, bias_q, bias_v, w_out, bias_out, gain_two, shift_two, w_up, bias_up, w_down, bias_down, lengths):
    model_width = inputs.shape[1]
    row_count = lengths.shape[0]
    normed_one = low(layer_norm(inputs, gain_one, shift_one))
    joined = jnp.dot(normed_one, w_qkv, precision=precise)
    queries = low_back(low(joined[:, :model_width] + bias_q))
    key_rows = low_back(low(joined[:, model_width:2 * model_width]))
    value_rows = low_back(low(joined[:, 2 * model_width:] + bias_v))
    shaped = (queries.reshape(row_count, -1, H, HEAD), key_rows.reshape(row_count, -1, H, HEAD), value_rows.reshape(row_count, -1, H, HEAD), lengths)
    attended = lax.map(attend_row, shaped).reshape(-1, model_width)
    attended_low = low_back(low(attended))
    middle = inputs + low_back(jnp.dot(attended_low, w_out, precision=precise)) + bias_out
    normed_two = low(layer_norm(middle, gain_two, shift_two))
    hidden = low_back(jnp.dot(normed_two, w_up, precision=precise) + bias_up)
    active = low(jax.nn.gelu(hidden))
    return middle + jnp.dot(active, w_down, precision=precise) + bias_down

def reference(inputs, gain_one, shift_one, w_qkv, bias_q, bias_v, w_out, bias_out, gain_two, shift_two, w_up, bias_up, w_down, bias_down, lengths, cotangent):
    floats = tuple((argument.astype(jnp.float32) for argument in (inputs, gain_one, shift_one, w_qkv, bias_q, bias_v, w_out, bias_out, gain_two, shift_two, w_up, bias_up, w_down, bias_down)))

    def wrapped(*params):
        return forward(*params, lengths)
    result, pullback = jax.vjp(wrapped, *floats)
    gradients = pullback(cotangent.astype(jnp.float32))
    return (result.astype(jnp.bfloat16), gradients[0].astype(jnp.bfloat16), gradients[1], gradients[2], gradients[3], gradients[4], gradients[5], gradients[6], gradients[7], gradients[8], gradients[9], gradients[10], gradients[11], gradients[12], gradients[13])
```

```python
import functools
import types

import jax
import jax.numpy as jnp
from jax import lax
from jax.experimental import pallas as pl
from jax.experimental.pallas import tpu as pltpu
from jax.sharding import PartitionSpec as P

H = 12
HEAD = 64


epsilon = 1e-05


def layer_norm(values, scales, offset):
    average = jnp.mean(values, axis=-1, keepdims=True)
    centered = values - average
    spread = jnp.mean(centered * centered, axis=-1, keepdims=True)
    return centered * lax.rsqrt(spread + epsilon) * scales + offset


def documents(places, row_lengths):
    finish = jnp.cumsum(row_lengths)
    begins = finish - row_lengths
    inside = (places[:, None] >= begins[None, :]) & (places[:, None] < finish[None, :])
    numbers = jnp.arange(row_lengths.shape[0], dtype=jnp.int32)
    doc_index = jnp.sum(jnp.where(inside, numbers[None, :], 0), axis=1)
    first_place = jnp.sum(jnp.where(inside, begins[None, :], 0), axis=1)
    return (doc_index, first_place == places)


def general_device(
    inputs,
    gain_one,
    shift_one,
    w_qkv,
    bias_q,
    bias_v,
    w_out,
    bias_out,
    gain_two,
    shift_two,
    w_up,
    bias_up,
    w_down,
    bias_down,
    lengths,
    cotangent,
):
    col_count = lax.axis_size("col")
    col_place = lax.axis_index("col")
    tok_rows = inputs.shape[0]
    model_width = inputs.shape[1]
    row_len = tok_rows * col_count
    block_rows = min(512, row_len)
    block_count = row_len // block_rows
    places = jnp.arange(row_len, dtype=jnp.int32)
    doc_index, first_flag = documents(places, lengths[0])
    own_first = col_place * tok_rows
    key_places = own_first + jnp.arange(tok_rows, dtype=jnp.int32)
    key_doc = lax.dynamic_slice_in_dim(doc_index, own_first, tok_rows, 0)
    key_first = lax.dynamic_slice_in_dim(first_flag, own_first, tok_rows, 0)
    floated = inputs.astype(jnp.float32)
    norm_first, first_back = jax.vjp(layer_norm, floated, gain_one, shift_one)
    normed_one = norm_first.astype(jnp.bfloat16)
    joined = jnp.dot(normed_one, w_qkv, preferred_element_type=jnp.float32)
    queries = (joined[:, :model_width] + bias_q).astype(jnp.bfloat16)
    key_rows = joined[:, model_width : 2 * model_width].astype(jnp.bfloat16)
    value_rows = (joined[:, 2 * model_width :] + bias_v).astype(jnp.bfloat16)
    key_heads = key_rows.reshape(tok_rows, H, HEAD)
    value_heads = value_rows.reshape(tok_rows, H, HEAD)
    all_queries = lax.all_gather(queries, "col", axis=0, tiled=True)

    def block_terms(source, block_index, carried):
        first_row = block_index * block_rows
        q_block = lax.dynamic_slice_in_dim(source, first_row, block_rows, 0).reshape(
            block_rows, H, HEAD
        )
        q_places = first_row + jnp.arange(block_rows, dtype=jnp.int32)
        q_doc = lax.dynamic_slice_in_dim(doc_index, first_row, block_rows, 0)
        scores = (
            jnp.einsum("khd,qhd->hkq", key_heads, q_block, preferred_element_type=jnp.float32)
            * 0.125
        )
        allowed = (key_places[:, None] <= q_places[None, :]) & (key_doc[:, None] == q_doc[None, :])
        chosen = (
            allowed
            & (key_places[:, None] < q_places[None, :])
            & jnp.logical_not(key_first)[:, None]
        )
        picked = jnp.where(chosen, jax.nn.softplus(scores[0]), 0.0) / row_len
        forgot = carried[:, None] + jnp.cumsum(picked, axis=1) - picked
        logits = jnp.where(allowed[None], scores - forgot[None], -jnp.inf)
        return (q_block, scores, chosen, picked, logits)

    def forward_block(carried, block_index):
        q_block, scores, chosen, picked, logits = block_terms(all_queries, block_index, carried)
        row_top = jnp.max(logits, axis=1)
        safe_top = jnp.where(row_top > -jnp.inf, row_top, 0.0)
        raised = jnp.exp(logits - safe_top[:, None, :])
        totals = jnp.sum(raised, axis=1)
        numerator = jnp.einsum(
            "hkq,khd->qhd",
            raised.astype(jnp.bfloat16),
            value_heads,
            preferred_element_type=jnp.float32,
        )
        return (
            carried + jnp.sum(picked, axis=1),
            (carried, row_top.T, totals.T, numerator.reshape(block_rows, model_width)),
        )

    indices = jnp.arange(block_count, dtype=jnp.int32)
    unused, (block_starts, row_tops, row_totals, numerators) = lax.scan(
        forward_block, jnp.zeros((tok_rows,), jnp.float32), indices
    )
    row_tops = row_tops.reshape(row_len, H)
    row_totals = row_totals.reshape(row_len, H)
    numerators = numerators.reshape(row_len, model_width)
    got_top, got_total, got_numer = (
        lax.all_to_all(
            row_tops[None].astype(jnp.bfloat16), "col", split_axis=1, concat_axis=0, tiled=True
        ).astype(jnp.float32),
        lax.all_to_all(
            row_totals[None].astype(jnp.bfloat16), "col", split_axis=1, concat_axis=0, tiled=True
        ).astype(jnp.float32),
        lax.all_to_all(
            numerators[None].astype(jnp.bfloat16), "col", split_axis=1, concat_axis=0, tiled=True
        ).astype(jnp.float32),
    )
    row_best = jnp.max(got_top, axis=0)
    factor = jnp.exp(got_top - row_best[None])
    totals_own = jnp.sum(factor * got_total, axis=0)
    numer_own = jnp.sum(got_numer.reshape(col_count, tok_rows, H, HEAD) * factor[..., None], axis=0)
    attended = (numer_own / totals_own[..., None]).reshape(tok_rows, model_width)
    row_lse = row_best + jnp.log(totals_own)
    attended_low = attended.astype(jnp.bfloat16)
    middle = floated + jnp.dot(attended_low, w_out, preferred_element_type=jnp.float32) + bias_out
    norm_second, second_back = jax.vjp(layer_norm, middle, gain_two, shift_two)
    normed_two = norm_second.astype(jnp.bfloat16)
    hidden = jnp.dot(normed_two, w_up, preferred_element_type=jnp.float32) + bias_up
    active_full, gelu_back = jax.vjp(jax.nn.gelu, hidden)
    active = active_full.astype(jnp.bfloat16)
    layer_out = (
        middle + jnp.dot(active, w_down, preferred_element_type=jnp.float32) + bias_down
    ).astype(jnp.bfloat16)
    d_output = cotangent.astype(jnp.float32)
    grad_w_down = jnp.einsum("tf,td->fd", active, cotangent, preferred_element_type=jnp.float32)
    grad_bias_down = jnp.sum(d_output, axis=0)
    d_active = jnp.einsum("td,fd->tf", cotangent, w_down, preferred_element_type=jnp.float32)
    d_hidden = gelu_back(d_active)[0].astype(jnp.bfloat16)
    grad_w_up = jnp.einsum("td,tf->df", normed_two, d_hidden, preferred_element_type=jnp.float32)
    grad_bias_up = jnp.sum(d_hidden.astype(jnp.float32), axis=0)
    d_normed_two = jnp.einsum("tf,df->td", d_hidden, w_up, preferred_element_type=jnp.float32)
    d_middle_norm, grad_gain_two, grad_shift_two = second_back(d_normed_two)
    d_middle = d_output + d_middle_norm
    d_branch = d_middle.astype(jnp.bfloat16)
    grad_w_out = jnp.einsum("td,te->de", attended_low, d_branch, preferred_element_type=jnp.float32)
    grad_bias_out = jnp.sum(d_middle, axis=0)
    d_attended = jnp.einsum(
        "te,de->td", d_branch, w_out, preferred_element_type=jnp.float32
    ).astype(jnp.bfloat16)
    row_delta = jnp.sum(
        (d_attended.astype(jnp.float32) * attended).reshape(tok_rows, H, HEAD), axis=2
    )
    back_queries, gathered_grad = (
        lax.all_gather(queries, "col", axis=0, tiled=True),
        lax.all_gather(d_attended, "col", axis=0, tiled=True),
    )
    all_lse, all_delta = (
        lax.all_gather(row_lse, "col", axis=0, tiled=True),
        lax.all_gather(row_delta, "col", axis=0, tiled=True),
    )

    def backward_block(carried_state, inputs_block):
        later_sum, key_grad, value_grad = carried_state
        block_index, carried = inputs_block
        q_block, scores, chosen, picked, logits = block_terms(back_queries, block_index, carried)
        first_row = block_index * block_rows
        grad_block = lax.dynamic_slice_in_dim(gathered_grad, first_row, block_rows, 0).reshape(
            block_rows, H, HEAD
        )
        lse_block = lax.dynamic_slice_in_dim(all_lse, first_row, block_rows, 0)
        delta_block = lax.dynamic_slice_in_dim(all_delta, first_row, block_rows, 0)
        weights = jnp.exp(logits - lse_block.T[:, None, :])
        value_grad = value_grad + jnp.einsum(
            "hkq,qhd->khd",
            weights.astype(jnp.bfloat16),
            grad_block,
            preferred_element_type=jnp.float32,
        )
        d_weights = jnp.einsum(
            "khd,qhd->hkq", value_heads, grad_block, preferred_element_type=jnp.float32
        )
        d_logits = weights * (d_weights - delta_block.T[:, None, :])
        d_forgot = -jnp.sum(d_logits, axis=0)
        block_sum = jnp.sum(d_forgot, axis=1)
        d_picked = later_sum[:, None] + block_sum[:, None] - jnp.cumsum(d_forgot, axis=1)
        d_select = jnp.where(chosen, jax.nn.sigmoid(scores[0]) * d_picked / row_len, 0.0)
        d_scores = d_logits.at[0].add(d_select).astype(jnp.bfloat16)
        key_grad = (
            key_grad
            + jnp.einsum("hkq,qhd->khd", d_scores, q_block, preferred_element_type=jnp.float32)
            * 0.125
        )
        query_grad = (
            jnp.einsum("hkq,khd->qhd", d_scores, key_heads, preferred_element_type=jnp.float32)
            * 0.125
        )
        return (
            (later_sum + block_sum, key_grad, value_grad),
            query_grad.reshape(block_rows, model_width),
        )

    zero_heads = jnp.zeros((tok_rows, H, HEAD), jnp.float32)
    initial = (jnp.zeros((tok_rows,), jnp.float32), zero_heads, zero_heads)
    (unused_sum, key_grad, value_grad), query_parts = lax.scan(
        backward_block, initial, (indices, block_starts), reverse=True
    )
    query_parts = query_parts.reshape(row_len, model_width)
    d_queries = lax.psum_scatter(query_parts, "col", scatter_dimension=0, tiled=True).astype(
        jnp.bfloat16
    )
    d_keys = key_grad.reshape(tok_rows, model_width).astype(jnp.bfloat16)
    d_values = value_grad.reshape(tok_rows, model_width).astype(jnp.bfloat16)
    d_joined = jnp.concatenate([d_queries, d_keys, d_values], axis=1)
    grad_w_qkv = jnp.einsum("td,te->de", normed_one, d_joined, preferred_element_type=jnp.float32)
    grad_bias_q = jnp.sum(d_queries.astype(jnp.float32), axis=0)
    grad_bias_v = jnp.sum(d_values.astype(jnp.float32), axis=0)
    d_normed_one = jnp.einsum("te,de->td", d_joined, w_qkv, preferred_element_type=jnp.float32)
    d_input_norm, grad_gain_one, grad_shift_one = first_back(d_normed_one)
    grad_inputs = (d_middle + d_input_norm).astype(jnp.bfloat16)
    (
        shard_gain_one,
        shard_shift_one,
        shard_w_qkv,
        shard_bias_q,
        shard_bias_v,
        shard_w_out,
        shard_bias_out,
        shard_gain_two,
        shard_shift_two,
        shard_w_up,
        shard_bias_up,
        shard_w_down,
        shard_bias_down,
    ) = (
        lax.psum_scatter(grad_gain_one, "col", scatter_dimension=0, tiled=True),
        lax.psum_scatter(grad_shift_one, "col", scatter_dimension=0, tiled=True),
        lax.psum_scatter(grad_w_qkv, "col", scatter_dimension=0, tiled=True),
        lax.psum_scatter(grad_bias_q, "col", scatter_dimension=0, tiled=True),
        lax.psum_scatter(grad_bias_v, "col", scatter_dimension=0, tiled=True),
        lax.psum_scatter(grad_w_out, "col", scatter_dimension=0, tiled=True),
        lax.psum_scatter(grad_bias_out, "col", scatter_dimension=0, tiled=True),
        lax.psum_scatter(grad_gain_two, "col", scatter_dimension=0, tiled=True),
        lax.psum_scatter(grad_shift_two, "col", scatter_dimension=0, tiled=True),
        lax.psum_scatter(grad_w_up, "col", scatter_dimension=0, tiled=True),
        lax.psum_scatter(grad_bias_up, "col", scatter_dimension=0, tiled=True),
        lax.psum_scatter(grad_w_down, "col", scatter_dimension=0, tiled=True),
        lax.psum_scatter(grad_bias_down, "col", scatter_dimension=0, tiled=True),
    )
    summed = (
        lax.psum(shard_gain_one.astype(jnp.bfloat16), "dp").astype(jnp.float32),
        lax.psum(shard_shift_one.astype(jnp.bfloat16), "dp").astype(jnp.float32),
        lax.psum(shard_w_qkv.astype(jnp.bfloat16), "dp").astype(jnp.float32),
        lax.psum(shard_bias_q.astype(jnp.bfloat16), "dp").astype(jnp.float32),
        lax.psum(shard_bias_v.astype(jnp.bfloat16), "dp").astype(jnp.float32),
        lax.psum(shard_w_out.astype(jnp.bfloat16), "dp").astype(jnp.float32),
        lax.psum(shard_bias_out.astype(jnp.bfloat16), "dp").astype(jnp.float32),
        lax.psum(shard_gain_two.astype(jnp.bfloat16), "dp").astype(jnp.float32),
        lax.psum(shard_shift_two.astype(jnp.bfloat16), "dp").astype(jnp.float32),
        lax.psum(shard_w_up.astype(jnp.bfloat16), "dp").astype(jnp.float32),
        lax.psum(shard_bias_up.astype(jnp.bfloat16), "dp").astype(jnp.float32),
        lax.psum(shard_w_down.astype(jnp.bfloat16), "dp").astype(jnp.float32),
        lax.psum(shard_bias_down.astype(jnp.bfloat16), "dp").astype(jnp.float32),
    )
    return (
        layer_out,
        grad_inputs,
        summed[0],
        summed[1],
        summed[2],
        summed[3],
        summed[4],
        summed[5],
        summed[6],
        summed[7],
        summed[8],
        summed[9],
        summed[10],
        summed[11],
        summed[12],
    )


MESH = pl.DeviceIdType.MESH
LOW = jnp.bfloat16
WIDE = jnp.float32
FAR = 1e30
ROW_UNITS = 12


def dot(a, b):
    return jnp.dot(a, b, preferred_element_type=WIDE)


def dot_rows(a, b):
    return lax.dot_general(a, b, (((1,), (1,)), ((), ())), preferred_element_type=WIDE)


def split_low(values):
    high = values.astype(LOW)
    return high, (values - high.astype(WIDE)).astype(LOW)


def norm_parts(values):
    average = jnp.mean(values, axis=-1, keepdims=True)
    centered = values - average
    spread = jnp.mean(centered * centered, axis=-1, keepdims=True)
    scale = lax.rsqrt(spread + epsilon)
    return centered * scale, scale


def norm_back(grad, unit, scale, gain):
    scaled = grad * gain
    first = jnp.mean(scaled, axis=-1, keepdims=True)
    second = jnp.mean(scaled * unit, axis=-1, keepdims=True)
    return scale * (scaled - first - unit * second)


SCRATCH = dict(
    wqkv=((768, 2304), LOW),
    wout=((768, 768), LOW),
    wup=((768, 3072), LOW),
    wdown=((32, 96, 768), LOW),
    kv=((3, 8, 2, 128, 256), LOW),
    turned=((6, 128, 1024), LOW),
    probs=((6, 1024, 256), LOW),
    sums=((8, 8, 128), WIDE),
    back_sums=((8, 8, 128), WIDE),
    forgot=((128, 1024), WIDE),
    forgot_t=((1024, 128), WIDE),
    sig_t=((1024, 128), WIDE),
    d_forgot_t=((1024, 128), WIDE),
    second_head=((1024, 128), LOW),
    q_low=((128, 768), LOW),
    q_turned=((768, 128), LOW),
    n1_t=((8, 96, 128), LOW),
    n2_t=((8, 96, 128), LOW),
    att_t=((768, 128), WIDE),
    att_low_t=((8, 96, 128), LOW),
    act=((128, 3072), LOW),
    act_t=((8, 4, 96, 128), LOW),
    d_act=((128, 3072), WIDE),
    middle=((128, 768), WIDE),
    d_mid=((128, 768), WIDE),
    unit_two=((128, 768), WIDE),
    d_att=((128, 768), LOW),
    d_att_t=((768, 128), LOW),
    dq_t=((768, 128), WIDE),
    cot2=((256, 768), LOW),
    dh2=((256, 3072), LOW),
    db2=((256, 768), LOW),
    dqkv2=((256, 2304), LOW),
    lhs_down=((4, 4, 96, 256), LOW),
    lhs_up=((4, 96, 256), LOW),
    lhs_out=((4, 96, 256), LOW),
    lhs_qkv=((4, 96, 256), LOW),
    give_down=((4, 4, 96, 128), LOW),
    give_up=((4, 96, 128), LOW),
    give_out=((4, 96, 128), LOW),
    give_qkv=((4, 96, 128), LOW),
    dkv=((3, 2, 2, 4, 128, 256), LOW),
    dkv_core=((3, 2, 4, 128, 256), LOW),
    dkv_one=((3, 2, 2, 128, 256), LOW),
    dkv_two=((3, 2, 128, 256), LOW),
    part=((4, 4, 96, 768), LOW),
    got_one=((ROW_UNITS, 2, 2, 96, 384), LOW),
    got_two=((ROW_UNITS, 2, 96, 384), LOW),
    mine=((ROW_UNITS, 2, 48, 768), LOW),
    got_z=((ROW_UNITS, 48, 768), LOW),
    got_zz=((ROW_UNITS, 48, 768), LOW),
    total=((ROW_UNITS, 2, 48, 768), LOW),
    small=((6, 8, 1152), WIDE),
    small_got=((5, 8, 1152), WIDE),
)


def layer_kernel(
    lengths_ref,
    x_ref,
    cot_ref,
    gain_one,
    shift_one,
    bias_q,
    bias_v,
    bias_out,
    gain_two,
    shift_two,
    bias_up,
    bias_down,
    w_qkv,
    w_out,
    w_up,
    w_down,
    out_ref,
    grad_ref,
    total_ref,
    small_ref,
    wide_ref,
    *scratch,
):
    s = types.SimpleNamespace(**dict(zip(SCRATCH, scratch)))
    sent, landed, local = scratch[len(SCRATCH) :]
    me = lax.axis_index("col")
    dp = lax.axis_index("dp")
    core = lax.rem(me, 2)
    x_bit = lax.rem(lax.div(me, 2), 2)
    y_bit = lax.div(me, 4)
    z_low = lax.rem(dp, 2)
    z_high = lax.div(dp, 2)

    def place(r):
        step = (r & 1) * (1 - 2 * core) + ((r >> 1) & 1) * (2 - 4 * x_bit)
        return me + step + (r >> 2) * (4 - 8 * y_bit)

    def near(r):
        return (dp, place(r))

    z_one = (dp + 1 - 2 * z_low, me)
    z_two = (dp + 2 - 4 * z_high, me)
    messages = []

    def send(source, target, device):
        at = len(messages)
        copy = pltpu.make_async_remote_copy(
            src_ref=source,
            dst_ref=target,
            send_sem=sent.at[at],
            recv_sem=landed.at[at],
            device_id=device,
            device_id_type=MESH,
        )
        copy.start()
        messages.append(copy)
        return copy

    loads = {}
    for at, (name, source, target) in enumerate(
        (
            ("qkv", w_qkv, s.wqkv),
            ("down", w_down, s.wdown),
            ("out", w_out, s.wout),
            ("up", w_up, s.wup),
        )
    ):
        loads[name] = pltpu.make_async_copy(source, target, local.at[at])
        loads[name].start()

    barrier = pltpu.get_barrier_semaphore()
    for device in [near(r) for r in range(1, 8)] + [z_one, z_two]:
        pl.semaphore_signal(barrier, inc=1, device_id=device, device_id_type=MESH)

    values_one = x_ref[...].astype(WIDE)
    unit_one, scale_one = norm_parts(values_one)
    normed_one = (unit_one * gain_one[...] + shift_one[...]).astype(LOW)
    loads["qkv"].wait()
    pl.semaphore_wait(barrier, 9)
    s.cot2[0:128, :] = cot_ref[...]
    gather = []
    for g in range(3):
        at = 256 * g
        s.kv[g, 0, 0] = dot(normed_one, s.wqkv[:, 768 + at : 1024 + at]).astype(LOW)
        s.kv[g, 0, 1] = (
            dot(normed_one, s.wqkv[:, 1536 + at : 1792 + at]) + bias_v[:, at : at + 256]
        ).astype(LOW)
        gather.append([send(s.kv.at[g, 0], s.kv.at[g, r], near(r)) for r in (2, 4, 1)])
    share_cot = send(s.cot2.at[pl.ds(0, 128)], s.cot2.at[pl.ds(128, 128)], near(1))
    for g in range(3):
        at = 256 * g
        q = (dot(normed_one, s.wqkv[:, at : at + 256]) + bias_q[:, at : at + 256]).astype(LOW)
        q = (q.astype(WIDE) * 0.125).astype(LOW)
        s.q_low[:, at : at + 256] = q
        s.q_turned[at : at + 256, :] = q.T

    def share(source, lhs, give):
        for slot, r in enumerate((0, 2, 6, 4)):
            ours = place(r)
            lhs[slot, ..., 0:128] = source[ours]
            give[slot] = source[ours + 1 - 2 * core]
        return send(give, lhs.at[..., pl.ds(128, 128)], near(1))

    s.n1_t[...] = normed_one.T.reshape(8, 96, 128)
    share_one = share(s.n1_t, s.lhs_qkv, s.give_qkv)

    more = [[] for _ in range(3)]
    diagonal = [[] for _ in range(3)]

    def forward(g):
        gather[g][0].wait_recv()
        diagonal[g].append(send(s.kv.at[g, 2, 0], s.kv.at[g, 6, 0], near(4)))
        more[g].append(send(s.kv.at[g, 2], s.kv.at[g, 3], near(1)))
        gather[g][1].wait_recv()
        diagonal[g].append(send(s.kv.at[g, 4, 1], s.kv.at[g, 6, 1], near(2)))
        more[g].append(send(s.kv.at[g, 4], s.kv.at[g, 5], near(1)))
        gather[g][2].wait_recv()

    def forward_diagonal(g):
        diagonal[g][0].wait_recv()
        more[g].append(send(s.kv.at[g, 6, 0], s.kv.at[g, 7, 0], near(1)))
        diagonal[g][1].wait_recv()
        more[g].append(send(s.kv.at[g, 6, 1], s.kv.at[g, 7, 1], near(1)))

    def gathered(g):
        for copy in more[g]:
            copy.wait_recv()

    def active_grad(first, last):
        for j in range(first, last):
            rows = s.wdown[4 * j : 4 * j + 4].reshape(384, 768)
            s.d_act[:, 384 * j : 384 * j + 384] = dot_rows(cot_ref[...], rows)

    loads["down"].wait()
    active_grad(0, 3)
    forward(0)
    active_grad(3, 5)
    forward_diagonal(0)
    forward(1)
    active_grad(5, 8)
    gathered(0)

    row_at = lax.broadcasted_iota(jnp.int32, (128, 128), 0)
    lane_at = lax.broadcasted_iota(jnp.int32, (128, 128), 1)
    query_at = row_at + me * 128
    begin_one = lengths_ref[0, 0]
    begin_two = begin_one + lengths_ref[0, 1]
    begin_three = begin_two + lengths_ref[0, 2]
    begin = jnp.where(query_at >= begin_one, begin_one, 0)
    begin = jnp.where(query_at >= begin_two, begin_two, begin)
    begin = jnp.where(query_at >= begin_three, begin_three, begin)
    earlier = jnp.where(lane_at < row_at, 1.0, 0.0).astype(LOW)
    first_lanes = jnp.where(lane_at < 64, 1.0, 0.0)
    head_zero = (s.q_low[:, 0:128].astype(WIDE) * first_lanes).astype(LOW)
    for r in range(8):
        scores = dot_rows(head_zero, s.kv[0, r, 0, :, 0:128])
        key_at = lane_at + place(r) * 128
        allowed = (key_at <= query_at) & (key_at >= begin)
        chosen = (key_at < query_at) & (key_at > begin)
        small_exp = jnp.exp(-jnp.abs(scores))
        soft = jnp.maximum(scores, 0.0) + jnp.log1p(small_exp)
        picked = jnp.where(chosen, soft, 0.0) * (1.0 / 1024)
        high, rest = split_low(picked)
        s.sums[0, r : r + 1, :] = jnp.sum(picked, axis=0, keepdims=True)
        within = dot(earlier, high) + dot(earlier, rest)
        s.forgot[:, 128 * r : 128 * r + 128] = jnp.where(allowed, within, FAR)
        sigmoid = jnp.where(scores >= 0, 1.0, small_exp) / (1.0 + small_exp)
        s.sig_t[128 * r : 128 * r + 128, :] = (jnp.where(chosen, sigmoid, 0.0) * (1.0 / 1024)).T
    sum_copies = [send(s.sums.at[0], s.sums.at[r], near(r)) for r in range(1, 8)]
    forward_diagonal(1)
    forward(2)
    gathered(1)
    for copy in sum_copies:
        copy.wait_recv()

    def others(sums, later):
        rows = [jnp.zeros((1, 128), WIDE) for _ in range(8)]
        for d in range(1, 8):
            ahead = place(d) > me if later else place(d) < me
            weight = jnp.where(ahead, 1.0, 0.0)
            for r in range(8):
                rows[r] = rows[r] + weight * sums[d, (r ^ d) : (r ^ d) + 1, :]
        return rows

    for r, row in enumerate(others(s.sums, False)):
        at = 128 * r
        s.forgot_t[at : at + 128, :] = (s.forgot[:, at : at + 128] + row).T

    feature_at = lax.broadcasted_iota(jnp.int32, (128, 256), 0)
    column_at = lax.broadcasted_iota(jnp.int32, (128, 256), 1)
    own_head_t = jnp.where((feature_at < 64) == (column_at < 128), 1.0, 0.0).astype(LOW)
    long_row = lax.broadcasted_iota(jnp.int32, (256, 128), 0)
    long_lane = lax.broadcasted_iota(jnp.int32, (256, 128), 1)
    own_head = jnp.where((long_row < 128) == (long_lane < 64), 1.0, 0.0).astype(LOW)

    def both_t(values):
        return jnp.concatenate([values, values], axis=1) * own_head_t

    def both(values):
        return jnp.concatenate([values, values], axis=0) * own_head

    def block(pair, part):
        at = 128 * (pair % 2)
        return s.kv[pair // 2, :, part, :, at : at + 128].reshape(1024, 128)

    def turn(pair, part):
        at = 128 * (pair % 2)
        for r in range(8):
            s.turned[pair, :, 128 * r : 128 * r + 128] = s.kv[
                pair // 2, r, part, :, at : at + 128
            ].T

    def attend(pair):
        at = 128 * pair
        turn(pair, 1)
        scores = dot(block(pair, 0), both_t(s.q_turned[at : at + 128, :]))
        forgot = s.forgot_t[...]
        logits = scores - jnp.concatenate([forgot, forgot], axis=1)
        raised = jnp.exp(logits - jnp.max(logits, axis=0, keepdims=True))
        probs = (raised * (1.0 / jnp.sum(raised, axis=0, keepdims=True))).astype(LOW)
        s.probs[pair] = probs
        mixed = dot(s.turned[pair], probs)
        s.att_t[at : at + 64, :] = mixed[0:64, 0:128]
        s.att_t[at + 64 : at + 128, :] = mixed[64:128, 128:256]

    attend(0)
    attend(1)
    forward_diagonal(2)
    attend(2)
    attend(3)
    gathered(2)
    attend(4)
    attend(5)

    attended_low_t = s.att_t[...].astype(LOW)
    s.att_low_t[...] = attended_low_t.reshape(8, 96, 128)
    loads["out"].wait()
    middle = values_one + dot(attended_low_t.T, s.wout[...]) + bias_out[...]
    s.middle[...] = middle
    unit_two, scale_two = norm_parts(middle)
    s.unit_two[...] = unit_two
    normed_two = (unit_two * gain_two[...] + shift_two[...]).astype(LOW)
    s.n2_t[...] = normed_two.T.reshape(8, 96, 128)
    share_two = share(s.n2_t, s.lhs_up, s.give_up)
    share_att = share(s.att_low_t, s.lhs_out, s.give_out)
    loads["up"].wait()
    share_hidden = []
    for j in range(4):
        at = 768 * j
        hidden = dot(normed_two, s.wup[:, at : at + 768]) + bias_up[:, at : at + 768]
        square = hidden * hidden
        bend = jnp.tanh(0.7978845608028654 * hidden * (1.0 + 0.044715 * square))
        half = 0.5 * (1.0 + bend)
        active = (hidden * half).astype(LOW)
        slope = half + 0.5 * hidden * (1.0 - bend * bend) * (
            0.7978845608028654 * (1.0 + 3 * 0.044715 * square)
        )
        s.act[:, at : at + 768] = active
        turned = active.T.reshape(2, 4, 96, 128)
        s.act_t[2 * j : 2 * j + 2] = turned
        d_hidden = (s.d_act[:, at : at + 768] * slope).astype(LOW)
        s.dh2[0:128, at : at + 768] = d_hidden
        s.small[0, 2 * j : 2 * j + 1, 768:1152] = jnp.sum(
            d_hidden[:, 0:384].astype(WIDE), axis=0, keepdims=True
        )
        s.small[0, 2 * j + 1 : 2 * j + 2, 768:1152] = jnp.sum(
            d_hidden[:, 384:768].astype(WIDE), axis=0, keepdims=True
        )
    share_down = share(s.act_t, s.lhs_down, s.give_down)
    share_hidden = send(s.dh2.at[pl.ds(0, 128)], s.dh2.at[pl.ds(128, 128)], near(1))

    class Unit:
        def __init__(self, at, lhs, rhs, grads):
            self.at, self.lhs, self.rhs, self.grads = at, lhs, rhs, grads

        def make(self):
            lhs = self.lhs[...].reshape(384, 256)
            for half in range(2):
                at = 384 * half
                grads = dot(lhs, self.rhs[:, at : at + 384]).astype(LOW)
                self.grads[:, :, at : at + 384] = grads.reshape(4, 96, 384)
            got = s.got_one.at[self.at]
            self.one = (
                send(self.grads.at[pl.ds(1, 2), :, pl.ds(0, 384)], got.at[0], near(2)),
                send(self.grads.at[pl.ds(2, 2), :, pl.ds(384, 384)], got.at[1], near(4)),
            )

        def add(self, slot, half, got):
            at = 384 * half
            ours = self.grads[slot, :, at : at + 384].astype(WIDE)
            return ours + got[...].astype(WIDE)

        def pass_on(self):
            got = s.got_one.at[self.at]
            two = []
            for half, slot, index, r in ((0, 3, 1, 4), (1, 1, 0, 2)):
                at = 384 * half
                self.one[half].wait_recv()
                total = self.add(slot, half, got.at[half, index]).astype(LOW)
                self.grads[slot, :, at : at + 384] = total
                two.append(
                    send(
                        self.grads.at[slot, :, pl.ds(at, 384)],
                        s.got_two.at[self.at, half],
                        near(r),
                    )
                )
            self.two = two

        def finish(self):
            got = s.got_one.at[self.at]
            for half, index in ((0, 0), (1, 1)):
                at = 384 * half
                self.two[half].wait_recv()
                total = self.add(0, half, got.at[half, index])
                total = (total + s.got_two[self.at, half].astype(WIDE)).astype(LOW)
                s.mine[self.at, :, :, at : at + 384] = total.reshape(2, 48, 384)
            self.z = send(s.mine.at[self.at, 1 - z_low], s.got_z.at[self.at], z_one)

        def z_pair(self):
            self.z.wait_recv()
            total = s.mine[self.at, z_low].astype(WIDE) + s.got_z[self.at].astype(WIDE)
            s.mine[self.at, z_low] = total.astype(LOW)
            self.z = send(s.mine.at[self.at, z_low], s.got_zz.at[self.at], z_two)

        def z_all(self):
            self.z.wait_recv()
            total = s.mine[self.at, z_low].astype(WIDE) + s.got_zz[self.at].astype(WIDE)
            s.total[self.at, z_low] = total.astype(LOW)
            self.z = send(s.total.at[self.at, z_low], s.total.at[self.at, z_low], z_one)

        def done(self):
            self.z.wait_recv()
            copy = pltpu.make_async_copy(
                s.total.at[self.at], total_ref.at[self.at], local.at[4 + self.at]
            )
            copy.start()
            writes.append(copy)

    writes = []
    units = []
    for j in range(4):
        units.append(Unit(j, s.lhs_down.at[:, j], s.cot2, s.part.at[j]))
    spare = [s.wdown.at[pl.ds(4 * j, 4)] for j in range(8)]
    units.append(Unit(4, s.lhs_out, s.db2, spare[0]))
    for j in range(4):
        units.append(Unit(5 + j, s.lhs_up, s.dh2.at[:, pl.ds(768 * j, 768)], spare[1 + j]))
    for j in range(3):
        units.append(Unit(9 + j, s.lhs_qkv, s.dqkv2.at[:, pl.ds(768 * j, 768)], spare[5 + j]))

    share_cot.wait_recv()
    share_down.wait_recv()
    units[0].make()
    units[1].make()

    d_output = cot_ref[...].astype(WIDE)
    parts = []
    for j in range(3):
        parts.append(dot_rows(s.dh2[0:128, :], s.wup[256 * j : 256 * j + 256, :]))
    d_normed = jnp.concatenate(parts, axis=1)
    unit_two = s.unit_two[...]
    s.small[0, 5:6, 0:768] = jnp.sum(d_normed * unit_two, axis=0, keepdims=True)
    s.small[0, 6:7, 0:768] = jnp.sum(d_normed, axis=0, keepdims=True)
    s.small[0, 7:8, 0:768] = jnp.sum(d_output, axis=0, keepdims=True)
    d_middle = d_output + norm_back(d_normed, unit_two, scale_two, gain_two[...])
    s.d_mid[...] = d_middle
    s.small[0, 4:5, 0:768] = jnp.sum(d_middle, axis=0, keepdims=True)
    d_branch = d_middle.astype(LOW)
    s.db2[0:128, :] = d_branch
    share_branch = send(s.db2.at[pl.ds(0, 128)], s.db2.at[pl.ds(128, 128)], near(1))
    d_att_t = dot(s.wout[...], d_branch.T).astype(LOW)
    s.d_att_t[...] = d_att_t
    s.d_att[...] = d_att_t.T

    mixed = jnp.zeros((128, 768), WIDE)
    for j in range(4):
        rows = s.wdown[8 * j : 8 * j + 8].reshape(768, 768)
        mixed = mixed + dot(s.act[:, 768 * j : 768 * j + 768], rows)
    out_ref[...] = (s.middle[...] + mixed + bias_down[...]).astype(LOW)

    def logit_grads(pair):
        at = 128 * pair
        grad_t = s.d_att_t[at : at + 128, :]
        products = grad_t.astype(WIDE) * s.att_t[at : at + 128, :]
        delta = jnp.concatenate(
            [
                jnp.sum(products[0:64], axis=0, keepdims=True),
                jnp.sum(products[64:128], axis=0, keepdims=True),
            ],
            axis=1,
        )
        d_probs = dot(block(pair, 1), both_t(grad_t))
        d_logits = s.probs[pair].astype(WIDE) * (d_probs - delta)
        both_heads = d_logits[:, 0:128] + d_logits[:, 128:256]
        if pair == 5:
            s.d_forgot_t[...] = both_heads
        else:
            s.d_forgot_t[...] += both_heads
        return d_logits

    def keep(pair, half, grads):
        at = 128 * (pair % 2)
        low = grads.astype(LOW)
        for r in range(8):
            slot = (0, 1, 3, 2)[r >> 1]
            s.dkv[pair // 2, r & 1, half, slot, :, at : at + 128] = low[128 * r : 128 * r + 128]

    def value_grads(pair):
        at = 128 * pair
        keep(pair, 1, dot(s.probs[pair], both(s.d_att[:, at : at + 128])))

    def score_grads(pair, d_scores):
        at = 128 * pair
        turn(pair, 0)
        keep(pair, 0, dot(d_scores, both(s.q_low[:, at : at + 128])))
        grads = dot(s.turned[pair], d_scores)
        s.dq_t[at : at + 64, :] = grads[0:64, 0:128]
        s.dq_t[at + 64 : at + 128, :] = grads[64:128, 128:256]

    def attend_back(pair):
        d_logits = logit_grads(pair)
        value_grads(pair)
        score_grads(pair, d_logits.astype(LOW))

    class KeyGroup:
        def __init__(self, g):
            self.g = g

        def across(self):
            self.core = send(s.dkv.at[self.g, 1], s.dkv_core.at[self.g], near(1))

        def make(self):
            g = self.g
            self.core.wait_recv()
            total = s.dkv[g, 0].astype(WIDE) + s.dkv_core[g].astype(WIDE)
            s.dkv[g, 0] = total.astype(LOW)
            self.one = (
                send(s.dkv.at[g, 0, 0, pl.ds(1, 2)], s.dkv_one.at[g, 0], near(2)),
                send(s.dkv.at[g, 0, 1, pl.ds(2, 2)], s.dkv_one.at[g, 1], near(4)),
            )

        def pass_on(self):
            g = self.g
            two = []
            for half, slot, index, r in ((0, 3, 1, 4), (1, 1, 0, 2)):
                self.one[half].wait_recv()
                total = s.dkv[g, 0, half, slot].astype(WIDE) + s.dkv_one[g, half, index].astype(WIDE)
                s.dkv[g, 0, half, slot] = total.astype(LOW)
                two.append(send(s.dkv.at[g, 0, half, slot], s.dkv_two.at[g, half], near(r)))
            self.two = two

        def finish(self):
            g = self.g
            for half, index in ((0, 0), (1, 1)):
                self.two[half].wait_recv()
                total = s.dkv[g, 0, half, 0].astype(WIDE) + s.dkv_one[g, half, index].astype(WIDE)
                total = total + s.dkv_two[g, half].astype(WIDE)
                at = 768 * (half + 1) + 256 * g
                s.dqkv2[0:128, at : at + 256] = total.astype(LOW)

    groups = [KeyGroup(g) for g in range(3)]
    share_two.wait_recv()
    share_hidden.wait_recv()
    units[5].make()
    units[0].pass_on()
    attend_back(5)
    units[1].pass_on()
    units[6].make()
    attend_back(4)
    groups[2].across()
    units[0].finish()
    attend_back(3)
    groups[2].make()
    units[5].pass_on()
    attend_back(2)
    groups[1].across()
    units[1].finish()
    attend_back(1)
    groups[1].make()
    units[6].pass_on()
    d_logits = logit_grads(0)
    s.forgot_t[...] = d_logits[:, 0:128]
    s.second_head[...] = d_logits[:, 128:256].astype(LOW)
    for r in range(8):
        turned = s.d_forgot_t[128 * r : 128 * r + 128, :].T
        s.back_sums[0, r : r + 1, :] = jnp.sum(turned, axis=0, keepdims=True)
    sum_copies = [send(s.back_sums.at[0], s.back_sums.at[r], near(r)) for r in range(1, 8)]
    value_grads(0)
    units[2].make()
    groups[2].pass_on()
    units[0].z_pair()
    units[1].z_pair()
    for copy in sum_copies:
        copy.wait_recv()
    later_rows = others(s.back_sums, True)
    following = jnp.where(row_at > lane_at, 1.0, 0.0).astype(LOW)
    selected = []
    for r in range(8):
        at = 128 * r
        high, rest = split_low(s.d_forgot_t[at : at + 128, :])
        later = jnp.broadcast_to(later_rows[r], (128, 128)).T
        d_picked = -(dot(high, following) + dot(rest, following) + later)
        selected.append(s.forgot_t[at : at + 128, :] + s.sig_t[at : at + 128, :] * d_picked)
    first_head = jnp.concatenate(selected, axis=0).astype(LOW)
    score_grads(0, jnp.concatenate([first_head, s.second_head[...]], axis=1))
    groups[0].across()
    for j in range(6):
        at = 128 * j
        d_q = (s.dq_t[at : at + 128, :] * 0.125).astype(LOW)
        s.dqkv2[0:128, at : at + 128] = d_q.T

    def share_part(j):
        cols = pl.ds(768 * j, 768)
        return send(
            s.dqkv2.at[pl.ds(0, 128), cols], s.dqkv2.at[pl.ds(128, 128), cols], near(1)
        )

    def input_part(j):
        cols = slice(768 * j, 768 * j + 768)
        parts = []
        for i in range(3):
            rows = s.wqkv[256 * i : 256 * i + 256, cols]
            parts.append(dot_rows(s.dqkv2[0:128, cols], rows))
        return jnp.concatenate(parts, axis=1)

    share_q = share_part(0)
    units[5].finish()
    groups[1].pass_on()
    groups[0].make()
    groups[2].finish()
    units[6].finish()
    units[3].make()
    units[2].pass_on()
    units[0].z_all()
    units[1].z_all()
    d_normed = input_part(0)
    groups[0].pass_on()
    groups[1].finish()
    share_att.wait_recv()
    share_branch.wait_recv()
    share_one.wait_recv()
    units[4].make()
    units[3].pass_on()
    units[2].finish()
    units[5].z_pair()
    units[6].z_pair()
    groups[0].finish()
    share_k = share_part(1)
    share_v = share_part(2)
    share_q.wait_recv()
    units[9].make()
    units[4].pass_on()
    d_normed = d_normed + input_part(1) + input_part(2)
    share_k.wait_recv()
    units[10].make()
    units[9].pass_on()
    share_v.wait_recv()
    units[11].make()
    units[10].pass_on()
    unit_one, scale_one = norm_parts(x_ref[...].astype(WIDE))
    s.small[0, 0:1, 0:768] = jnp.sum(d_normed * unit_one, axis=0, keepdims=True)
    s.small[0, 1:2, 0:768] = jnp.sum(d_normed, axis=0, keepdims=True)
    s.small[0, 2:3, 0:768] = jnp.sum(
        s.dqkv2[0:128, 0:768].astype(WIDE), axis=0, keepdims=True
    )
    s.small[0, 3:4, 0:768] = jnp.sum(
        s.dqkv2[0:128, 1536:2304].astype(WIDE), axis=0, keepdims=True
    )
    d_inputs = s.d_mid[...] + norm_back(d_normed, unit_one, scale_one, gain_one[...])
    grad_ref[...] = d_inputs.astype(LOW)
    devices = (near(1), near(2), near(4), z_one, z_two)

    def small_send(step):
        return send(s.small.at[step], s.small_got.at[step], devices[step])

    def small_add(step, copy):
        copy.wait_recv()
        s.small[step + 1] = s.small[step] + s.small_got[step]

    small_copy = small_send(0)
    units[7].make()
    units[11].pass_on()
    small_add(0, small_copy)
    small_copy = small_send(1)
    units[3].finish()
    units[4].finish()
    units[2].z_pair()
    units[5].z_all()
    units[6].z_all()
    units[9].finish()
    units[8].make()
    units[7].pass_on()
    small_add(1, small_copy)
    small_copy = small_send(2)
    units[10].finish()
    units[3].z_pair()
    units[4].z_pair()
    units[2].z_all()
    units[11].finish()
    units[9].z_pair()
    units[8].pass_on()
    small_add(2, small_copy)
    small_copy = small_send(3)
    units[7].finish()
    units[3].z_all()
    units[4].z_all()
    units[10].z_pair()
    units[11].z_pair()
    units[9].z_all()
    small_add(3, small_copy)
    small_copy = small_send(4)
    units[8].finish()
    units[7].z_pair()
    units[10].z_all()
    units[11].z_all()
    units[8].z_pair()
    units[7].z_all()
    for j in (0, 1, 5, 6, 2, 3, 4):
        units[j].done()
    small_add(4, small_copy)
    narrow = jnp.zeros((8, 96), WIDE)
    wide = jnp.zeros((1, 384), WIDE)
    for j in range(8):
        ours = jnp.where(me == j, 1.0, 0.0)
        narrow = narrow + ours * s.small[5, :, 96 * j : 96 * j + 96]
        wide = wide + ours * s.small[5, j : j + 1, 768:1152]
    small_ref[...] = narrow
    wide_ref[...] = wide
    units[8].z_all()
    for j in (9, 10, 11, 7, 8):
        units[j].done()
    for copy in writes:
        copy.wait()
    for copy in messages:
        copy.wait_send()


def spread_kernel(total_ref, small_ref, wide_ref, *outs):
    gain_one, shift_one, qkv, bias_q, bias_v, out, bias_out = outs[:7]
    gain_two, shift_two, up, bias_up, down, bias_down = outs[7:]
    for j in range(4):
        down[96 * j : 96 * j + 96, :] = total_ref[j].astype(WIDE)
        up[:, 768 * j : 768 * j + 768] = total_ref[5 + j].astype(WIDE)
    out[...] = total_ref[4].astype(WIDE)
    for j in range(3):
        qkv[:, 768 * j : 768 * j + 768] = total_ref[9 + j].astype(WIDE)
    rows = (gain_one, shift_one, bias_q, bias_v, bias_out, gain_two, shift_two, bias_down)
    for j, target in enumerate(rows):
        target[...] = small_ref[j, :]
    bias_up[...] = wide_ref[0, :]


def fused_device(
    inputs,
    gain_one,
    shift_one,
    w_qkv,
    bias_q,
    bias_v,
    w_out,
    bias_out,
    gain_two,
    shift_two,
    w_up,
    bias_up,
    w_down,
    bias_down,
    lengths,
    cotangent,
):
    vmem = pl.BlockSpec(memory_space=pltpu.VMEM)
    anywhere = pl.BlockSpec(memory_space=pl.ANY)
    vectors = [gain_one, shift_one, bias_q, bias_v, bias_out, gain_two, shift_two]
    vectors = [v.reshape(1, -1) for v in vectors + [bias_up, bias_down]]
    tokens, width = inputs.shape
    layer_out, grad_inputs, total, small, wide = pl.pallas_call(
        layer_kernel,
        out_shape=(
            jax.ShapeDtypeStruct((tokens, width), LOW),
            jax.ShapeDtypeStruct((tokens, width), LOW),
            jax.ShapeDtypeStruct((ROW_UNITS, 2, 48, 768), LOW),
            jax.ShapeDtypeStruct((8, 96), WIDE),
            jax.ShapeDtypeStruct((1, 384), WIDE),
        ),
        in_specs=[pl.BlockSpec(memory_space=pltpu.SMEM)] + [vmem] * 11 + [anywhere] * 4,
        out_specs=(vmem, vmem, anywhere, vmem, vmem),
        scratch_shapes=[pltpu.VMEM(shape, kind) for shape, kind in SCRATCH.values()]
        + [
            pltpu.SemaphoreType.DMA((180,)),
            pltpu.SemaphoreType.DMA((180,)),
            pltpu.SemaphoreType.DMA((4 + ROW_UNITS,)),
        ],
        compiler_params=pltpu.CompilerParams(
            collective_id=0, has_side_effects=True, vmem_limit_bytes=VMEM_BYTES
        ),
        name="layer",
    )(lengths, inputs, cotangent, *vectors, w_qkv, w_out, w_up, w_down.reshape(32, 96, width))
    grads = pl.pallas_call(
        spread_kernel,
        out_shape=tuple(
            jax.ShapeDtypeStruct(shape, WIDE)
            for shape in (
                (96,),
                (96,),
                (96, 2304),
                (96,),
                (96,),
                (96, 768),
                (96,),
                (96,),
                (96,),
                (96, 3072),
                (384,),
                (384, 768),
                (96,),
            )
        ),
        in_specs=[vmem] * 3,
        out_specs=(vmem,) * 13,
        compiler_params=pltpu.CompilerParams(vmem_limit_bytes=VMEM_BYTES),
        name="spread",
    )(total.reshape(ROW_UNITS, 96, width), small, wide)
    return (layer_out, grad_inputs, *grads)


VMEM_BYTES = 63 * 2**20


def per_device(*arguments):
    inputs, w_up = arguments[0], arguments[10]
    fits = (
        lax.axis_size("dp") == 4
        and lax.axis_size("col") == 8
        and inputs.shape == (128, 768)
        and w_up.shape == (768, 3072)
    )
    return fused_device(*arguments) if fits else general_device(*arguments)


def solution(mesh):
    return jax.shard_map(
        per_device,
        mesh=mesh,
        in_specs=(
            P(("dp", "col"), None),
            P(),
            P(),
            P(),
            P(),
            P(),
            P(),
            P(),
            P(),
            P(),
            P(),
            P(),
            P(),
            P(),
            P("dp", None),
            P(("dp", "col"), None),
        ),
        out_specs=(
            P(("dp", "col"), None),
            P(("dp", "col"), None),
            P("col"),
            P("col"),
            P("col", None),
            P("col"),
            P("col"),
            P("col", None),
            P("col"),
            P("col"),
            P("col"),
            P("col", None),
            P("col"),
            P("col", None),
            P("col"),
        ),
        check_vma=False,
    )
```

```python
import functools
import types

import jax
import jax.numpy as jnp
from jax import lax
from jax.experimental import pallas as pl
from jax.experimental.pallas import tpu as pltpu
from jax.sharding import PartitionSpec as P

H = 12
HEAD = 64


epsilon = 1e-05


def layer_norm(values, scales, offset):
    average = jnp.mean(values, axis=-1, keepdims=True)
    centered = values - average
    spread = jnp.mean(centered * centered, axis=-1, keepdims=True)
    return centered * lax.rsqrt(spread + epsilon) * scales + offset


def documents(places, row_lengths):
    finish = jnp.cumsum(row_lengths)
    begins = finish - row_lengths
    inside = (places[:, None] >= begins[None, :]) & (places[:, None] < finish[None, :])
    numbers = jnp.arange(row_lengths.shape[0], dtype=jnp.int32)
    doc_index = jnp.sum(jnp.where(inside, numbers[None, :], 0), axis=1)
    first_place = jnp.sum(jnp.where(inside, begins[None, :], 0), axis=1)
    return (doc_index, first_place == places)


def general_device(
    inputs,
    gain_one,
    shift_one,
    w_qkv,
    bias_q,
    bias_v,
    w_out,
    bias_out,
    gain_two,
    shift_two,
    w_up,
    bias_up,
    w_down,
    bias_down,
    lengths,
    cotangent,
):
    col_count = lax.axis_size("col")
    col_place = lax.axis_index("col")
    tok_rows = inputs.shape[0]
    model_width = inputs.shape[1]
    row_len = tok_rows * col_count
    block_rows = min(512, row_len)
    block_count = row_len // block_rows
    places = jnp.arange(row_len, dtype=jnp.int32)
    doc_index, first_flag = documents(places, lengths[0])
    own_first = col_place * tok_rows
    key_places = own_first + jnp.arange(tok_rows, dtype=jnp.int32)
    key_doc = lax.dynamic_slice_in_dim(doc_index, own_first, tok_rows, 0)
    key_first = lax.dynamic_slice_in_dim(first_flag, own_first, tok_rows, 0)
    floated = inputs.astype(jnp.float32)
    norm_first, first_back = jax.vjp(layer_norm, floated, gain_one, shift_one)
    normed_one = norm_first.astype(jnp.bfloat16)
    joined = jnp.dot(normed_one, w_qkv, preferred_element_type=jnp.float32)
    queries = (joined[:, :model_width] + bias_q).astype(jnp.bfloat16)
    key_rows = joined[:, model_width : 2 * model_width].astype(jnp.bfloat16)
    value_rows = (joined[:, 2 * model_width :] + bias_v).astype(jnp.bfloat16)
    key_heads = key_rows.reshape(tok_rows, H, HEAD)
    value_heads = value_rows.reshape(tok_rows, H, HEAD)
    all_queries = lax.all_gather(queries, "col", axis=0, tiled=True)

    def block_terms(source, block_index, carried):
        first_row = block_index * block_rows
        q_block = lax.dynamic_slice_in_dim(source, first_row, block_rows, 0).reshape(
            block_rows, H, HEAD
        )
        q_places = first_row + jnp.arange(block_rows, dtype=jnp.int32)
        q_doc = lax.dynamic_slice_in_dim(doc_index, first_row, block_rows, 0)
        scores = (
            jnp.einsum("khd,qhd->hkq", key_heads, q_block, preferred_element_type=jnp.float32)
            * 0.125
        )
        allowed = (key_places[:, None] <= q_places[None, :]) & (key_doc[:, None] == q_doc[None, :])
        chosen = (
            allowed
            & (key_places[:, None] < q_places[None, :])
            & jnp.logical_not(key_first)[:, None]
        )
        picked = jnp.where(chosen, jax.nn.softplus(scores[0]), 0.0) / row_len
        forgot = carried[:, None] + jnp.cumsum(picked, axis=1) - picked
        logits = jnp.where(allowed[None], scores - forgot[None], -jnp.inf)
        return (q_block, scores, chosen, picked, logits)

    def forward_block(carried, block_index):
        q_block, scores, chosen, picked, logits = block_terms(all_queries, block_index, carried)
        row_top = jnp.max(logits, axis=1)
        safe_top = jnp.where(row_top > -jnp.inf, row_top, 0.0)
        raised = jnp.exp(logits - safe_top[:, None, :])
        totals = jnp.sum(raised, axis=1)
        numerator = jnp.einsum(
            "hkq,khd->qhd",
            raised.astype(jnp.bfloat16),
            value_heads,
            preferred_element_type=jnp.float32,
        )
        return (
            carried + jnp.sum(picked, axis=1),
            (carried, row_top.T, totals.T, numerator.reshape(block_rows, model_width)),
        )

    indices = jnp.arange(block_count, dtype=jnp.int32)
    unused, (block_starts, row_tops, row_totals, numerators) = lax.scan(
        forward_block, jnp.zeros((tok_rows,), jnp.float32), indices
    )
    row_tops = row_tops.reshape(row_len, H)
    row_totals = row_totals.reshape(row_len, H)
    numerators = numerators.reshape(row_len, model_width)
    got_top, got_total, got_numer = (
        lax.all_to_all(
            row_tops[None].astype(jnp.bfloat16), "col", split_axis=1, concat_axis=0, tiled=True
        ).astype(jnp.float32),
        lax.all_to_all(
            row_totals[None].astype(jnp.bfloat16), "col", split_axis=1, concat_axis=0, tiled=True
        ).astype(jnp.float32),
        lax.all_to_all(
            numerators[None].astype(jnp.bfloat16), "col", split_axis=1, concat_axis=0, tiled=True
        ).astype(jnp.float32),
    )
    row_best = jnp.max(got_top, axis=0)
    factor = jnp.exp(got_top - row_best[None])
    totals_own = jnp.sum(factor * got_total, axis=0)
    numer_own = jnp.sum(got_numer.reshape(col_count, tok_rows, H, HEAD) * factor[..., None], axis=0)
    attended = (numer_own / totals_own[..., None]).reshape(tok_rows, model_width)
    row_lse = row_best + jnp.log(totals_own)
    attended_low = attended.astype(jnp.bfloat16)
    middle = floated + jnp.dot(attended_low, w_out, preferred_element_type=jnp.float32) + bias_out
    norm_second, second_back = jax.vjp(layer_norm, middle, gain_two, shift_two)
    normed_two = norm_second.astype(jnp.bfloat16)
    hidden = jnp.dot(normed_two, w_up, preferred_element_type=jnp.float32) + bias_up
    active_full, gelu_back = jax.vjp(jax.nn.gelu, hidden)
    active = active_full.astype(jnp.bfloat16)
    layer_out = (
        middle + jnp.dot(active, w_down, preferred_element_type=jnp.float32) + bias_down
    ).astype(jnp.bfloat16)
    d_output = cotangent.astype(jnp.float32)
    grad_w_down = jnp.einsum("tf,td->fd", active, cotangent, preferred_element_type=jnp.float32)
    grad_bias_down = jnp.sum(d_output, axis=0)
    d_active = jnp.einsum("td,fd->tf", cotangent, w_down, preferred_element_type=jnp.float32)
    d_hidden = gelu_back(d_active)[0].astype(jnp.bfloat16)
    grad_w_up = jnp.einsum("td,tf->df", normed_two, d_hidden, preferred_element_type=jnp.float32)
    grad_bias_up = jnp.sum(d_hidden.astype(jnp.float32), axis=0)
    d_normed_two = jnp.einsum("tf,df->td", d_hidden, w_up, preferred_element_type=jnp.float32)
    d_middle_norm, grad_gain_two, grad_shift_two = second_back(d_normed_two)
    d_middle = d_output + d_middle_norm
    d_branch = d_middle.astype(jnp.bfloat16)
    grad_w_out = jnp.einsum("td,te->de", attended_low, d_branch, preferred_element_type=jnp.float32)
    grad_bias_out = jnp.sum(d_middle, axis=0)
    d_attended = jnp.einsum(
        "te,de->td", d_branch, w_out, preferred_element_type=jnp.float32
    ).astype(jnp.bfloat16)
    row_delta = jnp.sum(
        (d_attended.astype(jnp.float32) * attended).reshape(tok_rows, H, HEAD), axis=2
    )
    back_queries, gathered_grad = (
        lax.all_gather(queries, "col", axis=0, tiled=True),
        lax.all_gather(d_attended, "col", axis=0, tiled=True),
    )
    all_lse, all_delta = (
        lax.all_gather(row_lse, "col", axis=0, tiled=True),
        lax.all_gather(row_delta, "col", axis=0, tiled=True),
    )

    def backward_block(carried_state, inputs_block):
        later_sum, key_grad, value_grad = carried_state
        block_index, carried = inputs_block
        q_block, scores, chosen, picked, logits = block_terms(back_queries, block_index, carried)
        first_row = block_index * block_rows
        grad_block = lax.dynamic_slice_in_dim(gathered_grad, first_row, block_rows, 0).reshape(
            block_rows, H, HEAD
        )
        lse_block = lax.dynamic_slice_in_dim(all_lse, first_row, block_rows, 0)
        delta_block = lax.dynamic_slice_in_dim(all_delta, first_row, block_rows, 0)
        weights = jnp.exp(logits - lse_block.T[:, None, :])
        value_grad = value_grad + jnp.einsum(
            "hkq,qhd->khd",
            weights.astype(jnp.bfloat16),
            grad_block,
            preferred_element_type=jnp.float32,
        )
        d_weights = jnp.einsum(
            "khd,qhd->hkq", value_heads, grad_block, preferred_element_type=jnp.float32
        )
        d_logits = weights * (d_weights - delta_block.T[:, None, :])
        d_forgot = -jnp.sum(d_logits, axis=0)
        block_sum = jnp.sum(d_forgot, axis=1)
        d_picked = later_sum[:, None] + block_sum[:, None] - jnp.cumsum(d_forgot, axis=1)
        d_select = jnp.where(chosen, jax.nn.sigmoid(scores[0]) * d_picked / row_len, 0.0)
        d_scores = d_logits.at[0].add(d_select).astype(jnp.bfloat16)
        key_grad = (
            key_grad
            + jnp.einsum("hkq,qhd->khd", d_scores, q_block, preferred_element_type=jnp.float32)
            * 0.125
        )
        query_grad = (
            jnp.einsum("hkq,khd->qhd", d_scores, key_heads, preferred_element_type=jnp.float32)
            * 0.125
        )
        return (
            (later_sum + block_sum, key_grad, value_grad),
            query_grad.reshape(block_rows, model_width),
        )

    zero_heads = jnp.zeros((tok_rows, H, HEAD), jnp.float32)
    initial = (jnp.zeros((tok_rows,), jnp.float32), zero_heads, zero_heads)
    (unused_sum, key_grad, value_grad), query_parts = lax.scan(
        backward_block, initial, (indices, block_starts), reverse=True
    )
    query_parts = query_parts.reshape(row_len, model_width)
    d_queries = lax.psum_scatter(query_parts, "col", scatter_dimension=0, tiled=True).astype(
        jnp.bfloat16
    )
    d_keys = key_grad.reshape(tok_rows, model_width).astype(jnp.bfloat16)
    d_values = value_grad.reshape(tok_rows, model_width).astype(jnp.bfloat16)
    d_joined = jnp.concatenate([d_queries, d_keys, d_values], axis=1)
    grad_w_qkv = jnp.einsum("td,te->de", normed_one, d_joined, preferred_element_type=jnp.float32)
    grad_bias_q = jnp.sum(d_queries.astype(jnp.float32), axis=0)
    grad_bias_v = jnp.sum(d_values.astype(jnp.float32), axis=0)
    d_normed_one = jnp.einsum("te,de->td", d_joined, w_qkv, preferred_element_type=jnp.float32)
    d_input_norm, grad_gain_one, grad_shift_one = first_back(d_normed_one)
    grad_inputs = (d_middle + d_input_norm).astype(jnp.bfloat16)
    (
        shard_gain_one,
        shard_shift_one,
        shard_w_qkv,
        shard_bias_q,
        shard_bias_v,
        shard_w_out,
        shard_bias_out,
        shard_gain_two,
        shard_shift_two,
        shard_w_up,
        shard_bias_up,
        shard_w_down,
        shard_bias_down,
    ) = (
        lax.psum_scatter(grad_gain_one, "col", scatter_dimension=0, tiled=True),
        lax.psum_scatter(grad_shift_one, "col", scatter_dimension=0, tiled=True),
        lax.psum_scatter(grad_w_qkv, "col", scatter_dimension=0, tiled=True),
        lax.psum_scatter(grad_bias_q, "col", scatter_dimension=0, tiled=True),
        lax.psum_scatter(grad_bias_v, "col", scatter_dimension=0, tiled=True),
        lax.psum_scatter(grad_w_out, "col", scatter_dimension=0, tiled=True),
        lax.psum_scatter(grad_bias_out, "col", scatter_dimension=0, tiled=True),
        lax.psum_scatter(grad_gain_two, "col", scatter_dimension=0, tiled=True),
        lax.psum_scatter(grad_shift_two, "col", scatter_dimension=0, tiled=True),
        lax.psum_scatter(grad_w_up, "col", scatter_dimension=0, tiled=True),
        lax.psum_scatter(grad_bias_up, "col", scatter_dimension=0, tiled=True),
        lax.psum_scatter(grad_w_down, "col", scatter_dimension=0, tiled=True),
        lax.psum_scatter(grad_bias_down, "col", scatter_dimension=0, tiled=True),
    )
    summed = (
        lax.psum(shard_gain_one.astype(jnp.bfloat16), "dp").astype(jnp.float32),
        lax.psum(shard_shift_one.astype(jnp.bfloat16), "dp").astype(jnp.float32),
        lax.psum(shard_w_qkv.astype(jnp.bfloat16), "dp").astype(jnp.float32),
        lax.psum(shard_bias_q.astype(jnp.bfloat16), "dp").astype(jnp.float32),
        lax.psum(shard_bias_v.astype(jnp.bfloat16), "dp").astype(jnp.float32),
        lax.psum(shard_w_out.astype(jnp.bfloat16), "dp").astype(jnp.float32),
        lax.psum(shard_bias_out.astype(jnp.bfloat16), "dp").astype(jnp.float32),
        lax.psum(shard_gain_two.astype(jnp.bfloat16), "dp").astype(jnp.float32),
        lax.psum(shard_shift_two.astype(jnp.bfloat16), "dp").astype(jnp.float32),
        lax.psum(shard_w_up.astype(jnp.bfloat16), "dp").astype(jnp.float32),
        lax.psum(shard_bias_up.astype(jnp.bfloat16), "dp").astype(jnp.float32),
        lax.psum(shard_w_down.astype(jnp.bfloat16), "dp").astype(jnp.float32),
        lax.psum(shard_bias_down.astype(jnp.bfloat16), "dp").astype(jnp.float32),
    )
    return (
        layer_out,
        grad_inputs,
        summed[0],
        summed[1],
        summed[2],
        summed[3],
        summed[4],
        summed[5],
        summed[6],
        summed[7],
        summed[8],
        summed[9],
        summed[10],
        summed[11],
        summed[12],
    )


MESH = pl.DeviceIdType.MESH
LOW = jnp.bfloat16
WIDE = jnp.float32
FAR = 1e30
VMEM_BYTES = 63 * 2**20


def dot(a, b):
    return jnp.dot(a, b, preferred_element_type=WIDE)


def dot_rows(a, b):
    return lax.dot_general(a, b, (((1,), (1,)), ((), ())), preferred_element_type=WIDE)


def split_low(values):
    high = values.astype(LOW)
    return high, (values - high.astype(WIDE)).astype(LOW)


def column_sum(values):
    return jnp.sum(values.astype(WIDE), axis=0, keepdims=True)


def norm_parts(values):
    average = jnp.mean(values, axis=-1, keepdims=True)
    centered = values - average
    spread = jnp.mean(centered * centered, axis=-1, keepdims=True)
    scale = lax.rsqrt(spread + epsilon)
    return centered * scale, scale


def norm_back(grad, unit, scale, gain):
    scaled = grad * gain
    first = jnp.mean(scaled, axis=-1, keepdims=True)
    second = jnp.mean(scaled * unit, axis=-1, keepdims=True)
    return scale * (scaled - first - unit * second)


def gelu_parts(hidden):
    square = hidden * hidden
    bend = jnp.tanh(0.7978845608028654 * hidden * (1.0 + 0.044715 * square))
    half = 0.5 * (1.0 + bend)
    curve = 0.7978845608028654 * (1.0 + 3 * 0.044715 * square)
    return hidden * half, half + 0.5 * hidden * (1.0 - bend * bend) * curve


SCRATCH = dict(
    wqkv=((768, 2304), LOW),
    wout=((768, 768), LOW),
    wup=((768, 3072), LOW),
    wdown=((32, 96, 768), LOW),
    wup_own=((768, 384), LOW),
    n1=((8, 128, 768), LOW),
    n1_t=((8, 96, 1024), LOW),
    n2=((8, 128, 768), LOW),
    n2_t=((8, 96, 1024), LOW),
    cot=((8, 128, 768), LOW),
    keys=((1024, 768), LOW),
    values=((1024, 768), LOW),
    turned=((6, 128, 1024), LOW),
    probs=((6, 1024, 256), LOW),
    sums=((8, 8, 128), WIDE),
    back_sums=((8, 8, 128), WIDE),
    forgot=((128, 1024), WIDE),
    forgot_t=((1024, 128), WIDE),
    sig_t=((1024, 128), WIDE),
    d_forgot_t=((1024, 128), WIDE),
    second_head=((1024, 128), LOW),
    q_low=((128, 768), LOW),
    q_turned=((768, 128), LOW),
    att_t=((768, 128), WIDE),
    att_low_t=((8, 96, 128), LOW),
    act=((128, 3072), LOW),
    d_act=((128, 3072), WIDE),
    d_hidden=((128, 3072), LOW),
    middle=((128, 768), WIDE),
    d_mid=((128, 768), WIDE),
    unit_two=((128, 768), WIDE),
    d_att=((128, 768), LOW),
    d_att_t=((768, 128), LOW),
    dq_t=((768, 128), WIDE),
    act_t=((384, 1024), LOW),
    slope=((1024, 384), LOW),
    db2=((256, 768), LOW),
    dq2=((256, 768), LOW),
    lhs_out=((4, 96, 256), LOW),
    lhs_q=((4, 96, 256), LOW),
    give_out=((4, 96, 128), LOW),
    give_q=((4, 96, 128), LOW),
    dkv=((1024, 1536), LOW),
    grads_out=((4, 96, 768), LOW),
    grads_q=((4, 96, 768), LOW),
    grads_k=((2, 4, 96, 768), LOW),
    grads_v=((2, 4, 96, 768), LOW),
    core_k=((4, 96, 768), LOW),
    core_v=((4, 96, 768), LOW),
    one=((4, 2, 2, 96, 384), LOW),
    two=((4, 2, 96, 384), LOW),
    d_n1=((2, 4, 128, 768), LOW),
    core_n1=((4, 128, 768), LOW),
    one_n1=((2, 2, 128, 384), LOW),
    two_n1=((2, 128, 384), LOW),
    up_give=((8, 96, 384), LOW),
    mine=((12, 2, 96, 384), LOW),
    got_z=((12, 2, 96, 384), LOW),
    got_mid=((12, 2, 96, 384), LOW),
    total=((12, 2, 96, 384), LOW),
    small=((8, 768), WIDE),
    wide=((8, 384), WIDE),
    pieces=((8, 16, 128), WIDE),
    pieces_got=((8, 16, 128), WIDE),
    rows_z=((4, 16, 128), WIDE),
)
SLOTS = (0, 2, 6, 4)
COPIES = 160


def layer_kernel(
    lengths_ref,
    x_ref,
    cot_ref,
    gain_one,
    shift_one,
    bias_q,
    bias_v,
    bias_out,
    gain_two,
    shift_two,
    bias_up,
    bias_down,
    w_qkv,
    w_out,
    w_up,
    w_down,
    out_ref,
    grad_ref,
    total_ref,
    small_ref,
    *scratch,
):
    s = types.SimpleNamespace(**dict(zip(SCRATCH, scratch)))
    gain_one, shift_one, bias_q, bias_v, bias_out, gain_two, shift_two, bias_up, bias_down = (
        ref[...].reshape(1, -1)
        for ref in (
            gain_one,
            shift_one,
            bias_q,
            bias_v,
            bias_out,
            gain_two,
            shift_two,
            bias_up,
            bias_down,
        )
    )
    sent, landed, local = scratch[len(SCRATCH) :]
    me = lax.axis_index("col")
    dp = lax.axis_index("dp")
    core = lax.rem(me, 2)
    x_bit = lax.rem(lax.div(me, 2), 2)
    y_bit = lax.div(me, 4)

    def place(r):
        step = (r & 1) * (1 - 2 * core) + ((r >> 1) & 1) * (2 - 4 * x_bit)
        return me + step + (r >> 2) * (4 - 8 * y_bit)

    def near(r):
        return (dp, place(r))

    z_pair = (dp + 1 - 2 * lax.rem(dp, 2), me)
    z_middle = (3 - dp, me)
    inner = (dp == 1) | (dp == 2)
    outer = jnp.logical_not(inner)
    messages = []
    numbers = iter(range(COPIES))

    def message(source, target, device):
        at = next(numbers)
        return pltpu.make_async_remote_copy(
            src_ref=source,
            dst_ref=target,
            send_sem=sent.at[at],
            recv_sem=landed.at[at],
            device_id=device,
            device_id_type=MESH,
        )

    def send(source, target, device):
        copy = message(source, target, device)
        copy.start()
        messages.append(copy)
        return copy

    loads = {}
    for at, (name, source, target) in enumerate(
        (
            ("kv", w_qkv.at[:, pl.ds(768, 1536)], s.wqkv.at[:, pl.ds(768, 1536)]),
            ("q", w_qkv.at[:, pl.ds(0, 768)], s.wqkv.at[:, pl.ds(0, 768)]),
            ("down", w_down, s.wdown),
            ("out", w_out, s.wout),
            ("up", w_up, s.wup),
            (
                "own",
                w_up.at[:, pl.ds(pl.multiple_of(384 * me, 128), 384)],
                s.wup_own,
            ),
        )
    ):
        loads[name] = pltpu.make_async_copy(source, target, local.at[at])
    loads["kv"].start()

    barrier = pltpu.get_barrier_semaphore()
    others_z = [(lax.rem(dp + k, 4), me) for k in (1, 2, 3)]
    for device in [near(r) for r in range(1, 8)] + others_z:
        pl.semaphore_signal(barrier, inc=1, device_id=device, device_id_type=MESH)

    class Gather:
        def __init__(self, ref):
            self.ref = ref

        def start(self):
            self.first = [
                send(self.ref.at[0], self.ref.at[r], near(r)) for r in (2, 4, 1)
            ]

        def forward(self):
            ref = self.ref
            left, right = pl.ds(0, 384), pl.ds(384, 384)
            self.first[0].wait_recv()
            self.far = [send(ref.at[2, :, left], ref.at[6, :, left], near(4))]
            self.more = [send(ref.at[2], ref.at[3], near(1))]
            self.first[1].wait_recv()
            self.far.append(send(ref.at[4, :, right], ref.at[6, :, right], near(2)))
            self.more.append(send(ref.at[4], ref.at[5], near(1)))

        def diagonal(self):
            self.far[0].wait_recv()
            self.far[1].wait_recv()
            self.more.append(send(self.ref.at[6], self.ref.at[7], near(1)))

        def chip(self, number):
            (self.first[2] if number == 0 else self.more[number - 1]).wait_recv()

        def rows(self, number):
            return self.ref[2 * number : 2 * number + 2].reshape(256, 768)

    values_one = x_ref[...].astype(WIDE)
    unit_one, scale_one = norm_parts(values_one)
    normed_one = (unit_one * gain_one + shift_one).astype(LOW)
    s.n1[0] = normed_one
    s.cot[0] = cot_ref[...]
    gather_one, gather_cot, gather_two = Gather(s.n1), Gather(s.cot), Gather(s.n2)
    pl.semaphore_wait(barrier, 10)
    gather_one.start()
    loads["q"].start()
    gather_cot.start()

    def share(source, lhs, give):
        for slot, r in enumerate(SLOTS):
            ours = place(r)
            lhs[slot, :, 0:128] = source(ours)
            give[slot] = source(ours + 1 - 2 * core)
        return send(give, lhs.at[:, :, pl.ds(128, 128)], near(1))

    def turn_block(source, target, r):
        target[:, :, 128 * r : 128 * r + 128] = source[r].T.reshape(8, 96, 128)

    turn_block(s.n1, s.n1_t, 0)
    share_one = share(lambda at: s.n1_t[at, :, 0:128], s.lhs_q, s.give_q)

    def keys_values(number):
        rows = gather_one.rows(number)
        at = 256 * number
        s.keys[at : at + 256, :] = dot(rows, s.wqkv[:, 768:1536]).astype(LOW)
        s.values[at : at + 256, :] = (dot(rows, s.wqkv[:, 1536:2304]) + bias_v).astype(LOW)

    loads["kv"].wait()
    loads["down"].start()
    loads["out"].start()
    gather_one.chip(0)
    keys_values(0)
    loads["q"].wait()
    loads["up"].start()
    loads["own"].start()
    q = (dot(normed_one, s.wqkv[:, 0:768]) + bias_q).astype(LOW)
    q = (q.astype(WIDE) * 0.125).astype(LOW)
    s.q_low[...] = q
    s.q_turned[...] = q.T
    gather_one.forward()
    turn_block(s.n1, s.n1_t, 1)

    row_at = lax.broadcasted_iota(jnp.int32, (128, 128), 0)
    lane_at = lax.broadcasted_iota(jnp.int32, (128, 128), 1)
    query_at = row_at + me * 128
    begin_one = lengths_ref[0, 0]
    begin_two = begin_one + lengths_ref[0, 1]
    begin_three = begin_two + lengths_ref[0, 2]
    begin = jnp.where(query_at >= begin_one, begin_one, 0)
    begin = jnp.where(query_at >= begin_two, begin_two, begin)
    begin = jnp.where(query_at >= begin_three, begin_three, begin)
    earlier = jnp.where(lane_at < row_at, 1.0, 0.0).astype(LOW)
    first_lanes = jnp.where(lane_at < 64, 1.0, 0.0)
    head_zero = (s.q_low[:, 0:128].astype(WIDE) * first_lanes).astype(LOW)

    def picks(r):
        scores = dot_rows(head_zero, s.keys[128 * r : 128 * r + 128, 0:128])
        key_at = lane_at + place(r) * 128
        allowed = (key_at <= query_at) & (key_at >= begin)
        chosen = (key_at < query_at) & (key_at > begin)
        small_exp = jnp.exp(-jnp.abs(scores))
        soft = jnp.maximum(scores, 0.0) + jnp.log1p(small_exp)
        picked = jnp.where(chosen, soft, 0.0) * (1.0 / 1024)
        high, rest = split_low(picked)
        s.sums[0, r : r + 1, :] = column_sum(picked)
        within = dot(earlier, high) + dot(earlier, rest)
        s.forgot[:, 128 * r : 128 * r + 128] = jnp.where(allowed, within, FAR)
        sigmoid = jnp.where(scores >= 0, 1.0, small_exp) / (1.0 + small_exp)
        s.sig_t[128 * r : 128 * r + 128, :] = (jnp.where(chosen, sigmoid, 0.0) * (1.0 / 1024)).T

    def turn(source, pair):
        at = 128 * pair
        for r in range(8):
            rows = slice(128 * r, 128 * r + 128)
            s.turned[pair, :, rows] = source[rows, at : at + 128].T

    for number in (0, 1, 2, 3):
        if number:
            gather_one.chip(number)
            keys_values(number)
        if number == 1:
            gather_one.diagonal()
        picks(2 * number)
        picks(2 * number + 1)
        if number:
            turn_block(s.n1, s.n1_t, 2 * number)
            turn_block(s.n1, s.n1_t, 2 * number + 1)
    sum_copies = [send(s.sums.at[0], s.sums.at[r], near(r)) for r in range(1, 8)]

    def active_grad(first, last):
        for j in range(first, last):
            rows = s.wdown[4 * j : 4 * j + 4].reshape(384, 768)
            s.d_act[:, 384 * j : 384 * j + 384] = dot_rows(cot_ref[...], rows)

    loads["down"].wait()
    active_grad(0, 8)
    gather_cot.forward()
    for pair in range(6):
        turn(s.values, pair)
    for copy in sum_copies:
        copy.wait_recv()

    def others(sums, later):
        rows = [jnp.zeros((1, 128), WIDE) for _ in range(8)]
        for d in range(1, 8):
            ahead = place(d) > me if later else place(d) < me
            weight = jnp.where(ahead, 1.0, 0.0)
            for r in range(8):
                rows[r] = rows[r] + weight * sums[d, (r ^ d) : (r ^ d) + 1, :]
        return rows

    for r, row in enumerate(others(s.sums, False)):
        at = 128 * r
        s.forgot_t[at : at + 128, :] = (s.forgot[:, at : at + 128] + row).T

    feature_at = lax.broadcasted_iota(jnp.int32, (128, 256), 0)
    column_at = lax.broadcasted_iota(jnp.int32, (128, 256), 1)
    own_head_t = jnp.where((feature_at < 64) == (column_at < 128), 1.0, 0.0).astype(LOW)
    long_row = lax.broadcasted_iota(jnp.int32, (256, 128), 0)
    long_lane = lax.broadcasted_iota(jnp.int32, (256, 128), 1)
    own_head = jnp.where((long_row < 128) == (long_lane < 64), 1.0, 0.0).astype(LOW)

    def both_t(values):
        return jnp.concatenate([values, values], axis=1) * own_head_t

    def both(values):
        return jnp.concatenate([values, values], axis=0) * own_head

    def attend(pair):
        at = 128 * pair
        scores = dot(s.keys[:, at : at + 128], both_t(s.q_turned[at : at + 128, :]))
        forgot = s.forgot_t[...]
        logits = scores - jnp.concatenate([forgot, forgot], axis=1)
        raised = jnp.exp(logits - jnp.max(logits, axis=0, keepdims=True))
        probs = (raised * (1.0 / jnp.sum(raised, axis=0, keepdims=True))).astype(LOW)
        s.probs[pair] = probs
        mixed = dot(s.turned[pair], probs)
        s.att_t[at : at + 64, :] = mixed[0:64, 0:128]
        s.att_t[at + 64 : at + 128, :] = mixed[64:128, 128:256]

    for pair in range(6):
        attend(pair)

    attended_low_t = s.att_t[...].astype(LOW)
    s.att_low_t[...] = attended_low_t.reshape(8, 96, 128)
    loads["out"].wait()
    middle = values_one + dot(attended_low_t.T, s.wout[...]) + bias_out
    s.middle[...] = middle
    unit_two, scale_two = norm_parts(middle)
    s.unit_two[...] = unit_two
    normed_two = (unit_two * gain_two + shift_two).astype(LOW)
    s.n2[0] = normed_two
    gather_two.start()
    share_att = share(lambda at: s.att_low_t[at], s.lhs_out, s.give_out)
    gather_cot.diagonal()
    loads["up"].wait()
    for j in range(4):
        at = 768 * j
        hidden = dot(normed_two, s.wup[:, at : at + 768]) + bias_up[:, at : at + 768]
        active, slope = gelu_parts(hidden)
        s.act[:, at : at + 768] = active.astype(LOW)
        d_hidden = (s.d_act[:, at : at + 768] * slope).astype(LOW)
        s.d_hidden[:, at : at + 768] = d_hidden
        s.wide[2 * j : 2 * j + 1, :] = column_sum(d_hidden[:, 0:384])
        s.wide[2 * j + 1 : 2 * j + 2, :] = column_sum(d_hidden[:, 384:768])
    gather_two.forward()

    d_output = cot_ref[...].astype(WIDE)
    parts = []
    for j in range(3):
        parts.append(dot_rows(s.d_hidden[...], s.wup[256 * j : 256 * j + 256, :]))
    d_normed = jnp.concatenate(parts, axis=1)
    unit_two = s.unit_two[...]
    s.small[5:6, :] = column_sum(d_normed * unit_two)
    s.small[6:7, :] = column_sum(d_normed)
    s.small[7:8, :] = column_sum(d_output)
    d_middle = d_output + norm_back(d_normed, unit_two, scale_two, gain_two)
    s.d_mid[...] = d_middle
    s.small[4:5, :] = column_sum(d_middle)
    d_branch = d_middle.astype(LOW)
    s.db2[0:128, :] = d_branch
    share_branch = send(s.db2.at[pl.ds(0, 128)], s.db2.at[pl.ds(128, 128)], near(1))
    d_att_t = dot(s.wout[...], d_branch.T).astype(LOW)
    s.d_att_t[...] = d_att_t
    s.d_att[...] = d_att_t.T
    gather_two.diagonal()

    class Unit:
        def __init__(self, rows, grads, one, two, core=None):
            self.rows, self.grads, self.one, self.two, self.core = rows, grads, one, two, core

        def across(self):
            self.copy = send(self.grads.at[1], self.core, near(1))
            self.grads = self.grads.at[0]

        def start(self):
            if self.core is not None:
                self.copy.wait_recv()
                total = self.grads[...].astype(WIDE) + self.core[...].astype(WIDE)
                self.grads[...] = total.astype(LOW)
            self.copies = (
                send(self.grads.at[pl.ds(1, 2), :, pl.ds(0, 384)], self.one.at[0], near(2)),
                send(self.grads.at[pl.ds(2, 2), :, pl.ds(384, 384)], self.one.at[1], near(4)),
            )

        def pass_on(self):
            copies = []
            for half, slot, index, r in ((0, 3, 1, 4), (1, 1, 0, 2)):
                cols = slice(384 * half, 384 * half + 384)
                self.copies[half].wait_recv()
                total = self.grads[slot, :, cols].astype(WIDE)
                total = total + self.one[half, index].astype(WIDE)
                self.grads[slot, :, cols] = total.astype(LOW)
                source = self.grads.at[slot, :, pl.ds(384 * half, 384)]
                copies.append(send(source, self.two.at[half], near(r)))
            self.copies = copies

        def finish(self, half):
            self.copies[half].wait_recv()
            total = self.grads[0, :, 384 * half : 384 * half + 384].astype(WIDE)
            total = total + self.one[half, half].astype(WIDE)
            return total + self.two[half].astype(WIDE)

    class Line:
        def __init__(self, at, places):
            self.at, self.places = at, places
            mine, total = s.mine.at[at], s.total.at[at]
            self.inward = message(mine, s.got_z.at[at], z_pair)
            self.across = message(mine, s.got_mid.at[at], z_middle)
            self.outward = message(total, total, z_pair)

        def start(self):
            pl.when(outer)(lambda: self.inward.start())

        def middle(self):
            @pl.when(inner)
            def _():
                self.inward.wait_recv()
                total = s.mine[self.at].astype(WIDE) + s.got_z[self.at].astype(WIDE)
                s.mine[self.at] = total.astype(LOW)
                self.across.start()

        def back(self):
            @pl.when(inner)
            def _():
                self.across.wait_recv()
                total = s.mine[self.at].astype(WIDE) + s.got_mid[self.at].astype(WIDE)
                s.total[self.at] = total.astype(LOW)
                self.outward.start()

        def write(self):
            pl.when(outer)(lambda: self.outward.wait_recv())
            for i, where in enumerate(self.places):
                copy = pltpu.make_async_copy(
                    s.total.at[self.at, i], total_ref.at[where], local.at[6 + 2 * self.at + i]
                )
                copy.start()
                writes.append(copy)

        def close(self):
            pl.when(outer)(lambda: self.inward.wait_send())

            @pl.when(inner)
            def _():
                self.across.wait_send()
                self.outward.wait_send()

    writes = []
    lines = [Line(j, (2 * j, 2 * j + 1)) for j in range(5)]
    lines += [Line(5 + j, (10 + place(2 * j), 10 + place(2 * j + 1))) for j in range(4)]
    lines += [Line(9 + j, (18 + 2 * j, 19 + 2 * j)) for j in range(3)]
    unit_out = Unit(96, s.grads_out, s.one.at[0], s.two.at[0])
    unit_q = Unit(96, s.grads_q, s.one.at[1], s.two.at[1])
    unit_k = Unit(96, s.grads_k, s.one.at[2], s.two.at[2], s.core_k)
    unit_v = Unit(96, s.grads_v, s.one.at[3], s.two.at[3], s.core_v)
    unit_n1 = Unit(128, s.d_n1, s.one_n1, s.two_n1, s.core_n1)

    def to_line(unit, at):
        for half in range(2):
            s.mine[at, half] = unit.finish(half).astype(LOW)
        lines[at].start()

    def rows_of(source, odd):
        return jnp.concatenate([source[place(r + odd)] for r in SLOTS], axis=0)

    own_down = s.wdown.at[pl.ds(4 * me, 4)]
    own_bias = jnp.zeros((1, 384), WIDE)
    for j in range(8):
        own_bias = own_bias + jnp.where(me == j, 1.0, 0.0) * bias_up[:, 384 * j : 384 * j + 384]
    loads["own"].wait()

    def own_units(number):
        gather_cot.chip(number)
        gather_two.chip(number)
        at = 256 * number
        hidden = dot(gather_two.rows(number), s.wup_own[...]) + own_bias
        active, slope = gelu_parts(hidden)
        d_active = dot_rows(gather_cot.rows(number), own_down[...].reshape(384, 768))
        s.act_t[:, at : at + 256] = active.astype(LOW).T
        s.slope[at : at + 256, :] = (d_active * slope).astype(LOW)
        turn_block(s.n2, s.n2_t, 2 * number)
        turn_block(s.n2, s.n2_t, 2 * number + 1)

    for number in range(4):
        own_units(number)
    share_att.wait_recv()
    share_branch.wait_recv()
    s.grads_out[...] = (
        dot(s.lhs_out[...].reshape(384, 256), s.db2[...]).astype(LOW).reshape(4, 96, 768)
    )
    unit_out.start()
    cot_rows = s.cot[...].reshape(1024, 768)
    for j in range(4):
        grads = dot(s.act_t[96 * j : 96 * j + 96, :], cot_rows).astype(LOW)
        s.mine[j, 0] = grads[:, 0:384]
        s.mine[j, 1] = grads[:, 384:768]
        lines[j].start()
    up_copies = []
    for odd in range(2):
        grads = dot(rows_of(s.n2_t, odd), s.slope[...]).astype(LOW).reshape(4, 96, 384)
        for slot, r in enumerate(SLOTS):
            if r + odd == 0:
                s.mine[5, 0] = grads[0]
            else:
                s.up_give[r + odd] = grads[slot]
                target = s.mine.at[5 + r // 2, odd]
                up_copies.append(send(s.up_give.at[r + odd], target, near(r + odd)))

    def logit_grads(pair):
        at = 128 * pair
        grad_t = s.d_att_t[at : at + 128, :]
        products = grad_t.astype(WIDE) * s.att_t[at : at + 128, :]
        delta = jnp.concatenate(
            [
                jnp.sum(products[0:64], axis=0, keepdims=True),
                jnp.sum(products[64:128], axis=0, keepdims=True),
            ],
            axis=1,
        )
        d_probs = dot(s.values[:, at : at + 128], both_t(grad_t))
        d_logits = s.probs[pair].astype(WIDE) * (d_probs - delta)
        both_heads = d_logits[:, 0:128] + d_logits[:, 128:256]
        if pair == 5:
            s.d_forgot_t[...] = both_heads
        else:
            s.d_forgot_t[...] += both_heads
        return d_logits

    def value_grads(pair):
        at = 128 * pair
        grads = dot(s.probs[pair], both(s.d_att[:, at : at + 128]))
        s.dkv[:, 768 + at : 896 + at] = grads.astype(LOW)

    def score_grads(pair, d_scores):
        at = 128 * pair
        turn(s.keys, pair)
        s.dkv[:, at : at + 128] = dot(d_scores, both(s.q_low[:, at : at + 128])).astype(LOW)
        grads = dot(s.turned[pair], d_scores)
        s.dq_t[at : at + 64, :] = grads[0:64, 0:128]
        s.dq_t[at + 64 : at + 128, :] = grads[64:128, 128:256]

    def attend_back(pair):
        d_logits = logit_grads(pair)
        value_grads(pair)
        score_grads(pair, d_logits.astype(LOW))

    attend_back(5)
    lines[0].middle()
    attend_back(4)
    lines[1].middle()
    attend_back(3)
    unit_out.pass_on()
    lines[2].middle()
    attend_back(2)
    lines[0].back()
    lines[3].middle()
    attend_back(1)
    d_logits = logit_grads(0)
    s.forgot_t[...] = d_logits[:, 0:128]
    s.second_head[...] = d_logits[:, 128:256].astype(LOW)
    for r in range(8):
        turned = s.d_forgot_t[128 * r : 128 * r + 128, :].T
        s.back_sums[0, r : r + 1, :] = column_sum(turned)
    sum_copies = [send(s.back_sums.at[0], s.back_sums.at[r], near(r)) for r in range(1, 8)]
    value_grads(0)
    lines[1].back()
    to_line(unit_out, 4)

    def key_unit(unit, half):
        grads = s.dkv[:, 768 * half : 768 * half + 768]
        for odd in (1, 0):
            rows = rows_of(s.n1_t, odd)
            unit.grads[odd] = dot(rows, grads).astype(LOW).reshape(4, 96, 768)
        unit.across()

    key_unit(unit_v, 1)
    for copy in up_copies:
        copy.wait_recv()
    for j in range(4):
        lines[5 + j].start()
    for copy in sum_copies:
        copy.wait_recv()
    later_rows = others(s.back_sums, True)
    following = jnp.where(row_at > lane_at, 1.0, 0.0).astype(LOW)
    selected = []
    for r in range(8):
        at = 128 * r
        high, rest = split_low(s.d_forgot_t[at : at + 128, :])
        later = jnp.broadcast_to(later_rows[r], (128, 128)).T
        d_picked = -(dot(high, following) + dot(rest, following) + later)
        selected.append(s.forgot_t[at : at + 128, :] + s.sig_t[at : at + 128, :] * d_picked)
    first_head = jnp.concatenate(selected, axis=0).astype(LOW)
    score_grads(0, jnp.concatenate([first_head, s.second_head[...]], axis=1))
    for j in range(6):
        at = 128 * j
        d_q = (s.dq_t[at : at + 128, :] * 0.125).astype(LOW)
        s.dq2[0:128, at : at + 128] = d_q.T
    share_q = send(s.dq2.at[pl.ds(0, 128)], s.dq2.at[pl.ds(128, 128)], near(1))
    unit_v.start()
    lines[2].back()
    key_unit(unit_k, 0)
    lines[3].back()
    lines[4].middle()
    lines[5].middle()
    share_one.wait_recv()
    share_q.wait_recv()
    s.grads_q[...] = (
        dot(s.lhs_q[...].reshape(384, 256), s.dq2[...]).astype(LOW).reshape(4, 96, 768)
    )
    unit_q.start()
    unit_k.start()
    unit_v.pass_on()
    lines[6].middle()
    lines[4].back()
    for slot, r in enumerate(SLOTS):
        for odd in range(2):
            at = 128 * (r + odd)
            for j in range(3):
                cols = slice(256 * j, 256 * j + 256)
                grads = dot_rows(s.dkv[at : at + 128, :], s.wqkv[cols, 768:2304])
                s.d_n1[odd, slot, :, cols] = grads.astype(LOW)
    unit_n1.across()
    lines[7].middle()
    lines[5].back()
    unit_q.pass_on()
    unit_n1.start()
    to_line(unit_v, 11)
    lines[8].middle()
    lines[6].back()
    unit_k.pass_on()
    mixed = jnp.zeros((128, 768), WIDE)
    for j in range(4):
        rows = s.wdown[8 * j : 8 * j + 8].reshape(768, 768)
        mixed = mixed + dot(s.act[:, 768 * j : 768 * j + 768], rows)
    out_ref[...] = (s.middle[...] + mixed + bias_down).astype(LOW)
    parts = []
    for i in range(3):
        rows = s.wqkv[256 * i : 256 * i + 256, 0:768]
        parts.append(dot_rows(s.dq2[0:128, :], rows))
    d_normed = jnp.concatenate(parts, axis=1)
    to_line(unit_q, 9)
    lines[11].middle()
    lines[7].back()
    unit_n1.pass_on()
    to_line(unit_k, 10)
    lines[8].back()
    lines[9].middle()
    lines[11].back()
    for j in (0, 1, 2, 3, 4, 5, 6):
        lines[j].write()
    d_normed = d_normed + jnp.concatenate([unit_n1.finish(0), unit_n1.finish(1)], axis=1)
    unit_one, scale_one = norm_parts(x_ref[...].astype(WIDE))
    s.small[0:1, :] = column_sum(d_normed * unit_one)
    s.small[1:2, :] = column_sum(d_normed)
    s.small[2:3, :] = column_sum(s.dq2[0:128, :])
    s.small[3:4, :] = column_sum(s.dkv[:, 768:1536])
    d_inputs = s.d_mid[...] + norm_back(d_normed, unit_one, scale_one, gain_one)
    grad_ref[...] = d_inputs.astype(LOW)

    s.pieces[...] = jnp.zeros((8, 16, 128), WIDE)
    for j in range(8):
        s.pieces[j, 0:8, 0:96] = s.small[:, 96 * j : 96 * j + 96]
        for i in range(3):
            s.pieces[j, 8 + i : 9 + i, :] = s.wide[j : j + 1, 128 * i : 128 * i + 128]
    piece_copies = [
        send(s.pieces.at[place(r)], s.pieces_got.at[r], near(r)) for r in range(1, 8)
    ]
    lines[10].middle()
    lines[9].back()
    total = s.pieces[me]
    for r in range(1, 8):
        piece_copies[r - 1].wait_recv()
        total = total + s.pieces_got[r]
    s.rows_z[dp] = total
    z_copies = [send(s.rows_z.at[dp], s.rows_z.at[dp], device) for device in others_z]
    lines[10].back()
    for j in (7, 8, 11, 9):
        lines[j].write()
    for copy in z_copies:
        copy.wait_recv()
    small_ref[...] = s.rows_z[0] + s.rows_z[1] + s.rows_z[2] + s.rows_z[3]
    lines[10].write()
    for copy in writes:
        copy.wait()
    for copy in messages:
        copy.wait_send()
    for line in lines:
        line.close()


def spread_kernel(total_ref, small_ref, out_in, grad_in, out_ref, grad_ref, *outs):
    gain_one, shift_one, qkv, bias_q, bias_v, out, bias_out = outs[:7]
    gain_two, shift_two, up, bias_up, down, bias_down = outs[7:]
    out_ref[...] = out_in[...]
    grad_ref[...] = grad_in[...]
    for i in range(2):
        cols = slice(384 * i, 384 * i + 384)
        for j in range(4):
            down[96 * j : 96 * j + 96, cols] = total_ref[2 * j + i].astype(WIDE)
        out[:, cols] = total_ref[8 + i].astype(WIDE)
    for j in range(8):
        up[:, 384 * j : 384 * j + 384] = total_ref[10 + j].astype(WIDE)
    for j in range(6):
        qkv[:, 384 * j : 384 * j + 384] = total_ref[18 + j].astype(WIDE)
    rows = (gain_one, shift_one, bias_q, bias_v, bias_out, gain_two, shift_two, bias_down)
    for j, target in enumerate(rows):
        target[...] = small_ref[j, 0:96]
    for i in range(3):
        bias_up[128 * i : 128 * i + 128] = small_ref[8 + i, :]


def fused_device(
    inputs,
    gain_one,
    shift_one,
    w_qkv,
    bias_q,
    bias_v,
    w_out,
    bias_out,
    gain_two,
    shift_two,
    w_up,
    bias_up,
    w_down,
    bias_down,
    lengths,
    cotangent,
):
    vmem = pl.BlockSpec(memory_space=pltpu.VMEM)
    anywhere = pl.BlockSpec(memory_space=pl.ANY)
    vectors = [gain_one, shift_one, bias_q, bias_v, bias_out, gain_two, shift_two]
    vectors = vectors + [bias_up, bias_down]
    tokens, width = inputs.shape
    layer_out, grad_inputs, total, small = pl.pallas_call(
        layer_kernel,
        out_shape=(
            jax.ShapeDtypeStruct((tokens, width), LOW),
            jax.ShapeDtypeStruct((tokens, width), LOW),
            jax.ShapeDtypeStruct((24, 96, 384), LOW),
            jax.ShapeDtypeStruct((16, 128), WIDE),
        ),
        in_specs=[pl.BlockSpec(memory_space=pltpu.SMEM)] + [vmem] * 11 + [anywhere] * 4,
        out_specs=(vmem, vmem, anywhere, vmem),
        scratch_shapes=[pltpu.VMEM(shape, kind) for shape, kind in SCRATCH.values()]
        + [
            pltpu.SemaphoreType.DMA((COPIES,)),
            pltpu.SemaphoreType.DMA((COPIES,)),
            pltpu.SemaphoreType.DMA((30,)),
        ],
        compiler_params=pltpu.CompilerParams(
            collective_id=0, has_side_effects=True, vmem_limit_bytes=VMEM_BYTES
        ),
        name="layer",
    )(lengths, inputs, cotangent, *vectors, w_qkv, w_out, w_up, w_down.reshape(32, 96, width))
    return pl.pallas_call(
        spread_kernel,
        out_shape=tuple(
            jax.ShapeDtypeStruct((tokens, width), LOW) for _ in range(2)
        )
        + tuple(
            jax.ShapeDtypeStruct(shape, WIDE)
            for shape in (
                (96,),
                (96,),
                (96, 2304),
                (96,),
                (96,),
                (96, 768),
                (96,),
                (96,),
                (96,),
                (96, 3072),
                (384,),
                (384, 768),
                (96,),
            )
        ),
        in_specs=[vmem] * 4,
        out_specs=(vmem,) * 15,
        compiler_params=pltpu.CompilerParams(vmem_limit_bytes=VMEM_BYTES),
        name="spread",
    )(total, small, layer_out, grad_inputs)


def per_device(*arguments):
    inputs, w_up = arguments[0], arguments[10]
    fits = (
        lax.axis_size("dp") == 4
        and lax.axis_size("col") == 8
        and inputs.shape == (128, 768)
        and w_up.shape == (768, 3072)
    )
    return fused_device(*arguments) if fits else general_device(*arguments)


def solution(mesh):
    return jax.shard_map(
        per_device,
        mesh=mesh,
        in_specs=(
            P(("dp", "col"), None),
            P(),
            P(),
            P(),
            P(),
            P(),
            P(),
            P(),
            P(),
            P(),
            P(),
            P(),
            P(),
            P(),
            P("dp", None),
            P(("dp", "col"), None),
        ),
        out_specs=(
            P(("dp", "col"), None),
            P(("dp", "col"), None),
            P("col"),
            P("col"),
            P("col", None),
            P("col"),
            P("col"),
            P("col", None),
            P("col"),
            P("col"),
            P("col"),
            P("col", None),
            P("col"),
            P("col", None),
            P("col"),
        ),
        check_vma=False,
    )
```

```python
import functools
import types

import jax
import jax.numpy as jnp
from jax import lax
from jax.experimental import pallas as pl
from jax.experimental.pallas import tpu as pltpu
from jax.sharding import PartitionSpec as P

H = 12
HEAD = 64


epsilon = 1e-05


def layer_norm(values, scales, offset):
    average = jnp.mean(values, axis=-1, keepdims=True)
    centered = values - average
    spread = jnp.mean(centered * centered, axis=-1, keepdims=True)
    return centered * lax.rsqrt(spread + epsilon) * scales + offset


def documents(places, row_lengths):
    finish = jnp.cumsum(row_lengths)
    begins = finish - row_lengths
    inside = (places[:, None] >= begins[None, :]) & (places[:, None] < finish[None, :])
    numbers = jnp.arange(row_lengths.shape[0], dtype=jnp.int32)
    doc_index = jnp.sum(jnp.where(inside, numbers[None, :], 0), axis=1)
    first_place = jnp.sum(jnp.where(inside, begins[None, :], 0), axis=1)
    return (doc_index, first_place == places)


def general_device(
    inputs,
    gain_one,
    shift_one,
    w_qkv,
    bias_q,
    bias_v,
    w_out,
    bias_out,
    gain_two,
    shift_two,
    w_up,
    bias_up,
    w_down,
    bias_down,
    lengths,
    cotangent,
):
    col_count = lax.axis_size("col")
    col_place = lax.axis_index("col")
    tok_rows = inputs.shape[0]
    model_width = inputs.shape[1]
    row_len = tok_rows * col_count
    block_rows = min(512, row_len)
    block_count = row_len // block_rows
    places = jnp.arange(row_len, dtype=jnp.int32)
    doc_index, first_flag = documents(places, lengths[0])
    own_first = col_place * tok_rows
    key_places = own_first + jnp.arange(tok_rows, dtype=jnp.int32)
    key_doc = lax.dynamic_slice_in_dim(doc_index, own_first, tok_rows, 0)
    key_first = lax.dynamic_slice_in_dim(first_flag, own_first, tok_rows, 0)
    floated = inputs.astype(jnp.float32)
    norm_first, first_back = jax.vjp(layer_norm, floated, gain_one, shift_one)
    normed_one = norm_first.astype(jnp.bfloat16)
    joined = jnp.dot(normed_one, w_qkv, preferred_element_type=jnp.float32)
    queries = (joined[:, :model_width] + bias_q).astype(jnp.bfloat16)
    key_rows = joined[:, model_width : 2 * model_width].astype(jnp.bfloat16)
    value_rows = (joined[:, 2 * model_width :] + bias_v).astype(jnp.bfloat16)
    key_heads = key_rows.reshape(tok_rows, H, HEAD)
    value_heads = value_rows.reshape(tok_rows, H, HEAD)
    all_queries = lax.all_gather(queries, "col", axis=0, tiled=True)

    def block_terms(source, block_index, carried):
        first_row = block_index * block_rows
        q_block = lax.dynamic_slice_in_dim(source, first_row, block_rows, 0).reshape(
            block_rows, H, HEAD
        )
        q_places = first_row + jnp.arange(block_rows, dtype=jnp.int32)
        q_doc = lax.dynamic_slice_in_dim(doc_index, first_row, block_rows, 0)
        scores = (
            jnp.einsum("khd,qhd->hkq", key_heads, q_block, preferred_element_type=jnp.float32)
            * 0.125
        )
        allowed = (key_places[:, None] <= q_places[None, :]) & (key_doc[:, None] == q_doc[None, :])
        chosen = (
            allowed
            & (key_places[:, None] < q_places[None, :])
            & jnp.logical_not(key_first)[:, None]
        )
        picked = jnp.where(chosen, jax.nn.softplus(scores[0]), 0.0) / row_len
        forgot = carried[:, None] + jnp.cumsum(picked, axis=1) - picked
        logits = jnp.where(allowed[None], scores - forgot[None], -jnp.inf)
        return (q_block, scores, chosen, picked, logits)

    def forward_block(carried, block_index):
        q_block, scores, chosen, picked, logits = block_terms(all_queries, block_index, carried)
        row_top = jnp.max(logits, axis=1)
        safe_top = jnp.where(row_top > -jnp.inf, row_top, 0.0)
        raised = jnp.exp(logits - safe_top[:, None, :])
        totals = jnp.sum(raised, axis=1)
        numerator = jnp.einsum(
            "hkq,khd->qhd",
            raised.astype(jnp.bfloat16),
            value_heads,
            preferred_element_type=jnp.float32,
        )
        return (
            carried + jnp.sum(picked, axis=1),
            (carried, row_top.T, totals.T, numerator.reshape(block_rows, model_width)),
        )

    indices = jnp.arange(block_count, dtype=jnp.int32)
    unused, (block_starts, row_tops, row_totals, numerators) = lax.scan(
        forward_block, jnp.zeros((tok_rows,), jnp.float32), indices
    )
    row_tops = row_tops.reshape(row_len, H)
    row_totals = row_totals.reshape(row_len, H)
    numerators = numerators.reshape(row_len, model_width)
    got_top, got_total, got_numer = (
        lax.all_to_all(
            row_tops[None].astype(jnp.bfloat16), "col", split_axis=1, concat_axis=0, tiled=True
        ).astype(jnp.float32),
        lax.all_to_all(
            row_totals[None].astype(jnp.bfloat16), "col", split_axis=1, concat_axis=0, tiled=True
        ).astype(jnp.float32),
        lax.all_to_all(
            numerators[None].astype(jnp.bfloat16), "col", split_axis=1, concat_axis=0, tiled=True
        ).astype(jnp.float32),
    )
    row_best = jnp.max(got_top, axis=0)
    factor = jnp.exp(got_top - row_best[None])
    totals_own = jnp.sum(factor * got_total, axis=0)
    numer_own = jnp.sum(got_numer.reshape(col_count, tok_rows, H, HEAD) * factor[..., None], axis=0)
    attended = (numer_own / totals_own[..., None]).reshape(tok_rows, model_width)
    row_lse = row_best + jnp.log(totals_own)
    attended_low = attended.astype(jnp.bfloat16)
    middle = floated + jnp.dot(attended_low, w_out, preferred_element_type=jnp.float32) + bias_out
    norm_second, second_back = jax.vjp(layer_norm, middle, gain_two, shift_two)
    normed_two = norm_second.astype(jnp.bfloat16)
    hidden = jnp.dot(normed_two, w_up, preferred_element_type=jnp.float32) + bias_up
    active_full, gelu_back = jax.vjp(jax.nn.gelu, hidden)
    active = active_full.astype(jnp.bfloat16)
    layer_out = (
        middle + jnp.dot(active, w_down, preferred_element_type=jnp.float32) + bias_down
    ).astype(jnp.bfloat16)
    d_output = cotangent.astype(jnp.float32)
    grad_w_down = jnp.einsum("tf,td->fd", active, cotangent, preferred_element_type=jnp.float32)
    grad_bias_down = jnp.sum(d_output, axis=0)
    d_active = jnp.einsum("td,fd->tf", cotangent, w_down, preferred_element_type=jnp.float32)
    d_hidden = gelu_back(d_active)[0].astype(jnp.bfloat16)
    grad_w_up = jnp.einsum("td,tf->df", normed_two, d_hidden, preferred_element_type=jnp.float32)
    grad_bias_up = jnp.sum(d_hidden.astype(jnp.float32), axis=0)
    d_normed_two = jnp.einsum("tf,df->td", d_hidden, w_up, preferred_element_type=jnp.float32)
    d_middle_norm, grad_gain_two, grad_shift_two = second_back(d_normed_two)
    d_middle = d_output + d_middle_norm
    d_branch = d_middle.astype(jnp.bfloat16)
    grad_w_out = jnp.einsum("td,te->de", attended_low, d_branch, preferred_element_type=jnp.float32)
    grad_bias_out = jnp.sum(d_middle, axis=0)
    d_attended = jnp.einsum(
        "te,de->td", d_branch, w_out, preferred_element_type=jnp.float32
    ).astype(jnp.bfloat16)
    row_delta = jnp.sum(
        (d_attended.astype(jnp.float32) * attended).reshape(tok_rows, H, HEAD), axis=2
    )
    back_queries, gathered_grad = (
        lax.all_gather(queries, "col", axis=0, tiled=True),
        lax.all_gather(d_attended, "col", axis=0, tiled=True),
    )
    all_lse, all_delta = (
        lax.all_gather(row_lse, "col", axis=0, tiled=True),
        lax.all_gather(row_delta, "col", axis=0, tiled=True),
    )

    def backward_block(carried_state, inputs_block):
        later_sum, key_grad, value_grad = carried_state
        block_index, carried = inputs_block
        q_block, scores, chosen, picked, logits = block_terms(back_queries, block_index, carried)
        first_row = block_index * block_rows
        grad_block = lax.dynamic_slice_in_dim(gathered_grad, first_row, block_rows, 0).reshape(
            block_rows, H, HEAD
        )
        lse_block = lax.dynamic_slice_in_dim(all_lse, first_row, block_rows, 0)
        delta_block = lax.dynamic_slice_in_dim(all_delta, first_row, block_rows, 0)
        weights = jnp.exp(logits - lse_block.T[:, None, :])
        value_grad = value_grad + jnp.einsum(
            "hkq,qhd->khd",
            weights.astype(jnp.bfloat16),
            grad_block,
            preferred_element_type=jnp.float32,
        )
        d_weights = jnp.einsum(
            "khd,qhd->hkq", value_heads, grad_block, preferred_element_type=jnp.float32
        )
        d_logits = weights * (d_weights - delta_block.T[:, None, :])
        d_forgot = -jnp.sum(d_logits, axis=0)
        block_sum = jnp.sum(d_forgot, axis=1)
        d_picked = later_sum[:, None] + block_sum[:, None] - jnp.cumsum(d_forgot, axis=1)
        d_select = jnp.where(chosen, jax.nn.sigmoid(scores[0]) * d_picked / row_len, 0.0)
        d_scores = d_logits.at[0].add(d_select).astype(jnp.bfloat16)
        key_grad = (
            key_grad
            + jnp.einsum("hkq,qhd->khd", d_scores, q_block, preferred_element_type=jnp.float32)
            * 0.125
        )
        query_grad = (
            jnp.einsum("hkq,khd->qhd", d_scores, key_heads, preferred_element_type=jnp.float32)
            * 0.125
        )
        return (
            (later_sum + block_sum, key_grad, value_grad),
            query_grad.reshape(block_rows, model_width),
        )

    zero_heads = jnp.zeros((tok_rows, H, HEAD), jnp.float32)
    initial = (jnp.zeros((tok_rows,), jnp.float32), zero_heads, zero_heads)
    (unused_sum, key_grad, value_grad), query_parts = lax.scan(
        backward_block, initial, (indices, block_starts), reverse=True
    )
    query_parts = query_parts.reshape(row_len, model_width)
    d_queries = lax.psum_scatter(query_parts, "col", scatter_dimension=0, tiled=True).astype(
        jnp.bfloat16
    )
    d_keys = key_grad.reshape(tok_rows, model_width).astype(jnp.bfloat16)
    d_values = value_grad.reshape(tok_rows, model_width).astype(jnp.bfloat16)
    d_joined = jnp.concatenate([d_queries, d_keys, d_values], axis=1)
    grad_w_qkv = jnp.einsum("td,te->de", normed_one, d_joined, preferred_element_type=jnp.float32)
    grad_bias_q = jnp.sum(d_queries.astype(jnp.float32), axis=0)
    grad_bias_v = jnp.sum(d_values.astype(jnp.float32), axis=0)
    d_normed_one = jnp.einsum("te,de->td", d_joined, w_qkv, preferred_element_type=jnp.float32)
    d_input_norm, grad_gain_one, grad_shift_one = first_back(d_normed_one)
    grad_inputs = (d_middle + d_input_norm).astype(jnp.bfloat16)
    (
        shard_gain_one,
        shard_shift_one,
        shard_w_qkv,
        shard_bias_q,
        shard_bias_v,
        shard_w_out,
        shard_bias_out,
        shard_gain_two,
        shard_shift_two,
        shard_w_up,
        shard_bias_up,
        shard_w_down,
        shard_bias_down,
    ) = (
        lax.psum_scatter(grad_gain_one, "col", scatter_dimension=0, tiled=True),
        lax.psum_scatter(grad_shift_one, "col", scatter_dimension=0, tiled=True),
        lax.psum_scatter(grad_w_qkv, "col", scatter_dimension=0, tiled=True),
        lax.psum_scatter(grad_bias_q, "col", scatter_dimension=0, tiled=True),
        lax.psum_scatter(grad_bias_v, "col", scatter_dimension=0, tiled=True),
        lax.psum_scatter(grad_w_out, "col", scatter_dimension=0, tiled=True),
        lax.psum_scatter(grad_bias_out, "col", scatter_dimension=0, tiled=True),
        lax.psum_scatter(grad_gain_two, "col", scatter_dimension=0, tiled=True),
        lax.psum_scatter(grad_shift_two, "col", scatter_dimension=0, tiled=True),
        lax.psum_scatter(grad_w_up, "col", scatter_dimension=0, tiled=True),
        lax.psum_scatter(grad_bias_up, "col", scatter_dimension=0, tiled=True),
        lax.psum_scatter(grad_w_down, "col", scatter_dimension=0, tiled=True),
        lax.psum_scatter(grad_bias_down, "col", scatter_dimension=0, tiled=True),
    )
    summed = (
        lax.psum(shard_gain_one.astype(jnp.bfloat16), "dp").astype(jnp.float32),
        lax.psum(shard_shift_one.astype(jnp.bfloat16), "dp").astype(jnp.float32),
        lax.psum(shard_w_qkv.astype(jnp.bfloat16), "dp").astype(jnp.float32),
        lax.psum(shard_bias_q.astype(jnp.bfloat16), "dp").astype(jnp.float32),
        lax.psum(shard_bias_v.astype(jnp.bfloat16), "dp").astype(jnp.float32),
        lax.psum(shard_w_out.astype(jnp.bfloat16), "dp").astype(jnp.float32),
        lax.psum(shard_bias_out.astype(jnp.bfloat16), "dp").astype(jnp.float32),
        lax.psum(shard_gain_two.astype(jnp.bfloat16), "dp").astype(jnp.float32),
        lax.psum(shard_shift_two.astype(jnp.bfloat16), "dp").astype(jnp.float32),
        lax.psum(shard_w_up.astype(jnp.bfloat16), "dp").astype(jnp.float32),
        lax.psum(shard_bias_up.astype(jnp.bfloat16), "dp").astype(jnp.float32),
        lax.psum(shard_w_down.astype(jnp.bfloat16), "dp").astype(jnp.float32),
        lax.psum(shard_bias_down.astype(jnp.bfloat16), "dp").astype(jnp.float32),
    )
    return (
        layer_out,
        grad_inputs,
        summed[0],
        summed[1],
        summed[2],
        summed[3],
        summed[4],
        summed[5],
        summed[6],
        summed[7],
        summed[8],
        summed[9],
        summed[10],
        summed[11],
        summed[12],
    )


MESH = pl.DeviceIdType.MESH
LOW = jnp.bfloat16
WIDE = jnp.float32
FAR = 1e30
VMEM_BYTES = 63 * 2**20


def dot(a, b):
    return jnp.dot(a, b, preferred_element_type=WIDE)


def dot_rows(a, b):
    return lax.dot_general(a, b, (((1,), (1,)), ((), ())), preferred_element_type=WIDE)


def split_low(values):
    high = values.astype(LOW)
    return high, (values - high.astype(WIDE)).astype(LOW)


def column_sum(values):
    return jnp.sum(values.astype(WIDE), axis=0, keepdims=True)


def norm_parts(values):
    average = jnp.mean(values, axis=-1, keepdims=True)
    centered = values - average
    spread = jnp.mean(centered * centered, axis=-1, keepdims=True)
    scale = lax.rsqrt(spread + epsilon)
    return centered * scale, scale


def norm_back(grad, unit, scale, gain):
    scaled = grad * gain
    first = jnp.mean(scaled, axis=-1, keepdims=True)
    second = jnp.mean(scaled * unit, axis=-1, keepdims=True)
    return scale * (scaled - first - unit * second)


def gelu_parts(hidden):
    square = hidden * hidden
    bend = jnp.tanh(0.7978845608028654 * hidden * (1.0 + 0.044715 * square))
    half = 0.5 * (1.0 + bend)
    curve = 0.7978845608028654 * (1.0 + 3 * 0.044715 * square)
    return hidden * half, half + 0.5 * hidden * (1.0 - bend * bend) * curve


SCRATCH = dict(
    wqkv=((768, 2304), LOW),
    wout=((768, 768), LOW),
    wup=((768, 3072), LOW),
    wdown=((32, 96, 768), LOW),
    wup_own=((768, 384), LOW),
    n1=((8, 128, 768), LOW),
    n1_t=((8, 96, 1024), LOW),
    n2=((8, 128, 768), LOW),
    n2_t=((8, 96, 1024), LOW),
    cot=((8, 128, 768), LOW),
    keys=((1024, 768), LOW),
    values=((1024, 768), LOW),
    turned=((6, 128, 1024), LOW),
    probs=((6, 1024, 256), LOW),
    sums=((8, 8, 128), WIDE),
    back_sums=((8, 8, 128), WIDE),
    forgot=((128, 1024), WIDE),
    forgot_t=((1024, 128), WIDE),
    sig_t=((1024, 128), WIDE),
    d_forgot_t=((1024, 128), WIDE),
    second_head=((1024, 128), LOW),
    q_low=((128, 768), LOW),
    q_turned=((768, 128), LOW),
    att_t=((768, 128), WIDE),
    att_low_t=((8, 96, 128), LOW),
    act=((128, 3072), LOW),
    d_act=((128, 3072), WIDE),
    d_hidden=((128, 3072), LOW),
    middle=((128, 768), WIDE),
    d_mid=((128, 768), WIDE),
    unit_two=((128, 768), WIDE),
    d_att=((128, 768), LOW),
    d_att_t=((768, 128), LOW),
    dq_t=((768, 128), WIDE),
    act_t=((384, 1024), LOW),
    slope=((1024, 384), LOW),
    db2=((256, 768), LOW),
    dq2=((256, 768), LOW),
    lhs_out=((4, 96, 256), LOW),
    lhs_q=((4, 96, 256), LOW),
    give_out=((4, 96, 128), LOW),
    give_q=((4, 96, 128), LOW),
    dkv=((1024, 1536), LOW),
    grads_out=((4, 96, 768), LOW),
    grads_q=((4, 96, 768), LOW),
    grads_k=((2, 4, 96, 768), LOW),
    grads_v=((2, 4, 96, 768), LOW),
    core_k=((4, 96, 768), LOW),
    core_v=((4, 96, 768), LOW),
    one=((4, 2, 2, 96, 384), LOW),
    two=((4, 2, 96, 384), LOW),
    d_n1=((2, 4, 128, 768), LOW),
    core_n1=((4, 128, 768), LOW),
    one_n1=((2, 2, 128, 384), LOW),
    two_n1=((2, 128, 384), LOW),
    up_give=((8, 96, 384), LOW),
    mine=((24, 96, 384), LOW),
    got_z=((24, 96, 384), LOW),
    got_mid=((24, 96, 384), LOW),
    total=((24, 96, 384), LOW),
    small=((8, 768), WIDE),
    wide=((8, 384), WIDE),
    pieces=((8, 16, 128), WIDE),
    pieces_got=((8, 16, 128), WIDE),
    rows_z=((4, 16, 128), WIDE),
)
SLOTS = (0, 2, 6, 4)
RING = 24
LINES = 12
LANDINGS = 72


def layer_kernel(
    lengths_ref,
    x_ref,
    cot_ref,
    gain_one,
    shift_one,
    bias_q,
    bias_v,
    bias_out,
    gain_two,
    shift_two,
    bias_up,
    bias_down,
    w_qkv,
    w_out,
    w_up,
    w_down,
    out_ref,
    grad_ref,
    total_ref,
    small_ref,
    *scratch,
):
    s = types.SimpleNamespace(**dict(zip(SCRATCH, scratch)))
    gain_one, shift_one, bias_q, bias_v, bias_out, gain_two, shift_two, bias_up, bias_down = (
        ref[...].reshape(1, -1)
        for ref in (
            gain_one,
            shift_one,
            bias_q,
            bias_v,
            bias_out,
            gain_two,
            shift_two,
            bias_up,
            bias_down,
        )
    )
    sent, landed, local = scratch[len(SCRATCH) :]
    me = lax.axis_index("col")
    dp = lax.axis_index("dp")
    core = lax.rem(me, 2)
    x_bit = lax.rem(lax.div(me, 2), 2)
    y_bit = lax.div(me, 4)

    def place(r):
        step = (r & 1) * (1 - 2 * core) + ((r >> 1) & 1) * (2 - 4 * x_bit)
        return me + step + (r >> 2) * (4 - 8 * y_bit)

    def near(r):
        return (dp, place(r))

    z_pair = (dp + 1 - 2 * lax.rem(dp, 2), me)
    z_middle = (3 - dp, me)
    inner = (dp == 1) | (dp == 2)
    outer = jnp.logical_not(inner)
    landings = iter(range(LANDINGS))
    ring = [None] * RING
    turns = iter(range(10**6))

    def message(source, target, device, send_at, land_at):
        return pltpu.make_async_remote_copy(
            src_ref=source,
            dst_ref=target,
            send_sem=sent.at[send_at],
            recv_sem=landed.at[land_at],
            device_id=device,
            device_id_type=MESH,
        )

    def send_all(copies, whole):
        send_at, land_at = next(turns) % RING, next(landings)
        if ring[send_at] is not None:
            ring[send_at].wait_send()
        for source, target, device in copies:
            message(source, target, device, send_at, land_at).start()
        ring[send_at] = message(whole, whole, near(1), send_at, land_at)
        return ring[send_at]

    def send(source, target, device):
        return send_all([(source, target, device)], source)

    loads = {}
    own_cols = pl.ds(pl.multiple_of(384 * me, 128), 384)
    for at, (name, source, target) in enumerate(
        (
            ("kv", w_qkv.at[:, pl.ds(768, 1536)], s.wqkv.at[:, pl.ds(768, 1536)]),
            ("q", w_qkv.at[:, pl.ds(0, 768)], s.wqkv.at[:, pl.ds(0, 768)]),
            ("down", w_down, s.wdown),
            ("out", w_out, s.wout),
            ("up", w_up, s.wup),
            ("own", w_up.at[:, own_cols], s.wup_own),
        )
    ):
        loads[name] = pltpu.make_async_copy(source, target, local.at[at])
        loads[name].start()

    barrier = pltpu.get_barrier_semaphore()
    others_z = [(lax.rem(dp + k, 4), me) for k in (1, 2, 3)]
    for device in [near(r) for r in range(1, 8)] + others_z:
        pl.semaphore_signal(barrier, inc=1, device_id=device, device_id_type=MESH)

    class Gather:
        def __init__(self, ref):
            self.ref = ref
            self.left, self.right = pl.ds(0, 384), pl.ds(384, 384)

        def start(self):
            ref, own = self.ref, self.ref.at[0]
            pair = []
            for first, second in ((self.left, self.right), (self.right, self.left)):
                copies = [
                    (own.at[:, first], ref.at[2, :, first], near(2)),
                    (own.at[:, second], ref.at[4, :, second], near(4)),
                ]
                pair.append(send_all(copies, own))
            self.early, self.late = pair
            self.other = send(own, ref.at[1], near(1))

        def forward(self):
            ref = self.ref
            self.early.wait_recv()
            copies = [
                (ref.at[2, :, self.left], ref.at[6, :, self.left], near(4)),
                (ref.at[4, :, self.right], ref.at[6, :, self.right], near(2)),
            ]
            self.far = send_all(copies, ref.at[6])

        def to_core(self):
            ref = self.ref
            self.late.wait_recv()
            self.more = [send(ref.at[r], ref.at[r + 1], near(1)) for r in (2, 4)]

        def diagonal(self):
            self.far.wait_recv()
            self.more.append(send(self.ref.at[6], self.ref.at[7], near(1)))

        def chip(self, number):
            (self.other if number == 0 else self.more[number - 1]).wait_recv()

        def rows(self, number):
            return self.ref[2 * number : 2 * number + 2].reshape(256, 768)

    values_one = x_ref[...].astype(WIDE)
    unit_one, scale_one = norm_parts(values_one)
    normed_one = (unit_one * gain_one + shift_one).astype(LOW)
    s.n1[0] = normed_one
    s.cot[0] = cot_ref[...]
    gather_one, gather_cot, gather_two = Gather(s.n1), Gather(s.cot), Gather(s.n2)
    pl.semaphore_wait(barrier, 10)
    gather_one.start()

    def share(source, lhs, give):
        for slot, r in enumerate(SLOTS):
            ours = place(r)
            lhs[slot, :, 0:128] = source(ours)
            give[slot] = source(ours + 1 - 2 * core)
        return send(give, lhs.at[:, :, pl.ds(128, 128)], near(1))

    def turn_block(source, target, r):
        target[:, :, 128 * r : 128 * r + 128] = source[r].T.reshape(8, 96, 128)

    def form_keys(number):
        at = 256 * number
        s.keys[at : at + 256, :] = dot(gather_one.rows(number), s.wqkv[:, 768:1536]).astype(LOW)

    def form_values(number):
        at = 256 * number
        rows = dot(gather_one.rows(number), s.wqkv[:, 1536:2304]) + bias_v
        s.values[at : at + 256, :] = rows.astype(LOW)

    def active_grad(first, last):
        for j in range(first, last):
            rows = s.wdown[4 * j : 4 * j + 4].reshape(384, 768)
            s.d_act[:, 384 * j : 384 * j + 384] = dot_rows(cot_ref[...], rows)

    loads["kv"].wait()
    gather_one.chip(0)
    form_keys(0)
    form_values(0)
    loads["q"].wait()
    q = (dot(normed_one, s.wqkv[:, 0:768]) + bias_q).astype(LOW)
    q = (q.astype(WIDE) * 0.125).astype(LOW)
    s.q_low[...] = q
    gather_one.forward()
    s.q_turned[...] = q.T
    loads["down"].wait()
    active_grad(0, 6)
    gather_one.to_core()
    active_grad(6, 8)

    row_at = lax.broadcasted_iota(jnp.int32, (128, 128), 0)
    lane_at = lax.broadcasted_iota(jnp.int32, (128, 128), 1)
    query_at = row_at + me * 128
    begin_one = lengths_ref[0, 0]
    begin_two = begin_one + lengths_ref[0, 1]
    begin_three = begin_two + lengths_ref[0, 2]
    begin = jnp.where(query_at >= begin_one, begin_one, 0)
    begin = jnp.where(query_at >= begin_two, begin_two, begin)
    begin = jnp.where(query_at >= begin_three, begin_three, begin)
    earlier = jnp.where(lane_at < row_at, 1.0, 0.0).astype(LOW)
    first_lanes = jnp.where(lane_at < 64, 1.0, 0.0)
    head_zero = (s.q_low[:, 0:128].astype(WIDE) * first_lanes).astype(LOW)

    def picks(r):
        scores = dot_rows(head_zero, s.keys[128 * r : 128 * r + 128, 0:128])
        key_at = lane_at + place(r) * 128
        allowed = (key_at <= query_at) & (key_at >= begin)
        chosen = (key_at < query_at) & (key_at > begin)
        small_exp = jnp.exp(-jnp.abs(scores))
        soft = jnp.maximum(scores, 0.0) + jnp.log1p(small_exp)
        picked = jnp.where(chosen, soft, 0.0) * (1.0 / 1024)
        high, rest = split_low(picked)
        s.sums[0, r : r + 1, :] = column_sum(picked)
        within = dot(earlier, high) + dot(earlier, rest)
        s.forgot[:, 128 * r : 128 * r + 128] = jnp.where(allowed, within, FAR)
        sigmoid = jnp.where(scores >= 0, 1.0, small_exp) / (1.0 + small_exp)
        s.sig_t[128 * r : 128 * r + 128, :] = (jnp.where(chosen, sigmoid, 0.0) * (1.0 / 1024)).T

    def turn(source, pair):
        at = 128 * pair
        for r in range(8):
            rows = slice(128 * r, 128 * r + 128)
            s.turned[pair, :, rows] = source[rows, at : at + 128].T

    picks(0)
    picks(1)
    gather_one.diagonal()
    gather_cot.start()
    for number in (1, 2, 3):
        gather_one.chip(number)
        form_keys(number)
        picks(2 * number)
        picks(2 * number + 1)
    sum_copy = send_all(
        [(s.sums.at[0], s.sums.at[r], near(r)) for r in range(1, 8)], s.sums.at[pl.ds(1, 7)]
    )
    for number in (1, 2, 3):
        form_values(number)
    for pair in range(6):
        turn(s.values, pair)
    gather_cot.forward()
    for r in range(8):
        turn_block(s.n1, s.n1_t, r)
    share_one = share(lambda at: s.n1_t[at, :, 0:128], s.lhs_q, s.give_q)
    sum_copy.wait_recv()

    def others(sums, later):
        rows = [jnp.zeros((1, 128), WIDE) for _ in range(8)]
        for d in range(1, 8):
            ahead = place(d) > me if later else place(d) < me
            weight = jnp.where(ahead, 1.0, 0.0)
            for r in range(8):
                rows[r] = rows[r] + weight * sums[d, (r ^ d) : (r ^ d) + 1, :]
        return rows

    for r, row in enumerate(others(s.sums, False)):
        at = 128 * r
        s.forgot_t[at : at + 128, :] = (s.forgot[:, at : at + 128] + row).T

    feature_at = lax.broadcasted_iota(jnp.int32, (128, 256), 0)
    column_at = lax.broadcasted_iota(jnp.int32, (128, 256), 1)
    own_head_t = jnp.where((feature_at < 64) == (column_at < 128), 1.0, 0.0).astype(LOW)
    long_row = lax.broadcasted_iota(jnp.int32, (256, 128), 0)
    long_lane = lax.broadcasted_iota(jnp.int32, (256, 128), 1)
    own_head = jnp.where((long_row < 128) == (long_lane < 64), 1.0, 0.0).astype(LOW)

    def both_t(values):
        return jnp.concatenate([values, values], axis=1) * own_head_t

    def both(values):
        return jnp.concatenate([values, values], axis=0) * own_head

    def attend(pair):
        at = 128 * pair
        scores = dot(s.keys[:, at : at + 128], both_t(s.q_turned[at : at + 128, :]))
        forgot = s.forgot_t[...]
        logits = scores - jnp.concatenate([forgot, forgot], axis=1)
        raised = jnp.exp(logits - jnp.max(logits, axis=0, keepdims=True))
        probs = (raised * (1.0 / jnp.sum(raised, axis=0, keepdims=True))).astype(LOW)
        s.probs[pair] = probs
        mixed = dot(s.turned[pair], probs)
        s.att_t[at : at + 64, :] = mixed[0:64, 0:128]
        s.att_t[at + 64 : at + 128, :] = mixed[64:128, 128:256]

    gather_cot.to_core()
    for pair in range(6):
        attend(pair)
    gather_cot.diagonal()

    attended_low_t = s.att_t[...].astype(LOW)
    s.att_low_t[...] = attended_low_t.reshape(8, 96, 128)
    loads["out"].wait()
    middle = values_one + dot(attended_low_t.T, s.wout[...]) + bias_out
    s.middle[...] = middle
    unit_two, scale_two = norm_parts(middle)
    s.unit_two[...] = unit_two
    normed_two = (unit_two * gain_two + shift_two).astype(LOW)
    s.n2[0] = normed_two
    gather_two.start()
    share_att = share(lambda at: s.att_low_t[at], s.lhs_out, s.give_out)
    loads["up"].wait()
    for j in range(4):
        at = 768 * j
        hidden = dot(normed_two, s.wup[:, at : at + 768]) + bias_up[:, at : at + 768]
        active, slope = gelu_parts(hidden)
        s.act[:, at : at + 768] = active.astype(LOW)
        d_hidden = (s.d_act[:, at : at + 768] * slope).astype(LOW)
        s.d_hidden[:, at : at + 768] = d_hidden
        s.wide[2 * j : 2 * j + 1, :] = column_sum(d_hidden[:, 0:384])
        s.wide[2 * j + 1 : 2 * j + 2, :] = column_sum(d_hidden[:, 384:768])

    d_output = cot_ref[...].astype(WIDE)
    parts = []
    for j in range(3):
        parts.append(dot_rows(s.d_hidden[...], s.wup[256 * j : 256 * j + 256, :]))
    d_normed = jnp.concatenate(parts, axis=1)
    gather_two.forward()
    unit_two = s.unit_two[...]
    s.small[5:6, :] = column_sum(d_normed * unit_two)
    s.small[6:7, :] = column_sum(d_normed)
    s.small[7:8, :] = column_sum(d_output)
    d_middle = d_output + norm_back(d_normed, unit_two, scale_two, gain_two)
    s.d_mid[...] = d_middle
    s.small[4:5, :] = column_sum(d_middle)
    d_branch = d_middle.astype(LOW)
    s.db2[0:128, :] = d_branch
    share_branch = send(s.db2.at[pl.ds(0, 128)], s.db2.at[pl.ds(128, 128)], near(1))
    d_att_t = dot(s.wout[...], d_branch.T).astype(LOW)
    s.d_att_t[...] = d_att_t
    s.d_att[...] = d_att_t.T
    gather_two.to_core()

    class Unit:
        def __init__(self, rows, grads, one, two, core=None):
            self.rows, self.grads, self.one, self.two, self.core = rows, grads, one, two, core

        def across(self):
            self.copy = send(self.grads.at[1], self.core, near(1))
            self.grads = self.grads.at[0]

        def start(self):
            if self.core is not None:
                self.copy.wait_recv()
                total = self.grads[...].astype(WIDE) + self.core[...].astype(WIDE)
                self.grads[...] = total.astype(LOW)
            copies = [
                (self.grads.at[pl.ds(1, 2), :, pl.ds(0, 384)], self.one.at[0], near(2)),
                (self.grads.at[pl.ds(2, 2), :, pl.ds(384, 384)], self.one.at[1], near(4)),
            ]
            self.copy = send_all(copies, self.one)

        def pass_on(self):
            self.copy.wait_recv()
            copies = []
            for half, slot, index, r in ((0, 3, 1, 4), (1, 1, 0, 2)):
                cols = slice(384 * half, 384 * half + 384)
                total = self.grads[slot, :, cols].astype(WIDE)
                total = total + self.one[half, index].astype(WIDE)
                self.grads[slot, :, cols] = total.astype(LOW)
                source = self.grads.at[slot, :, pl.ds(384 * half, 384)]
                copies.append((source, self.two.at[half], near(r)))
            self.copy = send_all(copies, self.two)

        def finish(self, half):
            if half == 0:
                self.copy.wait_recv()
            total = self.grads[0, :, 384 * half : 384 * half + 384].astype(WIDE)
            total = total + self.one[half, half].astype(WIDE)
            return total + self.two[half].astype(WIDE)

    class Line:
        def __init__(self, at, count, places):
            self.blocks, self.places = pl.ds(at, count), places
            self.at = next(line_numbers)
            send_at = RING + self.at
            first, second = next(landings), next(landings)
            mine, total = s.mine.at[self.blocks], s.total.at[self.blocks]
            self.inward = message(mine, s.got_z.at[self.blocks], z_pair, send_at, first)
            self.across = message(mine, s.got_mid.at[self.blocks], z_middle, send_at, second)
            self.outward = message(total, total, z_pair, send_at, first)

        def start(self):
            pl.when(outer)(lambda: self.inward.start())

        def middle(self):
            @pl.when(inner)
            def _():
                blocks = self.blocks
                self.inward.wait_recv()
                total = s.mine[blocks].astype(WIDE) + s.got_z[blocks].astype(WIDE)
                s.mine[blocks] = total.astype(LOW)
                self.across.start()

        def back(self):
            @pl.when(inner)
            def _():
                blocks = self.blocks
                self.across.wait_recv()
                total = s.mine[blocks].astype(WIDE) + s.got_mid[blocks].astype(WIDE)
                s.total[blocks] = total.astype(LOW)
                self.across.wait_send()
                self.outward.start()

        def write(self):
            pl.when(outer)(lambda: self.outward.wait_recv())
            landing = local.at[6 + self.at]
            for at, count, where in self.places:
                pltpu.make_async_copy(
                    s.total.at[pl.ds(at, count)], total_ref.at[pl.ds(where, count)], landing
                ).start()
            self.written = pltpu.make_async_copy(
                s.total.at[self.blocks], total_ref.at[self.blocks], landing
            )

        def close(self):
            self.written.wait()
            pl.when(outer)(lambda: self.inward.wait_send())
            pl.when(inner)(lambda: self.outward.wait_send())

    line_numbers = iter(range(LINES))

    def plain(at, count):
        return Line(at, count, ((at, count, at),))

    def spread(r):
        return Line(10 + r, 2, [(10 + i, 1, 10 + place(i)) for i in (r, r + 1)])

    line_down = [plain(2 * j, 2) for j in range(4)]
    line_out = plain(8, 2)
    line_up = [spread(2 * j) for j in range(4)]
    line_q, line_k, line_v = plain(18, 2), plain(20, 2), plain(22, 2)
    lines = line_down + [line_out] + line_up + [line_v, line_k, line_q]

    unit_out = Unit(96, s.grads_out, s.one.at[0], s.two.at[0])
    unit_q = Unit(96, s.grads_q, s.one.at[1], s.two.at[1])
    unit_k = Unit(96, s.grads_k, s.one.at[2], s.two.at[2], s.core_k)
    unit_v = Unit(96, s.grads_v, s.one.at[3], s.two.at[3], s.core_v)
    unit_n1 = Unit(128, s.d_n1, s.one_n1, s.two_n1, s.core_n1)

    def to_line(unit, at, line):
        for half in range(2):
            s.mine[at + half] = unit.finish(half).astype(LOW)
        line.start()

    def rows_of(source, odd):
        return jnp.concatenate([source[place(r + odd)] for r in SLOTS], axis=0)

    own_bias = jnp.zeros((1, 384), WIDE)
    for j in range(8):
        own_bias = own_bias + jnp.where(me == j, 1.0, 0.0) * bias_up[:, 384 * j : 384 * j + 384]
    loads["own"].wait()

    def own_units(number):
        gather_cot.chip(number)
        gather_two.chip(number)
        at = 256 * number
        hidden = dot(gather_two.rows(number), s.wup_own[...]) + own_bias
        active, slope = gelu_parts(hidden)
        d_active = dot_rows(gather_cot.rows(number), s.wdown[pl.ds(4 * me, 4)].reshape(384, 768))
        s.act_t[:, at : at + 256] = active.astype(LOW).T
        s.slope[at : at + 256, :] = (d_active * slope).astype(LOW)
        turn_block(s.n2, s.n2_t, 2 * number)
        turn_block(s.n2, s.n2_t, 2 * number + 1)

    def out_unit():
        share_att.wait_recv()
        share_branch.wait_recv()
        grads = dot(s.lhs_out[...].reshape(384, 256), s.db2[...]).astype(LOW)
        s.grads_out[...] = grads.reshape(4, 96, 768)
        unit_out.start()

    def down_grads():
        grads = dot(s.act_t[...], s.cot[...].reshape(1024, 768)).astype(LOW)
        for j in range(4):
            for i in range(2):
                s.mine[2 * j + i] = grads[96 * j : 96 * j + 96, 384 * i : 384 * i + 384]
        for line in line_down:
            line.start()

    def up_grads():
        copies = []
        for odd in range(2):
            grads = dot(rows_of(s.n2_t, odd), s.slope[...]).astype(LOW).reshape(4, 96, 384)
            for slot, r in enumerate(SLOTS):
                if r + odd == 0:
                    s.mine[10] = grads[0]
                else:
                    s.up_give[r + odd] = grads[slot]
                    copies.append((s.up_give.at[r + odd], s.mine.at[10 + r + odd], near(r + odd)))
        return copies

    def logit_grads(pair):
        at = 128 * pair
        grad_t = s.d_att_t[at : at + 128, :]
        products = grad_t.astype(WIDE) * s.att_t[at : at + 128, :]
        delta = jnp.concatenate(
            [
                jnp.sum(products[0:64], axis=0, keepdims=True),
                jnp.sum(products[64:128], axis=0, keepdims=True),
            ],
            axis=1,
        )
        d_probs = dot(s.values[:, at : at + 128], both_t(grad_t))
        d_logits = s.probs[pair].astype(WIDE) * (d_probs - delta)
        both_heads = d_logits[:, 0:128] + d_logits[:, 128:256]
        if pair == 5:
            s.d_forgot_t[...] = both_heads
        else:
            s.d_forgot_t[...] += both_heads
        return d_logits

    def value_grads(pair):
        at = 128 * pair
        grads = dot(s.probs[pair], both(s.d_att[:, at : at + 128]))
        s.dkv[:, 768 + at : 896 + at] = grads.astype(LOW)

    def score_grads(pair, d_scores):
        at = 128 * pair
        turn(s.keys, pair)
        s.dkv[:, at : at + 128] = dot(d_scores, both(s.q_low[:, at : at + 128])).astype(LOW)
        grads = dot(s.turned[pair], d_scores)
        s.dq_t[at : at + 64, :] = grads[0:64, 0:128]
        s.dq_t[at + 64 : at + 128, :] = grads[64:128, 128:256]

    def attend_back(pair):
        d_logits = logit_grads(pair)
        value_grads(pair)
        score_grads(pair, d_logits.astype(LOW))

    def back_sums():
        d_logits = logit_grads(0)
        s.forgot_t[...] = d_logits[:, 0:128]
        s.second_head[...] = d_logits[:, 128:256].astype(LOW)
        for r in range(8):
            turned = s.d_forgot_t[128 * r : 128 * r + 128, :].T
            s.back_sums[0, r : r + 1, :] = column_sum(turned)
        return send_all(
            [(s.back_sums.at[0], s.back_sums.at[r], near(r)) for r in range(1, 8)],
            s.back_sums.at[pl.ds(1, 7)],
        )

    def key_unit(unit, half):
        grads = s.dkv[:, 768 * half : 768 * half + 768]
        for odd in (1, 0):
            rows = rows_of(s.n1_t, odd)
            unit.grads[odd] = dot(rows, grads).astype(LOW).reshape(4, 96, 768)
        unit.across()

    def first_pair():
        later_rows = others(s.back_sums, True)
        following = jnp.where(row_at > lane_at, 1.0, 0.0).astype(LOW)
        selected = []
        for r in range(8):
            at = 128 * r
            high, rest = split_low(s.d_forgot_t[at : at + 128, :])
            later = jnp.broadcast_to(later_rows[r], (128, 128)).T
            d_picked = -(dot(high, following) + dot(rest, following) + later)
            selected.append(s.forgot_t[at : at + 128, :] + s.sig_t[at : at + 128, :] * d_picked)
        first_head = jnp.concatenate(selected, axis=0).astype(LOW)
        score_grads(0, jnp.concatenate([first_head, s.second_head[...]], axis=1))
        for j in range(6):
            at = 128 * j
            d_q = (s.dq_t[at : at + 128, :] * 0.125).astype(LOW)
            s.dq2[0:128, at : at + 128] = d_q.T
        return send(s.dq2.at[pl.ds(0, 128)], s.dq2.at[pl.ds(128, 128)], near(1))

    def query_unit():
        grads = dot(s.lhs_q[...].reshape(384, 256), s.dq2[...]).astype(LOW)
        s.grads_q[...] = grads.reshape(4, 96, 768)
        unit_q.start()

    def normed_part(j):
        cols = slice(256 * j, 256 * j + 256)
        grads = dot_rows(s.dkv[...], s.wqkv[cols, 768:2304]).astype(LOW)
        for slot, r in enumerate(SLOTS):
            for odd in range(2):
                at = 128 * (r + odd)
                s.d_n1[odd, slot, :, cols] = grads[at : at + 128]

    own_units(0)
    own_units(1)
    own_units(2)
    gather_two.diagonal()
    out_unit()
    own_units(3)
    down_grads()
    up_copies = up_grads()
    up_copy = send_all(up_copies, s.up_give.at[pl.ds(1, 7)])
    attend_back(5)
    unit_out.pass_on()
    attend_back(4)
    attend_back(3)
    attend_back(2)
    line_down[0].middle()
    attend_back(1)
    sum_copy = back_sums()
    value_grads(0)
    key_unit(unit_v, 1)
    line_down[1].middle()
    sum_copy.wait_recv()
    unit_v.start()
    line_down[0].back()
    share_q = first_pair()
    line_down[2].middle()
    to_line(unit_out, 8, line_out)
    up_copy.wait_recv()
    for line in line_up:
        line.start()
    key_unit(unit_k, 0)
    line_down[1].back()
    share_one.wait_recv()
    share_q.wait_recv()
    query_unit()
    unit_v.pass_on()
    unit_k.start()
    line_down[3].middle()
    normed_part(0)
    line_down[2].back()
    normed_part(1)
    line_out.middle()
    unit_q.pass_on()
    normed_part(2)
    unit_n1.across()
    line_down[3].back()
    to_line(unit_v, 22, line_v)
    line_up[0].middle()
    unit_k.pass_on()
    unit_n1.start()
    line_out.back()
    mixed = jnp.zeros((128, 768), WIDE)
    for j in range(4):
        rows = s.wdown[8 * j : 8 * j + 8].reshape(768, 768)
        mixed = mixed + dot(s.act[:, 768 * j : 768 * j + 768], rows)
    out_ref[...] = (s.middle[...] + mixed + bias_down).astype(LOW)
    line_up[1].middle()
    to_line(unit_q, 18, line_q)
    to_line(unit_k, 20, line_k)
    line_up[0].back()
    parts = []
    for i in range(3):
        rows = s.wqkv[256 * i : 256 * i + 256, 0:768]
        parts.append(dot_rows(s.dq2[0:128, :], rows))
    d_normed = jnp.concatenate(parts, axis=1)
    unit_n1.pass_on()
    line_up[2].middle()
    line_up[1].back()
    line_up[3].middle()
    d_normed = d_normed + jnp.concatenate([unit_n1.finish(0), unit_n1.finish(1)], axis=1)
    unit_one, scale_one = norm_parts(x_ref[...].astype(WIDE))
    s.small[0:1, :] = column_sum(d_normed * unit_one)
    s.small[1:2, :] = column_sum(d_normed)
    s.small[2:3, :] = column_sum(s.dq2[0:128, :])
    s.small[3:4, :] = column_sum(s.dkv[:, 768:1536])
    d_inputs = s.d_mid[...] + norm_back(d_normed, unit_one, scale_one, gain_one)
    grad_ref[...] = d_inputs.astype(LOW)

    s.pieces[...] = jnp.zeros((8, 16, 128), WIDE)
    for j in range(8):
        s.pieces[j, 0:8, 0:96] = s.small[:, 96 * j : 96 * j + 96]
        for i in range(3):
            s.pieces[j, 8 + i : 9 + i, :] = s.wide[j : j + 1, 128 * i : 128 * i + 128]
    piece_copy = send_all(
        [(s.pieces.at[place(r)], s.pieces_got.at[r], near(r)) for r in range(1, 8)],
        s.pieces_got.at[pl.ds(1, 7)],
    )
    line_up[2].back()
    line_v.middle()
    piece_copy.wait_recv()
    total = s.pieces[me]
    for r in range(1, 8):
        total = total + s.pieces_got[r]
    s.rows_z[dp] = total
    z_copy = send_all(
        [(s.rows_z.at[dp], s.rows_z.at[dp], device) for device in others_z],
        s.rows_z.at[pl.ds(0, 3)],
    )
    line_up[3].back()
    line_q.middle()
    for line in line_down:
        line.write()
    line_v.back()
    line_k.middle()
    line_out.write()
    line_q.back()
    for line in line_up:
        line.write()
    line_k.back()
    line_v.write()
    line_q.write()
    z_copy.wait_recv()
    small_ref[...] = s.rows_z[0] + s.rows_z[1] + s.rows_z[2] + s.rows_z[3]
    line_k.write()
    for line in lines:
        line.close()
    for copy in ring:
        if copy is not None:
            copy.wait_send()


def spread_kernel(total_ref, small_ref, out_in, grad_in, out_ref, grad_ref, *outs):
    gain_one, shift_one, qkv, bias_q, bias_v, out, bias_out = outs[:7]
    gain_two, shift_two, up, bias_up, down, bias_down = outs[7:]
    out_ref[...] = out_in[...]
    grad_ref[...] = grad_in[...]
    for i in range(2):
        cols = slice(384 * i, 384 * i + 384)
        for j in range(4):
            down[96 * j : 96 * j + 96, cols] = total_ref[2 * j + i].astype(WIDE)
        out[:, cols] = total_ref[8 + i].astype(WIDE)
    for j in range(8):
        up[:, 384 * j : 384 * j + 384] = total_ref[10 + j].astype(WIDE)
    for j in range(6):
        qkv[:, 384 * j : 384 * j + 384] = total_ref[18 + j].astype(WIDE)
    rows = (gain_one, shift_one, bias_q, bias_v, bias_out, gain_two, shift_two, bias_down)
    for j, target in enumerate(rows):
        target[...] = small_ref[j, 0:96]
    for i in range(3):
        bias_up[128 * i : 128 * i + 128] = small_ref[8 + i, :]


def fused_device(
    inputs,
    gain_one,
    shift_one,
    w_qkv,
    bias_q,
    bias_v,
    w_out,
    bias_out,
    gain_two,
    shift_two,
    w_up,
    bias_up,
    w_down,
    bias_down,
    lengths,
    cotangent,
):
    vmem = pl.BlockSpec(memory_space=pltpu.VMEM)
    anywhere = pl.BlockSpec(memory_space=pl.ANY)
    vectors = [gain_one, shift_one, bias_q, bias_v, bias_out, gain_two, shift_two]
    vectors = vectors + [bias_up, bias_down]
    tokens, width = inputs.shape
    layer_out, grad_inputs, total, small = pl.pallas_call(
        layer_kernel,
        out_shape=(
            jax.ShapeDtypeStruct((tokens, width), LOW),
            jax.ShapeDtypeStruct((tokens, width), LOW),
            jax.ShapeDtypeStruct((24, 96, 384), LOW),
            jax.ShapeDtypeStruct((16, 128), WIDE),
        ),
        in_specs=[pl.BlockSpec(memory_space=pltpu.SMEM)] + [vmem] * 11 + [anywhere] * 4,
        out_specs=(vmem, vmem, anywhere, vmem),
        scratch_shapes=[pltpu.VMEM(shape, kind) for shape, kind in SCRATCH.values()]
        + [
            pltpu.SemaphoreType.DMA((RING + LINES,)),
            pltpu.SemaphoreType.DMA((LANDINGS,)),
            pltpu.SemaphoreType.DMA((6 + LINES,)),
        ],
        compiler_params=pltpu.CompilerParams(
            collective_id=0, has_side_effects=True, vmem_limit_bytes=VMEM_BYTES
        ),
        name="layer",
    )(lengths, inputs, cotangent, *vectors, w_qkv, w_out, w_up, w_down.reshape(32, 96, width))
    return pl.pallas_call(
        spread_kernel,
        out_shape=tuple(
            jax.ShapeDtypeStruct((tokens, width), LOW) for _ in range(2)
        )
        + tuple(
            jax.ShapeDtypeStruct(shape, WIDE)
            for shape in (
                (96,),
                (96,),
                (96, 2304),
                (96,),
                (96,),
                (96, 768),
                (96,),
                (96,),
                (96,),
                (96, 3072),
                (384,),
                (384, 768),
                (96,),
            )
        ),
        in_specs=[vmem] * 4,
        out_specs=(vmem,) * 15,
        compiler_params=pltpu.CompilerParams(vmem_limit_bytes=VMEM_BYTES),
        name="spread",
    )(total, small, layer_out, grad_inputs)


def per_device(*arguments):
    inputs, w_up = arguments[0], arguments[10]
    fits = (
        lax.axis_size("dp") == 4
        and lax.axis_size("col") == 8
        and inputs.shape == (128, 768)
        and w_up.shape == (768, 3072)
    )
    return fused_device(*arguments) if fits else general_device(*arguments)


def solution(mesh):
    return jax.shard_map(
        per_device,
        mesh=mesh,
        in_specs=(
            P(("dp", "col"), None),
            P(),
            P(),
            P(),
            P(),
            P(),
            P(),
            P(),
            P(),
            P(),
            P(),
            P(),
            P(),
            P(),
            P("dp", None),
            P(("dp", "col"), None),
        ),
        out_specs=(
            P(("dp", "col"), None),
            P(("dp", "col"), None),
            P("col"),
            P("col"),
            P("col", None),
            P("col"),
            P("col"),
            P("col", None),
            P("col"),
            P("col"),
            P("col"),
            P("col", None),
            P("col"),
            P("col", None),
            P("col"),
        ),
        check_vma=False,
    )
```

```python
import functools
import types

import jax
import jax.numpy as jnp
from jax import lax
from jax.experimental import pallas as pl
from jax.experimental.pallas import tpu as pltpu
from jax.sharding import PartitionSpec as P

H = 12
HEAD = 64


epsilon = 1e-05


def layer_norm(values, scales, offset):
    average = jnp.mean(values, axis=-1, keepdims=True)
    centered = values - average
    spread = jnp.mean(centered * centered, axis=-1, keepdims=True)
    return centered * lax.rsqrt(spread + epsilon) * scales + offset


def documents(places, row_lengths):
    finish = jnp.cumsum(row_lengths)
    begins = finish - row_lengths
    inside = (places[:, None] >= begins[None, :]) & (places[:, None] < finish[None, :])
    numbers = jnp.arange(row_lengths.shape[0], dtype=jnp.int32)
    doc_index = jnp.sum(jnp.where(inside, numbers[None, :], 0), axis=1)
    first_place = jnp.sum(jnp.where(inside, begins[None, :], 0), axis=1)
    return (doc_index, first_place == places)


def general_device(
    inputs,
    gain_one,
    shift_one,
    w_qkv,
    bias_q,
    bias_v,
    w_out,
    bias_out,
    gain_two,
    shift_two,
    w_up,
    bias_up,
    w_down,
    bias_down,
    lengths,
    cotangent,
):
    col_count = lax.axis_size("col")
    col_place = lax.axis_index("col")
    tok_rows = inputs.shape[0]
    model_width = inputs.shape[1]
    row_len = tok_rows * col_count
    block_rows = min(512, row_len)
    block_count = row_len // block_rows
    places = jnp.arange(row_len, dtype=jnp.int32)
    doc_index, first_flag = documents(places, lengths[0])
    own_first = col_place * tok_rows
    key_places = own_first + jnp.arange(tok_rows, dtype=jnp.int32)
    key_doc = lax.dynamic_slice_in_dim(doc_index, own_first, tok_rows, 0)
    key_first = lax.dynamic_slice_in_dim(first_flag, own_first, tok_rows, 0)
    floated = inputs.astype(jnp.float32)
    norm_first, first_back = jax.vjp(layer_norm, floated, gain_one, shift_one)
    normed_one = norm_first.astype(jnp.bfloat16)
    joined = jnp.dot(normed_one, w_qkv, preferred_element_type=jnp.float32)
    queries = (joined[:, :model_width] + bias_q).astype(jnp.bfloat16)
    key_rows = joined[:, model_width : 2 * model_width].astype(jnp.bfloat16)
    value_rows = (joined[:, 2 * model_width :] + bias_v).astype(jnp.bfloat16)
    key_heads = key_rows.reshape(tok_rows, H, HEAD)
    value_heads = value_rows.reshape(tok_rows, H, HEAD)
    all_queries = lax.all_gather(queries, "col", axis=0, tiled=True)

    def block_terms(source, block_index, carried):
        first_row = block_index * block_rows
        q_block = lax.dynamic_slice_in_dim(source, first_row, block_rows, 0).reshape(
            block_rows, H, HEAD
        )
        q_places = first_row + jnp.arange(block_rows, dtype=jnp.int32)
        q_doc = lax.dynamic_slice_in_dim(doc_index, first_row, block_rows, 0)
        scores = (
            jnp.einsum("khd,qhd->hkq", key_heads, q_block, preferred_element_type=jnp.float32)
            * 0.125
        )
        allowed = (key_places[:, None] <= q_places[None, :]) & (key_doc[:, None] == q_doc[None, :])
        chosen = (
            allowed
            & (key_places[:, None] < q_places[None, :])
            & jnp.logical_not(key_first)[:, None]
        )
        picked = jnp.where(chosen, jax.nn.softplus(scores[0]), 0.0) / row_len
        forgot = carried[:, None] + jnp.cumsum(picked, axis=1) - picked
        logits = jnp.where(allowed[None], scores - forgot[None], -jnp.inf)
        return (q_block, scores, chosen, picked, logits)

    def forward_block(carried, block_index):
        q_block, scores, chosen, picked, logits = block_terms(all_queries, block_index, carried)
        row_top = jnp.max(logits, axis=1)
        safe_top = jnp.where(row_top > -jnp.inf, row_top, 0.0)
        raised = jnp.exp(logits - safe_top[:, None, :])
        totals = jnp.sum(raised, axis=1)
        numerator = jnp.einsum(
            "hkq,khd->qhd",
            raised.astype(jnp.bfloat16),
            value_heads,
            preferred_element_type=jnp.float32,
        )
        return (
            carried + jnp.sum(picked, axis=1),
            (carried, row_top.T, totals.T, numerator.reshape(block_rows, model_width)),
        )

    indices = jnp.arange(block_count, dtype=jnp.int32)
    unused, (block_starts, row_tops, row_totals, numerators) = lax.scan(
        forward_block, jnp.zeros((tok_rows,), jnp.float32), indices
    )
    row_tops = row_tops.reshape(row_len, H)
    row_totals = row_totals.reshape(row_len, H)
    numerators = numerators.reshape(row_len, model_width)
    got_top, got_total, got_numer = (
        lax.all_to_all(
            row_tops[None].astype(jnp.bfloat16), "col", split_axis=1, concat_axis=0, tiled=True
        ).astype(jnp.float32),
        lax.all_to_all(
            row_totals[None].astype(jnp.bfloat16), "col", split_axis=1, concat_axis=0, tiled=True
        ).astype(jnp.float32),
        lax.all_to_all(
            numerators[None].astype(jnp.bfloat16), "col", split_axis=1, concat_axis=0, tiled=True
        ).astype(jnp.float32),
    )
    row_best = jnp.max(got_top, axis=0)
    factor = jnp.exp(got_top - row_best[None])
    totals_own = jnp.sum(factor * got_total, axis=0)
    numer_own = jnp.sum(got_numer.reshape(col_count, tok_rows, H, HEAD) * factor[..., None], axis=0)
    attended = (numer_own / totals_own[..., None]).reshape(tok_rows, model_width)
    row_lse = row_best + jnp.log(totals_own)
    attended_low = attended.astype(jnp.bfloat16)
    middle = floated + jnp.dot(attended_low, w_out, preferred_element_type=jnp.float32) + bias_out
    norm_second, second_back = jax.vjp(layer_norm, middle, gain_two, shift_two)
    normed_two = norm_second.astype(jnp.bfloat16)
    hidden = jnp.dot(normed_two, w_up, preferred_element_type=jnp.float32) + bias_up
    active_full, gelu_back = jax.vjp(jax.nn.gelu, hidden)
    active = active_full.astype(jnp.bfloat16)
    layer_out = (
        middle + jnp.dot(active, w_down, preferred_element_type=jnp.float32) + bias_down
    ).astype(jnp.bfloat16)
    d_output = cotangent.astype(jnp.float32)
    grad_w_down = jnp.einsum("tf,td->fd", active, cotangent, preferred_element_type=jnp.float32)
    grad_bias_down = jnp.sum(d_output, axis=0)
    d_active = jnp.einsum("td,fd->tf", cotangent, w_down, preferred_element_type=jnp.float32)
    d_hidden = gelu_back(d_active)[0].astype(jnp.bfloat16)
    grad_w_up = jnp.einsum("td,tf->df", normed_two, d_hidden, preferred_element_type=jnp.float32)
    grad_bias_up = jnp.sum(d_hidden.astype(jnp.float32), axis=0)
    d_normed_two = jnp.einsum("tf,df->td", d_hidden, w_up, preferred_element_type=jnp.float32)
    d_middle_norm, grad_gain_two, grad_shift_two = second_back(d_normed_two)
    d_middle = d_output + d_middle_norm
    d_branch = d_middle.astype(jnp.bfloat16)
    grad_w_out = jnp.einsum("td,te->de", attended_low, d_branch, preferred_element_type=jnp.float32)
    grad_bias_out = jnp.sum(d_middle, axis=0)
    d_attended = jnp.einsum(
        "te,de->td", d_branch, w_out, preferred_element_type=jnp.float32
    ).astype(jnp.bfloat16)
    row_delta = jnp.sum(
        (d_attended.astype(jnp.float32) * attended).reshape(tok_rows, H, HEAD), axis=2
    )
    back_queries, gathered_grad = (
        lax.all_gather(queries, "col", axis=0, tiled=True),
        lax.all_gather(d_attended, "col", axis=0, tiled=True),
    )
    all_lse, all_delta = (
        lax.all_gather(row_lse, "col", axis=0, tiled=True),
        lax.all_gather(row_delta, "col", axis=0, tiled=True),
    )

    def backward_block(carried_state, inputs_block):
        later_sum, key_grad, value_grad = carried_state
        block_index, carried = inputs_block
        q_block, scores, chosen, picked, logits = block_terms(back_queries, block_index, carried)
        first_row = block_index * block_rows
        grad_block = lax.dynamic_slice_in_dim(gathered_grad, first_row, block_rows, 0).reshape(
            block_rows, H, HEAD
        )
        lse_block = lax.dynamic_slice_in_dim(all_lse, first_row, block_rows, 0)
        delta_block = lax.dynamic_slice_in_dim(all_delta, first_row, block_rows, 0)
        weights = jnp.exp(logits - lse_block.T[:, None, :])
        value_grad = value_grad + jnp.einsum(
            "hkq,qhd->khd",
            weights.astype(jnp.bfloat16),
            grad_block,
            preferred_element_type=jnp.float32,
        )
        d_weights = jnp.einsum(
            "khd,qhd->hkq", value_heads, grad_block, preferred_element_type=jnp.float32
        )
        d_logits = weights * (d_weights - delta_block.T[:, None, :])
        d_forgot = -jnp.sum(d_logits, axis=0)
        block_sum = jnp.sum(d_forgot, axis=1)
        d_picked = later_sum[:, None] + block_sum[:, None] - jnp.cumsum(d_forgot, axis=1)
        d_select = jnp.where(chosen, jax.nn.sigmoid(scores[0]) * d_picked / row_len, 0.0)
        d_scores = d_logits.at[0].add(d_select).astype(jnp.bfloat16)
        key_grad = (
            key_grad
            + jnp.einsum("hkq,qhd->khd", d_scores, q_block, preferred_element_type=jnp.float32)
            * 0.125
        )
        query_grad = (
            jnp.einsum("hkq,khd->qhd", d_scores, key_heads, preferred_element_type=jnp.float32)
            * 0.125
        )
        return (
            (later_sum + block_sum, key_grad, value_grad),
            query_grad.reshape(block_rows, model_width),
        )

    zero_heads = jnp.zeros((tok_rows, H, HEAD), jnp.float32)
    initial = (jnp.zeros((tok_rows,), jnp.float32), zero_heads, zero_heads)
    (unused_sum, key_grad, value_grad), query_parts = lax.scan(
        backward_block, initial, (indices, block_starts), reverse=True
    )
    query_parts = query_parts.reshape(row_len, model_width)
    d_queries = lax.psum_scatter(query_parts, "col", scatter_dimension=0, tiled=True).astype(
        jnp.bfloat16
    )
    d_keys = key_grad.reshape(tok_rows, model_width).astype(jnp.bfloat16)
    d_values = value_grad.reshape(tok_rows, model_width).astype(jnp.bfloat16)
    d_joined = jnp.concatenate([d_queries, d_keys, d_values], axis=1)
    grad_w_qkv = jnp.einsum("td,te->de", normed_one, d_joined, preferred_element_type=jnp.float32)
    grad_bias_q = jnp.sum(d_queries.astype(jnp.float32), axis=0)
    grad_bias_v = jnp.sum(d_values.astype(jnp.float32), axis=0)
    d_normed_one = jnp.einsum("te,de->td", d_joined, w_qkv, preferred_element_type=jnp.float32)
    d_input_norm, grad_gain_one, grad_shift_one = first_back(d_normed_one)
    grad_inputs = (d_middle + d_input_norm).astype(jnp.bfloat16)
    (
        shard_gain_one,
        shard_shift_one,
        shard_w_qkv,
        shard_bias_q,
        shard_bias_v,
        shard_w_out,
        shard_bias_out,
        shard_gain_two,
        shard_shift_two,
        shard_w_up,
        shard_bias_up,
        shard_w_down,
        shard_bias_down,
    ) = (
        lax.psum_scatter(grad_gain_one, "col", scatter_dimension=0, tiled=True),
        lax.psum_scatter(grad_shift_one, "col", scatter_dimension=0, tiled=True),
        lax.psum_scatter(grad_w_qkv, "col", scatter_dimension=0, tiled=True),
        lax.psum_scatter(grad_bias_q, "col", scatter_dimension=0, tiled=True),
        lax.psum_scatter(grad_bias_v, "col", scatter_dimension=0, tiled=True),
        lax.psum_scatter(grad_w_out, "col", scatter_dimension=0, tiled=True),
        lax.psum_scatter(grad_bias_out, "col", scatter_dimension=0, tiled=True),
        lax.psum_scatter(grad_gain_two, "col", scatter_dimension=0, tiled=True),
        lax.psum_scatter(grad_shift_two, "col", scatter_dimension=0, tiled=True),
        lax.psum_scatter(grad_w_up, "col", scatter_dimension=0, tiled=True),
        lax.psum_scatter(grad_bias_up, "col", scatter_dimension=0, tiled=True),
        lax.psum_scatter(grad_w_down, "col", scatter_dimension=0, tiled=True),
        lax.psum_scatter(grad_bias_down, "col", scatter_dimension=0, tiled=True),
    )
    summed = (
        lax.psum(shard_gain_one.astype(jnp.bfloat16), "dp").astype(jnp.float32),
        lax.psum(shard_shift_one.astype(jnp.bfloat16), "dp").astype(jnp.float32),
        lax.psum(shard_w_qkv.astype(jnp.bfloat16), "dp").astype(jnp.float32),
        lax.psum(shard_bias_q.astype(jnp.bfloat16), "dp").astype(jnp.float32),
        lax.psum(shard_bias_v.astype(jnp.bfloat16), "dp").astype(jnp.float32),
        lax.psum(shard_w_out.astype(jnp.bfloat16), "dp").astype(jnp.float32),
        lax.psum(shard_bias_out.astype(jnp.bfloat16), "dp").astype(jnp.float32),
        lax.psum(shard_gain_two.astype(jnp.bfloat16), "dp").astype(jnp.float32),
        lax.psum(shard_shift_two.astype(jnp.bfloat16), "dp").astype(jnp.float32),
        lax.psum(shard_w_up.astype(jnp.bfloat16), "dp").astype(jnp.float32),
        lax.psum(shard_bias_up.astype(jnp.bfloat16), "dp").astype(jnp.float32),
        lax.psum(shard_w_down.astype(jnp.bfloat16), "dp").astype(jnp.float32),
        lax.psum(shard_bias_down.astype(jnp.bfloat16), "dp").astype(jnp.float32),
    )
    return (
        layer_out,
        grad_inputs,
        summed[0],
        summed[1],
        summed[2],
        summed[3],
        summed[4],
        summed[5],
        summed[6],
        summed[7],
        summed[8],
        summed[9],
        summed[10],
        summed[11],
        summed[12],
    )


MESH = pl.DeviceIdType.MESH
LOW = jnp.bfloat16
WIDE = jnp.float32
FAR = 1e30
VMEM_BYTES = 63 * 2**20


def dot(a, b):
    return jnp.dot(a, b, preferred_element_type=WIDE)


def dot_rows(a, b):
    return lax.dot_general(a, b, (((1,), (1,)), ((), ())), preferred_element_type=WIDE)


def split_low(values):
    high = values.astype(LOW)
    return high, (values - high.astype(WIDE)).astype(LOW)


def column_sum(values):
    return jnp.sum(values.astype(WIDE), axis=0, keepdims=True)


def norm_parts(values):
    average = jnp.mean(values, axis=-1, keepdims=True)
    centered = values - average
    spread = jnp.mean(centered * centered, axis=-1, keepdims=True)
    scale = lax.rsqrt(spread + epsilon)
    return centered * scale, scale


def norm_back(grad, unit, scale, gain):
    scaled = grad * gain
    first = jnp.mean(scaled, axis=-1, keepdims=True)
    second = jnp.mean(scaled * unit, axis=-1, keepdims=True)
    return scale * (scaled - first - unit * second)


def gelu_parts(hidden):
    square = hidden * hidden
    bend = jnp.tanh(0.7978845608028654 * hidden * (1.0 + 0.044715 * square))
    half = 0.5 * (1.0 + bend)
    curve = 0.7978845608028654 * (1.0 + 3 * 0.044715 * square)
    return hidden * half, half + 0.5 * hidden * (1.0 - bend * bend) * curve


SCRATCH = dict(
    wqkv=((768, 2304), LOW),
    wout=((768, 768), LOW),
    wup=((768, 3072), LOW),
    wdown=((32, 96, 768), LOW),
    wup_own=((768, 384), LOW),
    n1=((8, 128, 768), LOW),
    n1_t=((8, 96, 1024), LOW),
    n2=((8, 128, 768), LOW),
    n2_t=((8, 96, 1024), LOW),
    cot=((8, 128, 768), LOW),
    keys=((1024, 768), LOW),
    values=((1024, 768), LOW),
    turned=((6, 128, 1024), LOW),
    probs=((6, 1024, 256), LOW),
    sums=((8, 8, 128), WIDE),
    back_sums=((8, 8, 128), WIDE),
    forgot=((128, 1024), WIDE),
    forgot_t=((1024, 128), WIDE),
    sig=((128, 1024), WIDE),
    d_forgot_t=((1024, 128), WIDE),
    second_head=((1024, 128), LOW),
    q_low=((128, 768), LOW),
    q_turned=((768, 128), LOW),
    att_t=((768, 128), WIDE),
    att_low_t=((8, 96, 128), LOW),
    act=((128, 3072), LOW),
    d_act=((128, 3072), WIDE),
    d_hidden=((128, 3072), LOW),
    middle=((128, 768), WIDE),
    d_mid=((128, 768), WIDE),
    unit_two=((128, 768), WIDE),
    d_att=((128, 768), LOW),
    d_att_t=((768, 128), LOW),
    dq_t=((768, 128), WIDE),
    act_t=((384, 1024), LOW),
    slope=((1024, 384), LOW),
    db2=((256, 768), LOW),
    dq2=((256, 768), LOW),
    lhs_out=((4, 96, 256), LOW),
    lhs_q=((4, 96, 256), LOW),
    give_out=((4, 96, 128), LOW),
    give_q=((4, 96, 128), LOW),
    dkv=((1024, 1536), LOW),
    grads_out=((4, 96, 768), LOW),
    grads_q=((4, 96, 768), LOW),
    grads_k=((2, 4, 96, 768), LOW),
    grads_v=((2, 4, 96, 768), LOW),
    core_k=((4, 96, 768), LOW),
    core_v=((4, 96, 768), LOW),
    one=((4, 2, 2, 96, 384), LOW),
    two=((4, 2, 96, 384), LOW),
    d_n1=((2, 4, 128, 768), LOW),
    core_n1=((4, 128, 768), LOW),
    one_n1=((2, 2, 128, 384), LOW),
    two_n1=((2, 128, 384), LOW),
    up_give=((8, 96, 384), LOW),
    mine=((24, 96, 384), LOW),
    got_z=((24, 96, 384), LOW),
    got_mid=((24, 96, 384), LOW),
    total=((24, 96, 384), LOW),
    small=((8, 768), WIDE),
    wide=((8, 384), WIDE),
    pieces=((8, 16, 128), WIDE),
    pieces_got=((8, 16, 128), WIDE),
    rows_z=((4, 16, 128), WIDE),
    out=((128, 768), LOW),
    grad=((128, 768), LOW),
)
SLOTS = (0, 2, 6, 4)
RING = 24
LINES = 14
LANDINGS = 76


def layer_kernel(
    lengths_ref,
    x_ref,
    cot_ref,
    gain_one,
    shift_one,
    bias_q,
    bias_v,
    bias_out,
    gain_two,
    shift_two,
    bias_up,
    bias_down,
    w_qkv,
    w_out,
    w_up,
    w_down,
    out_ref,
    grad_ref,
    total_ref,
    small_ref,
    *scratch,
):
    s = types.SimpleNamespace(**dict(zip(SCRATCH, scratch)))
    gain_one, shift_one, bias_q, bias_v, bias_out, gain_two, shift_two, bias_up, bias_down = (
        ref[...].reshape(1, -1)
        for ref in (
            gain_one,
            shift_one,
            bias_q,
            bias_v,
            bias_out,
            gain_two,
            shift_two,
            bias_up,
            bias_down,
        )
    )
    sent, landed, local = scratch[len(SCRATCH) :]
    me = lax.axis_index("col")
    dp = lax.axis_index("dp")
    core = lax.rem(me, 2)
    x_bit = lax.rem(lax.div(me, 2), 2)
    y_bit = lax.div(me, 4)

    def place(r):
        step = (r & 1) * (1 - 2 * core) + ((r >> 1) & 1) * (2 - 4 * x_bit)
        return me + step + (r >> 2) * (4 - 8 * y_bit)

    def near(r):
        return (dp, place(r))

    z_pair = (dp + 1 - 2 * lax.rem(dp, 2), me)
    z_middle = (3 - dp, me)
    inner = (dp == 1) | (dp == 2)
    outer = jnp.logical_not(inner)
    barrier = pltpu.get_barrier_semaphore()
    others_z = [(lax.rem(dp + k, 4), me) for k in (1, 2, 3)]
    for device in [near(r) for r in range(1, 8)] + others_z:
        pl.semaphore_signal(barrier, inc=1, device_id=device, device_id_type=MESH)

    landings = iter(range(LANDINGS))
    ring = [None] * RING
    turns = iter(range(10**6))

    def message(source, target, device, send_at, land_at):
        return pltpu.make_async_remote_copy(
            src_ref=source,
            dst_ref=target,
            send_sem=sent.at[send_at],
            recv_sem=landed.at[land_at],
            device_id=device,
            device_id_type=MESH,
        )

    def send_all(copies, whole):
        send_at, land_at = next(turns) % RING, next(landings)
        if ring[send_at] is not None:
            ring[send_at].wait_send()
        for source, target, device in copies:
            message(source, target, device, send_at, land_at).start()
        ring[send_at] = message(whole, whole, near(1), send_at, land_at)
        return ring[send_at]

    def send(source, target, device):
        return send_all([(source, target, device)], source)

    loads = {}
    own_cols = pl.ds(pl.multiple_of(384 * me, 128), 384)
    for at, (name, source, target) in enumerate(
        (
            ("kv", w_qkv.at[:, pl.ds(768, 1536)], s.wqkv.at[:, pl.ds(768, 1536)]),
            ("q", w_qkv.at[:, pl.ds(0, 768)], s.wqkv.at[:, pl.ds(0, 768)]),
            ("down", w_down, s.wdown),
            ("out", w_out, s.wout),
            ("up", w_up, s.wup),
            ("own", w_up.at[:, own_cols], s.wup_own),
        )
    ):
        loads[name] = pltpu.make_async_copy(source, target, local.at[at])
        loads[name].start()

    class Gather:
        def __init__(self, ref):
            self.ref = ref
            self.left, self.right = pl.ds(0, 384), pl.ds(384, 384)

        def start(self):
            ref, own = self.ref, self.ref.at[0]
            pair = []
            for first, second in ((self.left, self.right), (self.right, self.left)):
                copies = [
                    (own.at[:, first], ref.at[2, :, first], near(2)),
                    (own.at[:, second], ref.at[4, :, second], near(4)),
                ]
                pair.append(send_all(copies, own))
            self.early, self.late = pair
            self.other = send(own, ref.at[1], near(1))

        def forward(self):
            ref = self.ref
            self.early.wait_recv()
            copies = [
                (ref.at[2, :, self.left], ref.at[6, :, self.left], near(4)),
                (ref.at[4, :, self.right], ref.at[6, :, self.right], near(2)),
            ]
            self.far = send_all(copies, ref.at[6])

        def to_core(self):
            ref = self.ref
            self.late.wait_recv()
            self.more = [send(ref.at[r], ref.at[r + 1], near(1)) for r in (2, 4)]

        def diagonal(self):
            self.far.wait_recv()
            self.more.append(send(self.ref.at[6], self.ref.at[7], near(1)))

        def chip(self, number):
            (self.other if number == 0 else self.more[number - 1]).wait_recv()

        def rows(self, number):
            return self.ref[2 * number : 2 * number + 2].reshape(256, 768)

    values_one = x_ref[...].astype(WIDE)
    unit_one, scale_one = norm_parts(values_one)
    normed_one = (unit_one * gain_one + shift_one).astype(LOW)
    s.n1[0] = normed_one
    s.cot[0] = cot_ref[...]
    gather_one, gather_cot, gather_two = Gather(s.n1), Gather(s.cot), Gather(s.n2)
    pl.semaphore_wait(barrier, 10)
    gather_one.start()

    def share(source, lhs, give):
        for slot, r in enumerate(SLOTS):
            ours = place(r)
            lhs[slot, :, 0:128] = source(ours)
            give[slot] = source(ours + 1 - 2 * core)
        return send(give, lhs.at[:, :, pl.ds(128, 128)], near(1))

    def turn_block(source, target, r):
        target[:, :, 128 * r : 128 * r + 128] = source[r].T.reshape(8, 96, 128)

    def form_keys(number):
        at = 256 * number
        s.keys[at : at + 256, :] = dot(gather_one.rows(number), s.wqkv[:, 768:1536]).astype(LOW)

    def form_values(number):
        at = 256 * number
        rows = dot(gather_one.rows(number), s.wqkv[:, 1536:2304]) + bias_v
        s.values[at : at + 256, :] = rows.astype(LOW)

    def active_grad(first, last):
        for j in range(first, last):
            rows = s.wdown[4 * j : 4 * j + 4].reshape(384, 768)
            s.d_act[:, 384 * j : 384 * j + 384] = dot_rows(cot_ref[...], rows)

    loads["kv"].wait()
    gather_one.chip(0)
    form_keys(0)
    form_values(0)
    loads["q"].wait()
    q = (dot(normed_one, s.wqkv[:, 0:768]) + bias_q).astype(LOW)
    q = (q.astype(WIDE) * 0.125).astype(LOW)
    s.q_low[...] = q
    row_at = lax.broadcasted_iota(jnp.int32, (128, 128), 0)
    lane_at = lax.broadcasted_iota(jnp.int32, (128, 128), 1)
    query_at = row_at + me * 128
    begin_one = lengths_ref[0, 0]
    begin_two = begin_one + lengths_ref[0, 1]
    begin_three = begin_two + lengths_ref[0, 2]
    begin = jnp.where(query_at >= begin_one, begin_one, 0)
    begin = jnp.where(query_at >= begin_two, begin_two, begin)
    begin = jnp.where(query_at >= begin_three, begin_three, begin)
    earlier = jnp.where(lane_at < row_at, 1.0, 0.0).astype(LOW)
    first_lanes = jnp.where(lane_at < 64, 1.0, 0.0)
    head_zero = (s.q_low[:, 0:128].astype(WIDE) * first_lanes).astype(LOW)

    def picks(number):
        at = 256 * number
        scores = dot_rows(head_zero, s.keys[at : at + 256, 0:128])
        key_at = jnp.concatenate(
            [lane_at + place(r) * 128 for r in (2 * number, 2 * number + 1)], axis=1
        )
        queries_at = jnp.concatenate([query_at, query_at], axis=1)
        begins = jnp.concatenate([begin, begin], axis=1)
        allowed = (key_at <= queries_at) & (key_at >= begins)
        chosen = (key_at < queries_at) & (key_at > begins)
        small_exp = jnp.exp(-jnp.abs(scores))
        soft = jnp.maximum(scores, 0.0) + jnp.log1p(small_exp)
        picked = jnp.where(chosen, soft, 0.0) * (1.0 / 1024)
        high, rest = split_low(picked)
        sums = column_sum(picked)
        s.sums[0, 2 * number : 2 * number + 1, :] = sums[:, 0:128]
        s.sums[0, 2 * number + 1 : 2 * number + 2, :] = sums[:, 128:256]
        within = dot(earlier, high) + dot(earlier, rest)
        s.forgot[:, at : at + 256] = jnp.where(allowed, within, FAR)
        sigmoid = jnp.where(scores >= 0, 1.0, small_exp) / (1.0 + small_exp)
        s.sig[:, at : at + 256] = jnp.where(chosen, sigmoid, 0.0) * (1.0 / 1024)

    def turn(source, pair):
        at = 128 * pair
        for r in range(8):
            rows = slice(128 * r, 128 * r + 128)
            s.turned[pair, :, rows] = source[rows, at : at + 128].T

    picks(0)
    turn_block(s.n1, s.n1_t, 0)
    gather_one.forward()
    s.q_turned[...] = q.T
    loads["down"].wait()
    active_grad(0, 6)
    gather_one.to_core()
    active_grad(6, 8)

    gather_one.diagonal()
    for number in (1, 2, 3):
        gather_one.chip(number)
        form_keys(number)
        picks(number)
    sum_copy = send_all(
        [(s.sums.at[0], s.sums.at[r], near(r)) for r in range(1, 8)], s.sums.at[pl.ds(1, 7)]
    )
    gather_cot.start()
    for number in (1, 2, 3):
        form_values(number)
    for pair in range(6):
        turn(s.values, pair)
    share_one = share(lambda at: s.n1_t[at, :, 0:128], s.lhs_q, s.give_q)
    sum_copy.wait_recv()

    def others(sums, later):
        rows = [jnp.zeros((1, 128), WIDE) for _ in range(8)]
        for d in range(1, 8):
            ahead = place(d) > me if later else place(d) < me
            weight = jnp.where(ahead, 1.0, 0.0)
            for r in range(8):
                rows[r] = rows[r] + weight * sums[d, (r ^ d) : (r ^ d) + 1, :]
        return rows

    for r, row in enumerate(others(s.sums, False)):
        at = 128 * r
        s.forgot_t[at : at + 128, :] = (s.forgot[:, at : at + 128] + row).T

    feature_at = lax.broadcasted_iota(jnp.int32, (128, 256), 0)
    column_at = lax.broadcasted_iota(jnp.int32, (128, 256), 1)
    own_head_t = jnp.where((feature_at < 64) == (column_at < 128), 1.0, 0.0).astype(LOW)
    long_row = lax.broadcasted_iota(jnp.int32, (256, 128), 0)
    long_lane = lax.broadcasted_iota(jnp.int32, (256, 128), 1)
    own_head = jnp.where((long_row < 128) == (long_lane < 64), 1.0, 0.0).astype(LOW)

    def both_t(values):
        return jnp.concatenate([values, values], axis=1) * own_head_t

    def both(values):
        return jnp.concatenate([values, values], axis=0) * own_head

    def attend(pair):
        at = 128 * pair
        scores = dot(s.keys[:, at : at + 128], both_t(s.q_turned[at : at + 128, :]))
        forgot = s.forgot_t[...]
        logits = scores - jnp.concatenate([forgot, forgot], axis=1)
        raised = jnp.exp(logits - jnp.max(logits, axis=0, keepdims=True))
        probs = (raised * (1.0 / jnp.sum(raised, axis=0, keepdims=True))).astype(LOW)
        s.probs[pair] = probs
        mixed = dot(s.turned[pair], probs)
        s.att_t[at : at + 64, :] = mixed[0:64, 0:128]
        s.att_t[at + 64 : at + 128, :] = mixed[64:128, 128:256]

    for pair in range(6):
        if pair == 2:
            gather_cot.forward()
        if pair == 4:
            gather_cot.to_core()
        attend(pair)

    attended_low_t = s.att_t[...].astype(LOW)
    s.att_low_t[...] = attended_low_t.reshape(8, 96, 128)
    loads["out"].wait()
    middle = values_one + dot(attended_low_t.T, s.wout[...]) + bias_out
    s.middle[...] = middle
    unit_two, scale_two = norm_parts(middle)
    s.unit_two[...] = unit_two
    normed_two = (unit_two * gain_two + shift_two).astype(LOW)
    s.n2[0] = normed_two
    gather_two.start()
    share_att = share(lambda at: s.att_low_t[at], s.lhs_out, s.give_out)
    gather_cot.diagonal()
    loads["up"].wait()
    for j in range(4):
        at = 768 * j
        hidden = dot(normed_two, s.wup[:, at : at + 768]) + bias_up[:, at : at + 768]
        active, slope = gelu_parts(hidden)
        s.act[:, at : at + 768] = active.astype(LOW)
        d_hidden = (s.d_act[:, at : at + 768] * slope).astype(LOW)
        s.d_hidden[:, at : at + 768] = d_hidden
        s.wide[2 * j : 2 * j + 1, :] = column_sum(d_hidden[:, 0:384])
        s.wide[2 * j + 1 : 2 * j + 2, :] = column_sum(d_hidden[:, 384:768])

    d_output = cot_ref[...].astype(WIDE)
    parts = []
    for j in range(3):
        parts.append(dot_rows(s.d_hidden[...], s.wup[256 * j : 256 * j + 256, :]))
    d_normed = jnp.concatenate(parts, axis=1)
    gather_two.forward()
    unit_two = s.unit_two[...]
    s.small[5:6, :] = column_sum(d_normed * unit_two)
    s.small[6:7, :] = column_sum(d_normed)
    s.small[7:8, :] = column_sum(d_output)
    d_middle = d_output + norm_back(d_normed, unit_two, scale_two, gain_two)
    s.d_mid[...] = d_middle
    s.small[4:5, :] = column_sum(d_middle)
    d_branch = d_middle.astype(LOW)
    s.db2[0:128, :] = d_branch
    share_branch = send(s.db2.at[pl.ds(0, 128)], s.db2.at[pl.ds(128, 128)], near(1))
    d_att_t = dot(s.wout[...], d_branch.T).astype(LOW)
    s.d_att_t[...] = d_att_t
    s.d_att[...] = d_att_t.T
    gather_two.to_core()

    class Unit:
        def __init__(self, rows, grads, one, two, core=None):
            self.rows, self.grads, self.one, self.two, self.core = rows, grads, one, two, core

        def across(self):
            self.copy = send(self.grads.at[1], self.core, near(1))
            self.grads = self.grads.at[0]

        def start(self):
            if self.core is not None:
                self.copy.wait_recv()
                total = self.grads[...].astype(WIDE) + self.core[...].astype(WIDE)
                self.grads[...] = total.astype(LOW)
            copies = [
                (self.grads.at[pl.ds(1, 2), :, pl.ds(0, 384)], self.one.at[0], near(2)),
                (self.grads.at[pl.ds(2, 2), :, pl.ds(384, 384)], self.one.at[1], near(4)),
            ]
            self.copy = send_all(copies, self.one)

        def pass_on(self):
            self.copy.wait_recv()
            copies = []
            for half, slot, index, r in ((0, 3, 1, 4), (1, 1, 0, 2)):
                cols = slice(384 * half, 384 * half + 384)
                total = self.grads[slot, :, cols].astype(WIDE)
                total = total + self.one[half, index].astype(WIDE)
                self.grads[slot, :, cols] = total.astype(LOW)
                source = self.grads.at[slot, :, pl.ds(384 * half, 384)]
                copies.append((source, self.two.at[half], near(r)))
            self.copy = send_all(copies, self.two)

        def finish(self, half):
            if half == 0:
                self.copy.wait_recv()
            total = self.grads[0, :, 384 * half : 384 * half + 384].astype(WIDE)
            total = total + self.one[half, half].astype(WIDE)
            return total + self.two[half].astype(WIDE)

    class Line:
        def __init__(self, at, count, places):
            self.blocks, self.places = pl.ds(at, count), places
            self.at = next(line_numbers)
            send_at = RING + self.at
            first, second = next(landings), next(landings)
            mine, total = s.mine.at[self.blocks], s.total.at[self.blocks]
            self.inward = message(mine, s.got_z.at[self.blocks], z_pair, send_at, first)
            self.across = message(mine, s.got_mid.at[self.blocks], z_middle, send_at, second)
            self.outward = message(total, total, z_pair, send_at, first)

        def start(self):
            pl.when(outer)(lambda: self.inward.start())

        def middle(self):
            @pl.when(inner)
            def _():
                blocks = self.blocks
                self.inward.wait_recv()
                total = s.mine[blocks].astype(WIDE) + s.got_z[blocks].astype(WIDE)
                s.mine[blocks] = total.astype(LOW)
                self.across.start()

        def back(self):
            @pl.when(inner)
            def _():
                blocks = self.blocks
                self.across.wait_recv()
                total = s.mine[blocks].astype(WIDE) + s.got_mid[blocks].astype(WIDE)
                s.total[blocks] = total.astype(LOW)
                self.across.wait_send()
                self.outward.start()

        def write(self):
            pl.when(outer)(lambda: self.outward.wait_recv())
            landing = local.at[6 + self.at]
            for at, count, where in self.places:
                pltpu.make_async_copy(
                    s.total.at[pl.ds(at, count)], total_ref.at[pl.ds(where, count)], landing
                ).start()
            self.written = pltpu.make_async_copy(
                s.total.at[self.blocks], total_ref.at[self.blocks], landing
            )

        def close(self):
            self.written.wait()
            pl.when(outer)(lambda: self.inward.wait_send())
            pl.when(inner)(lambda: self.outward.wait_send())

    line_numbers = iter(range(LINES))

    def plain(at, count):
        return Line(at, count, ((at, count, at),))

    def spread(r):
        return Line(10 + r, 2, [(10 + i, 1, 10 + place(i)) for i in (r, r + 1)])

    line_down = [plain(at, count) for at, count in ((0, 1), (1, 1), (2, 2), (4, 2), (6, 2))]
    line_out = plain(8, 2)
    line_up = [spread(2 * j) for j in range(4)]
    line_v, line_q, line_k = plain(22, 2), plain(18, 2), [plain(20, 1), plain(21, 1)]
    lines = line_down + [line_out] + line_up + [line_v, line_q] + line_k

    unit_out = Unit(96, s.grads_out, s.one.at[0], s.two.at[0])
    unit_q = Unit(96, s.grads_q, s.one.at[1], s.two.at[1])
    unit_k = Unit(96, s.grads_k, s.one.at[2], s.two.at[2], s.core_k)
    unit_v = Unit(96, s.grads_v, s.one.at[3], s.two.at[3], s.core_v)
    unit_n1 = Unit(128, s.d_n1, s.one_n1, s.two_n1, s.core_n1)

    def to_line(unit, at, *parts):
        for half in range(2):
            s.mine[at + half] = unit.finish(half).astype(LOW)
        for line in parts:
            line.start()

    def rows_of(source, odd):
        return jnp.concatenate([source[place(r + odd)] for r in SLOTS], axis=0)

    own_bias = jnp.zeros((1, 384), WIDE)
    for j in range(8):
        own_bias = own_bias + jnp.where(me == j, 1.0, 0.0) * bias_up[:, 384 * j : 384 * j + 384]
    loads["own"].wait()

    def own_units(number):
        gather_cot.chip(number)
        gather_two.chip(number)
        at = 256 * number
        hidden = dot(gather_two.rows(number), s.wup_own[...]) + own_bias
        active, slope = gelu_parts(hidden)
        d_active = dot_rows(gather_cot.rows(number), s.wdown[pl.ds(4 * me, 4)].reshape(384, 768))
        s.act_t[:, at : at + 256] = active.astype(LOW).T
        s.slope[at : at + 256, :] = (d_active * slope).astype(LOW)

    def out_unit():
        share_att.wait_recv()
        share_branch.wait_recv()
        grads = dot(s.lhs_out[...].reshape(384, 256), s.db2[...]).astype(LOW)
        s.grads_out[...] = grads.reshape(4, 96, 768)
        unit_out.start()

    def down_grads():
        grads = dot(s.act_t[...], s.cot[...].reshape(1024, 768)).astype(LOW)
        for j in range(4):
            for i in range(2):
                s.mine[2 * j + i] = grads[96 * j : 96 * j + 96, 384 * i : 384 * i + 384]
        for line in line_down:
            line.start()

    def up_grads(odd):
        copies = []
        grads = dot(rows_of(s.n2_t, odd), s.slope[...]).astype(LOW).reshape(4, 96, 384)
        for slot, r in enumerate(SLOTS):
            if r + odd == 0:
                s.mine[10] = grads[0]
            else:
                s.up_give[r + odd] = grads[slot]
                copies.append((s.up_give.at[r + odd], s.mine.at[10 + r + odd], near(r + odd)))
        return copies, s.up_give.at[pl.ds(0, len(copies))]

    def logit_grads(pair):
        at = 128 * pair
        grad_t = s.d_att_t[at : at + 128, :]
        products = grad_t.astype(WIDE) * s.att_t[at : at + 128, :]
        delta = jnp.concatenate(
            [
                jnp.sum(products[0:64], axis=0, keepdims=True),
                jnp.sum(products[64:128], axis=0, keepdims=True),
            ],
            axis=1,
        )
        d_probs = dot(s.values[:, at : at + 128], both_t(grad_t))
        d_logits = s.probs[pair].astype(WIDE) * (d_probs - delta)
        both_heads = d_logits[:, 0:128] + d_logits[:, 128:256]
        if pair == 5:
            s.d_forgot_t[...] = both_heads
        else:
            s.d_forgot_t[...] += both_heads
        return d_logits

    def value_grads(pair):
        at = 128 * pair
        grads = dot(s.probs[pair], both(s.d_att[:, at : at + 128]))
        s.dkv[:, 768 + at : 896 + at] = grads.astype(LOW)

    def score_grads(pair, d_scores):
        at = 128 * pair
        turn(s.keys, pair)
        s.dkv[:, at : at + 128] = dot(d_scores, both(s.q_low[:, at : at + 128])).astype(LOW)
        grads = dot(s.turned[pair], d_scores)
        s.dq_t[at : at + 64, :] = grads[0:64, 0:128]
        s.dq_t[at + 64 : at + 128, :] = grads[64:128, 128:256]

    def attend_back(pair):
        d_logits = logit_grads(pair)
        value_grads(pair)
        score_grads(pair, d_logits.astype(LOW))

    def back_sums():
        d_logits = logit_grads(0)
        s.forgot_t[...] = d_logits[:, 0:128]
        s.second_head[...] = d_logits[:, 128:256].astype(LOW)
        for r in range(8):
            turned = s.d_forgot_t[128 * r : 128 * r + 128, :].T
            s.back_sums[0, r : r + 1, :] = column_sum(turned)
        return send_all(
            [(s.back_sums.at[0], s.back_sums.at[r], near(r)) for r in range(1, 8)],
            s.back_sums.at[pl.ds(1, 7)],
        )

    def key_unit(unit, half, odd):
        grads = s.dkv[:, 768 * half : 768 * half + 768]
        rows = rows_of(s.n1_t, odd)
        unit.grads[odd] = dot(rows, grads).astype(LOW).reshape(4, 96, 768)

    def first_pair():
        later_rows = others(s.back_sums, True)
        following = jnp.where(row_at > lane_at, 1.0, 0.0).astype(LOW)
        selected = []
        for r in range(8):
            at = 128 * r
            high, rest = split_low(s.d_forgot_t[at : at + 128, :])
            later = jnp.broadcast_to(later_rows[r], (128, 128)).T
            d_picked = -(dot(high, following) + dot(rest, following) + later)
            selected.append(s.forgot_t[at : at + 128, :] + s.sig[:, at : at + 128].T * d_picked)
        first_head = jnp.concatenate(selected, axis=0).astype(LOW)
        score_grads(0, jnp.concatenate([first_head, s.second_head[...]], axis=1))
        for j in range(6):
            at = 128 * j
            d_q = (s.dq_t[at : at + 128, :] * 0.125).astype(LOW)
            s.dq2[0:128, at : at + 128] = d_q.T
        return send(s.dq2.at[pl.ds(0, 128)], s.dq2.at[pl.ds(128, 128)], near(1))

    def query_unit():
        grads = dot(s.lhs_q[...].reshape(384, 256), s.dq2[...]).astype(LOW)
        s.grads_q[...] = grads.reshape(4, 96, 768)
        unit_q.start()

    def normed_part(j):
        cols = slice(256 * j, 256 * j + 256)
        grads = dot_rows(s.dkv[...], s.wqkv[cols, 768:2304]).astype(LOW)
        for slot, r in enumerate(SLOTS):
            for odd in range(2):
                at = 128 * (r + odd)
                s.d_n1[odd, slot, :, cols] = grads[at : at + 128]

    own_units(0)
    own_units(1)
    own_units(2)
    gather_two.diagonal()
    out_unit()
    own_units(3)
    down_grads()
    for r in range(8):
        turn_block(s.n2, s.n2_t, r)
        if r:
            turn_block(s.n1, s.n1_t, r)
    up_odd = send_all(*up_grads(1))
    up_even = up_grads(0)
    attend_back(5)
    attend_back(4)
    unit_out.pass_on()
    attend_back(3)
    line_down[0].middle()
    attend_back(2)
    line_down[1].middle()
    line_down[0].back()
    attend_back(1)
    sum_copy = back_sums()
    up_even = send_all(*up_even)
    value_grads(0)
    key_unit(unit_v, 1, 1)
    line_down[2].middle()
    key_unit(unit_v, 1, 0)
    unit_v.across()
    line_down[1].back()
    to_line(unit_out, 8, line_out)
    sum_copy.wait_recv()
    share_q = first_pair()
    unit_v.start()
    line_down[3].middle()
    line_down[2].back()
    key_unit(unit_k, 0, 1)
    key_unit(unit_k, 0, 0)
    unit_k.across()
    share_one.wait_recv()
    share_q.wait_recv()
    query_unit()
    up_odd.wait_recv()
    up_even.wait_recv()
    for line in line_up:
        line.start()
    line_down[4].middle()
    line_down[3].back()
    normed_part(0)
    unit_v.pass_on()
    unit_k.start()
    line_out.middle()
    line_down[4].back()
    normed_part(1)
    normed_part(2)
    unit_n1.across()
    unit_q.pass_on()
    line_up[0].middle()
    line_out.back()
    to_line(unit_v, 22, line_v)
    mixed = jnp.zeros((128, 768), WIDE)
    for j in range(4):
        rows = s.wdown[8 * j : 8 * j + 8].reshape(768, 768)
        mixed = mixed + dot(s.act[:, 768 * j : 768 * j + 768], rows)
    s.out[...] = (s.middle[...] + mixed + bias_down).astype(LOW)
    out_copy = pltpu.make_async_copy(s.out, out_ref, local.at[6 + LINES])
    out_copy.start()
    unit_k.pass_on()
    unit_n1.start()
    line_up[1].middle()
    line_up[0].back()
    to_line(unit_q, 18, line_q)
    line_up[2].middle()
    to_line(unit_k, 20, *line_k)
    line_up[1].back()
    parts = []
    for i in range(3):
        rows = s.wqkv[256 * i : 256 * i + 256, 0:768]
        parts.append(dot_rows(s.dq2[0:128, :], rows))
    d_normed = jnp.concatenate(parts, axis=1)
    line_up[3].middle()
    line_up[2].back()
    unit_n1.pass_on()
    line_v.middle()
    line_up[3].back()
    d_normed = d_normed + jnp.concatenate([unit_n1.finish(0), unit_n1.finish(1)], axis=1)
    unit_one, scale_one = norm_parts(x_ref[...].astype(WIDE))
    s.small[0:1, :] = column_sum(d_normed * unit_one)
    s.small[1:2, :] = column_sum(d_normed)
    s.small[2:3, :] = column_sum(s.dq2[0:128, :])
    s.small[3:4, :] = column_sum(s.dkv[:, 768:1536])
    d_inputs = s.d_mid[...] + norm_back(d_normed, unit_one, scale_one, gain_one)
    s.grad[...] = d_inputs.astype(LOW)
    grad_copy = pltpu.make_async_copy(s.grad, grad_ref, local.at[7 + LINES])
    grad_copy.start()

    s.pieces[...] = jnp.zeros((8, 16, 128), WIDE)
    for j in range(8):
        s.pieces[j, 0:8, 0:96] = s.small[:, 96 * j : 96 * j + 96]
        for i in range(3):
            s.pieces[j, 8 + i : 9 + i, :] = s.wide[j : j + 1, 128 * i : 128 * i + 128]
    piece_copy = send_all(
        [(s.pieces.at[place(r)], s.pieces_got.at[r], near(r)) for r in range(1, 8)],
        s.pieces_got.at[pl.ds(1, 7)],
    )
    line_q.middle()
    line_v.back()
    line_k[0].middle()
    line_k[1].middle()
    line_q.back()
    piece_copy.wait_recv()
    total = s.pieces[me]
    for r in range(1, 8):
        total = total + s.pieces_got[r]
    s.rows_z[dp] = total
    z_copy = send_all(
        [(s.rows_z.at[dp], s.rows_z.at[dp], device) for device in others_z],
        s.rows_z.at[pl.ds(0, 3)],
    )
    line_k[0].back()
    line_k[1].back()
    for line in line_down + [line_out] + line_up:
        line.write()
    line_v.write()
    line_q.write()
    z_copy.wait_recv()
    small_ref[...] = s.rows_z[0] + s.rows_z[1] + s.rows_z[2] + s.rows_z[3]
    for line in line_k:
        line.write()
    out_copy.wait()
    grad_copy.wait()
    for line in lines:
        line.close()
    for copy in ring:
        if copy is not None:
            copy.wait_send()


def spread_kernel(total_ref, small_ref, out_in, grad_in, out_ref, grad_ref, *outs):
    gain_one, shift_one, qkv, bias_q, bias_v, out, bias_out = outs[:7]
    gain_two, shift_two, up, bias_up, down, bias_down = outs[7:]
    out_ref[...] = out_in[...]
    grad_ref[...] = grad_in[...]
    for i in range(2):
        cols = slice(384 * i, 384 * i + 384)
        for j in range(4):
            down[96 * j : 96 * j + 96, cols] = total_ref[2 * j + i].astype(WIDE)
        out[:, cols] = total_ref[8 + i].astype(WIDE)
    for j in range(8):
        up[:, 384 * j : 384 * j + 384] = total_ref[10 + j].astype(WIDE)
    for j in range(6):
        qkv[:, 384 * j : 384 * j + 384] = total_ref[18 + j].astype(WIDE)
    rows = (gain_one, shift_one, bias_q, bias_v, bias_out, gain_two, shift_two, bias_down)
    for j, target in enumerate(rows):
        target[...] = small_ref[j, 0:96]
    for i in range(3):
        bias_up[128 * i : 128 * i + 128] = small_ref[8 + i, :]


def fused_device(
    inputs,
    gain_one,
    shift_one,
    w_qkv,
    bias_q,
    bias_v,
    w_out,
    bias_out,
    gain_two,
    shift_two,
    w_up,
    bias_up,
    w_down,
    bias_down,
    lengths,
    cotangent,
):
    vmem = pl.BlockSpec(memory_space=pltpu.VMEM)
    anywhere = pl.BlockSpec(memory_space=pl.ANY)
    vectors = [gain_one, shift_one, bias_q, bias_v, bias_out, gain_two, shift_two]
    vectors = vectors + [bias_up, bias_down]
    tokens, width = inputs.shape
    layer_out, grad_inputs, total, small = pl.pallas_call(
        layer_kernel,
        out_shape=(
            jax.ShapeDtypeStruct((tokens, width), LOW),
            jax.ShapeDtypeStruct((tokens, width), LOW),
            jax.ShapeDtypeStruct((24, 96, 384), LOW),
            jax.ShapeDtypeStruct((16, 128), WIDE),
        ),
        in_specs=[pl.BlockSpec(memory_space=pltpu.SMEM)] + [vmem] * 11 + [anywhere] * 4,
        out_specs=(anywhere, anywhere, anywhere, vmem),
        scratch_shapes=[pltpu.VMEM(shape, kind) for shape, kind in SCRATCH.values()]
        + [
            pltpu.SemaphoreType.DMA((RING + LINES,)),
            pltpu.SemaphoreType.DMA((LANDINGS,)),
            pltpu.SemaphoreType.DMA((8 + LINES,)),
        ],
        compiler_params=pltpu.CompilerParams(
            collective_id=0, has_side_effects=True, vmem_limit_bytes=VMEM_BYTES
        ),
        name="layer",
    )(lengths, inputs, cotangent, *vectors, w_qkv, w_out, w_up, w_down.reshape(32, 96, width))
    return pl.pallas_call(
        spread_kernel,
        out_shape=tuple(
            jax.ShapeDtypeStruct((tokens, width), LOW) for _ in range(2)
        )
        + tuple(
            jax.ShapeDtypeStruct(shape, WIDE)
            for shape in (
                (96,),
                (96,),
                (96, 2304),
                (96,),
                (96,),
                (96, 768),
                (96,),
                (96,),
                (96,),
                (96, 3072),
                (384,),
                (384, 768),
                (96,),
            )
        ),
        in_specs=[vmem] * 4,
        out_specs=(vmem,) * 15,
        compiler_params=pltpu.CompilerParams(vmem_limit_bytes=VMEM_BYTES),
        name="spread",
    )(total, small, layer_out, grad_inputs)


def per_device(*arguments):
    inputs, w_up = arguments[0], arguments[10]
    fits = (
        lax.axis_size("dp") == 4
        and lax.axis_size("col") == 8
        and inputs.shape == (128, 768)
        and w_up.shape == (768, 3072)
    )
    return fused_device(*arguments) if fits else general_device(*arguments)


def solution(mesh):
    return jax.shard_map(
        per_device,
        mesh=mesh,
        in_specs=(
            P(("dp", "col"), None),
            P(),
            P(),
            P(),
            P(),
            P(),
            P(),
            P(),
            P(),
            P(),
            P(),
            P(),
            P(),
            P(),
            P("dp", None),
            P(("dp", "col"), None),
        ),
        out_specs=(
            P(("dp", "col"), None),
            P(("dp", "col"), None),
            P("col"),
            P("col"),
            P("col", None),
            P("col"),
            P("col"),
            P("col", None),
            P("col"),
            P("col"),
            P("col"),
            P("col", None),
            P("col"),
            P("col", None),
            P("col"),
        ),
        check_vma=False,
    )
```

```python
import functools
import types

import jax
import jax.numpy as jnp
from jax import lax
from jax.experimental import pallas as pl
from jax.experimental.pallas import tpu as pltpu
from jax.sharding import PartitionSpec as P

H = 12
HEAD = 64


epsilon = 1e-05


def layer_norm(values, scales, offset):
    average = jnp.mean(values, axis=-1, keepdims=True)
    centered = values - average
    spread = jnp.mean(centered * centered, axis=-1, keepdims=True)
    return centered * lax.rsqrt(spread + epsilon) * scales + offset


def documents(places, row_lengths):
    finish = jnp.cumsum(row_lengths)
    begins = finish - row_lengths
    inside = (places[:, None] >= begins[None, :]) & (places[:, None] < finish[None, :])
    numbers = jnp.arange(row_lengths.shape[0], dtype=jnp.int32)
    doc_index = jnp.sum(jnp.where(inside, numbers[None, :], 0), axis=1)
    first_place = jnp.sum(jnp.where(inside, begins[None, :], 0), axis=1)
    return (doc_index, first_place == places)


def general_device(
    inputs,
    gain_one,
    shift_one,
    w_qkv,
    bias_q,
    bias_v,
    w_out,
    bias_out,
    gain_two,
    shift_two,
    w_up,
    bias_up,
    w_down,
    bias_down,
    lengths,
    cotangent,
):
    col_count = lax.axis_size("col")
    col_place = lax.axis_index("col")
    tok_rows = inputs.shape[0]
    model_width = inputs.shape[1]
    row_len = tok_rows * col_count
    block_rows = min(512, row_len)
    block_count = row_len // block_rows
    places = jnp.arange(row_len, dtype=jnp.int32)
    doc_index, first_flag = documents(places, lengths[0])
    own_first = col_place * tok_rows
    key_places = own_first + jnp.arange(tok_rows, dtype=jnp.int32)
    key_doc = lax.dynamic_slice_in_dim(doc_index, own_first, tok_rows, 0)
    key_first = lax.dynamic_slice_in_dim(first_flag, own_first, tok_rows, 0)
    floated = inputs.astype(jnp.float32)
    norm_first, first_back = jax.vjp(layer_norm, floated, gain_one, shift_one)
    normed_one = norm_first.astype(jnp.bfloat16)
    joined = jnp.dot(normed_one, w_qkv, preferred_element_type=jnp.float32)
    queries = (joined[:, :model_width] + bias_q).astype(jnp.bfloat16)
    key_rows = joined[:, model_width : 2 * model_width].astype(jnp.bfloat16)
    value_rows = (joined[:, 2 * model_width :] + bias_v).astype(jnp.bfloat16)
    key_heads = key_rows.reshape(tok_rows, H, HEAD)
    value_heads = value_rows.reshape(tok_rows, H, HEAD)
    all_queries = lax.all_gather(queries, "col", axis=0, tiled=True)

    def block_terms(source, block_index, carried):
        first_row = block_index * block_rows
        q_block = lax.dynamic_slice_in_dim(source, first_row, block_rows, 0).reshape(
            block_rows, H, HEAD
        )
        q_places = first_row + jnp.arange(block_rows, dtype=jnp.int32)
        q_doc = lax.dynamic_slice_in_dim(doc_index, first_row, block_rows, 0)
        scores = (
            jnp.einsum("khd,qhd->hkq", key_heads, q_block, preferred_element_type=jnp.float32)
            * 0.125
        )
        allowed = (key_places[:, None] <= q_places[None, :]) & (key_doc[:, None] == q_doc[None, :])
        chosen = (
            allowed
            & (key_places[:, None] < q_places[None, :])
            & jnp.logical_not(key_first)[:, None]
        )
        picked = jnp.where(chosen, jax.nn.softplus(scores[0]), 0.0) / row_len
        forgot = carried[:, None] + jnp.cumsum(picked, axis=1) - picked
        logits = jnp.where(allowed[None], scores - forgot[None], -jnp.inf)
        return (q_block, scores, chosen, picked, logits)

    def forward_block(carried, block_index):
        q_block, scores, chosen, picked, logits = block_terms(all_queries, block_index, carried)
        row_top = jnp.max(logits, axis=1)
        safe_top = jnp.where(row_top > -jnp.inf, row_top, 0.0)
        raised = jnp.exp(logits - safe_top[:, None, :])
        totals = jnp.sum(raised, axis=1)
        numerator = jnp.einsum(
            "hkq,khd->qhd",
            raised.astype(jnp.bfloat16),
            value_heads,
            preferred_element_type=jnp.float32,
        )
        return (
            carried + jnp.sum(picked, axis=1),
            (carried, row_top.T, totals.T, numerator.reshape(block_rows, model_width)),
        )

    indices = jnp.arange(block_count, dtype=jnp.int32)
    unused, (block_starts, row_tops, row_totals, numerators) = lax.scan(
        forward_block, jnp.zeros((tok_rows,), jnp.float32), indices
    )
    row_tops = row_tops.reshape(row_len, H)
    row_totals = row_totals.reshape(row_len, H)
    numerators = numerators.reshape(row_len, model_width)
    got_top, got_total, got_numer = (
        lax.all_to_all(
            row_tops[None].astype(jnp.bfloat16), "col", split_axis=1, concat_axis=0, tiled=True
        ).astype(jnp.float32),
        lax.all_to_all(
            row_totals[None].astype(jnp.bfloat16), "col", split_axis=1, concat_axis=0, tiled=True
        ).astype(jnp.float32),
        lax.all_to_all(
            numerators[None].astype(jnp.bfloat16), "col", split_axis=1, concat_axis=0, tiled=True
        ).astype(jnp.float32),
    )
    row_best = jnp.max(got_top, axis=0)
    factor = jnp.exp(got_top - row_best[None])
    totals_own = jnp.sum(factor * got_total, axis=0)
    numer_own = jnp.sum(got_numer.reshape(col_count, tok_rows, H, HEAD) * factor[..., None], axis=0)
    attended = (numer_own / totals_own[..., None]).reshape(tok_rows, model_width)
    row_lse = row_best + jnp.log(totals_own)
    attended_low = attended.astype(jnp.bfloat16)
    middle = floated + jnp.dot(attended_low, w_out, preferred_element_type=jnp.float32) + bias_out
    norm_second, second_back = jax.vjp(layer_norm, middle, gain_two, shift_two)
    normed_two = norm_second.astype(jnp.bfloat16)
    hidden = jnp.dot(normed_two, w_up, preferred_element_type=jnp.float32) + bias_up
    active_full, gelu_back = jax.vjp(jax.nn.gelu, hidden)
    active = active_full.astype(jnp.bfloat16)
    layer_out = (
        middle + jnp.dot(active, w_down, preferred_element_type=jnp.float32) + bias_down
    ).astype(jnp.bfloat16)
    d_output = cotangent.astype(jnp.float32)
    grad_w_down = jnp.einsum("tf,td->fd", active, cotangent, preferred_element_type=jnp.float32)
    grad_bias_down = jnp.sum(d_output, axis=0)
    d_active = jnp.einsum("td,fd->tf", cotangent, w_down, preferred_element_type=jnp.float32)
    d_hidden = gelu_back(d_active)[0].astype(jnp.bfloat16)
    grad_w_up = jnp.einsum("td,tf->df", normed_two, d_hidden, preferred_element_type=jnp.float32)
    grad_bias_up = jnp.sum(d_hidden.astype(jnp.float32), axis=0)
    d_normed_two = jnp.einsum("tf,df->td", d_hidden, w_up, preferred_element_type=jnp.float32)
    d_middle_norm, grad_gain_two, grad_shift_two = second_back(d_normed_two)
    d_middle = d_output + d_middle_norm
    d_branch = d_middle.astype(jnp.bfloat16)
    grad_w_out = jnp.einsum("td,te->de", attended_low, d_branch, preferred_element_type=jnp.float32)
    grad_bias_out = jnp.sum(d_middle, axis=0)
    d_attended = jnp.einsum(
        "te,de->td", d_branch, w_out, preferred_element_type=jnp.float32
    ).astype(jnp.bfloat16)
    row_delta = jnp.sum(
        (d_attended.astype(jnp.float32) * attended).reshape(tok_rows, H, HEAD), axis=2
    )
    back_queries, gathered_grad = (
        lax.all_gather(queries, "col", axis=0, tiled=True),
        lax.all_gather(d_attended, "col", axis=0, tiled=True),
    )
    all_lse, all_delta = (
        lax.all_gather(row_lse, "col", axis=0, tiled=True),
        lax.all_gather(row_delta, "col", axis=0, tiled=True),
    )

    def backward_block(carried_state, inputs_block):
        later_sum, key_grad, value_grad = carried_state
        block_index, carried = inputs_block
        q_block, scores, chosen, picked, logits = block_terms(back_queries, block_index, carried)
        first_row = block_index * block_rows
        grad_block = lax.dynamic_slice_in_dim(gathered_grad, first_row, block_rows, 0).reshape(
            block_rows, H, HEAD
        )
        lse_block = lax.dynamic_slice_in_dim(all_lse, first_row, block_rows, 0)
        delta_block = lax.dynamic_slice_in_dim(all_delta, first_row, block_rows, 0)
        weights = jnp.exp(logits - lse_block.T[:, None, :])
        value_grad = value_grad + jnp.einsum(
            "hkq,qhd->khd",
            weights.astype(jnp.bfloat16),
            grad_block,
            preferred_element_type=jnp.float32,
        )
        d_weights = jnp.einsum(
            "khd,qhd->hkq", value_heads, grad_block, preferred_element_type=jnp.float32
        )
        d_logits = weights * (d_weights - delta_block.T[:, None, :])
        d_forgot = -jnp.sum(d_logits, axis=0)
        block_sum = jnp.sum(d_forgot, axis=1)
        d_picked = later_sum[:, None] + block_sum[:, None] - jnp.cumsum(d_forgot, axis=1)
        d_select = jnp.where(chosen, jax.nn.sigmoid(scores[0]) * d_picked / row_len, 0.0)
        d_scores = d_logits.at[0].add(d_select).astype(jnp.bfloat16)
        key_grad = (
            key_grad
            + jnp.einsum("hkq,qhd->khd", d_scores, q_block, preferred_element_type=jnp.float32)
            * 0.125
        )
        query_grad = (
            jnp.einsum("hkq,khd->qhd", d_scores, key_heads, preferred_element_type=jnp.float32)
            * 0.125
        )
        return (
            (later_sum + block_sum, key_grad, value_grad),
            query_grad.reshape(block_rows, model_width),
        )

    zero_heads = jnp.zeros((tok_rows, H, HEAD), jnp.float32)
    initial = (jnp.zeros((tok_rows,), jnp.float32), zero_heads, zero_heads)
    (unused_sum, key_grad, value_grad), query_parts = lax.scan(
        backward_block, initial, (indices, block_starts), reverse=True
    )
    query_parts = query_parts.reshape(row_len, model_width)
    d_queries = lax.psum_scatter(query_parts, "col", scatter_dimension=0, tiled=True).astype(
        jnp.bfloat16
    )
    d_keys = key_grad.reshape(tok_rows, model_width).astype(jnp.bfloat16)
    d_values = value_grad.reshape(tok_rows, model_width).astype(jnp.bfloat16)
    d_joined = jnp.concatenate([d_queries, d_keys, d_values], axis=1)
    grad_w_qkv = jnp.einsum("td,te->de", normed_one, d_joined, preferred_element_type=jnp.float32)
    grad_bias_q = jnp.sum(d_queries.astype(jnp.float32), axis=0)
    grad_bias_v = jnp.sum(d_values.astype(jnp.float32), axis=0)
    d_normed_one = jnp.einsum("te,de->td", d_joined, w_qkv, preferred_element_type=jnp.float32)
    d_input_norm, grad_gain_one, grad_shift_one = first_back(d_normed_one)
    grad_inputs = (d_middle + d_input_norm).astype(jnp.bfloat16)
    (
        shard_gain_one,
        shard_shift_one,
        shard_w_qkv,
        shard_bias_q,
        shard_bias_v,
        shard_w_out,
        shard_bias_out,
        shard_gain_two,
        shard_shift_two,
        shard_w_up,
        shard_bias_up,
        shard_w_down,
        shard_bias_down,
    ) = (
        lax.psum_scatter(grad_gain_one, "col", scatter_dimension=0, tiled=True),
        lax.psum_scatter(grad_shift_one, "col", scatter_dimension=0, tiled=True),
        lax.psum_scatter(grad_w_qkv, "col", scatter_dimension=0, tiled=True),
        lax.psum_scatter(grad_bias_q, "col", scatter_dimension=0, tiled=True),
        lax.psum_scatter(grad_bias_v, "col", scatter_dimension=0, tiled=True),
        lax.psum_scatter(grad_w_out, "col", scatter_dimension=0, tiled=True),
        lax.psum_scatter(grad_bias_out, "col", scatter_dimension=0, tiled=True),
        lax.psum_scatter(grad_gain_two, "col", scatter_dimension=0, tiled=True),
        lax.psum_scatter(grad_shift_two, "col", scatter_dimension=0, tiled=True),
        lax.psum_scatter(grad_w_up, "col", scatter_dimension=0, tiled=True),
        lax.psum_scatter(grad_bias_up, "col", scatter_dimension=0, tiled=True),
        lax.psum_scatter(grad_w_down, "col", scatter_dimension=0, tiled=True),
        lax.psum_scatter(grad_bias_down, "col", scatter_dimension=0, tiled=True),
    )
    summed = (
        lax.psum(shard_gain_one.astype(jnp.bfloat16), "dp").astype(jnp.float32),
        lax.psum(shard_shift_one.astype(jnp.bfloat16), "dp").astype(jnp.float32),
        lax.psum(shard_w_qkv.astype(jnp.bfloat16), "dp").astype(jnp.float32),
        lax.psum(shard_bias_q.astype(jnp.bfloat16), "dp").astype(jnp.float32),
        lax.psum(shard_bias_v.astype(jnp.bfloat16), "dp").astype(jnp.float32),
        lax.psum(shard_w_out.astype(jnp.bfloat16), "dp").astype(jnp.float32),
        lax.psum(shard_bias_out.astype(jnp.bfloat16), "dp").astype(jnp.float32),
        lax.psum(shard_gain_two.astype(jnp.bfloat16), "dp").astype(jnp.float32),
        lax.psum(shard_shift_two.astype(jnp.bfloat16), "dp").astype(jnp.float32),
        lax.psum(shard_w_up.astype(jnp.bfloat16), "dp").astype(jnp.float32),
        lax.psum(shard_bias_up.astype(jnp.bfloat16), "dp").astype(jnp.float32),
        lax.psum(shard_w_down.astype(jnp.bfloat16), "dp").astype(jnp.float32),
        lax.psum(shard_bias_down.astype(jnp.bfloat16), "dp").astype(jnp.float32),
    )
    return (
        layer_out,
        grad_inputs,
        summed[0],
        summed[1],
        summed[2],
        summed[3],
        summed[4],
        summed[5],
        summed[6],
        summed[7],
        summed[8],
        summed[9],
        summed[10],
        summed[11],
        summed[12],
    )


MESH = pl.DeviceIdType.MESH
LOW = jnp.bfloat16
WIDE = jnp.float32
FAR = 1e30
VMEM_BYTES = 63 * 2**20


def dot(a, b):
    return jnp.dot(a, b, preferred_element_type=WIDE)


def dot_rows(a, b):
    return lax.dot_general(a, b, (((1,), (1,)), ((), ())), preferred_element_type=WIDE)


def split_low(values):
    high = values.astype(LOW)
    return high, (values - high.astype(WIDE)).astype(LOW)


def column_sum(values):
    return jnp.sum(values.astype(WIDE), axis=0, keepdims=True)


def norm_parts(values):
    average = jnp.mean(values, axis=-1, keepdims=True)
    centered = values - average
    spread = jnp.mean(centered * centered, axis=-1, keepdims=True)
    scale = lax.rsqrt(spread + epsilon)
    return centered * scale, scale


def norm_back(grad, unit, scale, gain):
    scaled = grad * gain
    first = jnp.mean(scaled, axis=-1, keepdims=True)
    second = jnp.mean(scaled * unit, axis=-1, keepdims=True)
    return scale * (scaled - first - unit * second)


def gelu_parts(hidden):
    square = hidden * hidden
    bend = jnp.tanh(0.7978845608028654 * hidden * (1.0 + 0.044715 * square))
    half = 0.5 * (1.0 + bend)
    curve = 0.7978845608028654 * (1.0 + 3 * 0.044715 * square)
    return hidden * half, half + 0.5 * hidden * (1.0 - bend * bend) * curve


SCRATCH = dict(
    wqkv=((768, 2304), LOW),
    wout=((768, 768), LOW),
    wup=((768, 3072), LOW),
    wdown=((32, 96, 768), LOW),
    wup_own=((768, 384), LOW),
    n1=((8, 128, 768), LOW),
    n1_t=((8, 96, 1024), LOW),
    n2=((8, 128, 768), LOW),
    n2_t=((8, 96, 1024), LOW),
    cot=((8, 128, 768), LOW),
    keys=((1024, 768), LOW),
    values=((1024, 768), LOW),
    turned=((6, 128, 1024), LOW),
    probs=((6, 1024, 256), LOW),
    sums=((8, 8, 128), WIDE),
    back_sums=((8, 8, 128), WIDE),
    forgot=((128, 1024), WIDE),
    forgot_t=((1024, 128), WIDE),
    sig=((128, 1024), WIDE),
    d_forgot_t=((1024, 128), WIDE),
    second_head=((1024, 128), LOW),
    q_low=((128, 768), LOW),
    q_turned=((768, 128), LOW),
    att_t=((768, 128), WIDE),
    att_low_t=((8, 96, 128), LOW),
    act=((128, 3072), LOW),
    d_act=((128, 3072), WIDE),
    d_hidden=((128, 3072), LOW),
    middle=((128, 768), WIDE),
    d_mid=((128, 768), WIDE),
    unit_two=((128, 768), WIDE),
    d_att=((128, 768), LOW),
    d_att_t=((768, 128), LOW),
    dq_t=((768, 128), WIDE),
    act_t=((384, 1024), LOW),
    slope=((1024, 384), LOW),
    db2=((256, 768), LOW),
    dq2=((256, 768), LOW),
    lhs_out=((4, 96, 256), LOW),
    lhs_q=((4, 96, 256), LOW),
    give_out=((4, 96, 128), LOW),
    give_q=((4, 96, 128), LOW),
    dkv=((1024, 1536), LOW),
    grads_out=((4, 96, 768), LOW),
    grads_q=((4, 96, 768), LOW),
    grads_k=((2, 4, 96, 768), LOW),
    grads_v=((2, 4, 96, 768), LOW),
    core_k=((4, 96, 768), LOW),
    core_v=((4, 96, 768), LOW),
    one=((4, 2, 2, 96, 384), LOW),
    two=((4, 2, 96, 384), LOW),
    d_n1=((2, 4, 128, 768), LOW),
    core_n1=((4, 128, 768), LOW),
    one_n1=((2, 2, 128, 384), LOW),
    two_n1=((2, 128, 384), LOW),
    up_give=((8, 96, 384), LOW),
    mine=((24, 96, 384), LOW),
    got_z=((24, 96, 384), LOW),
    got_mid=((24, 96, 384), LOW),
    total=((24, 96, 384), LOW),
    small=((8, 768), WIDE),
    wide=((8, 384), WIDE),
    pieces=((8, 16, 128), WIDE),
    pieces_got=((8, 16, 128), WIDE),
    rows_z=((4, 16, 128), WIDE),
    out=((128, 768), LOW),
    grad=((128, 768), LOW),
)
SLOTS = (0, 2, 6, 4)
RING = 24
LINES = 15
LANDINGS = 78


def layer_kernel(
    lengths_ref,
    x_ref,
    cot_ref,
    gain_one,
    shift_one,
    bias_q,
    bias_v,
    bias_out,
    gain_two,
    shift_two,
    bias_up,
    bias_down,
    w_qkv,
    w_out,
    w_up,
    w_down,
    out_ref,
    grad_ref,
    total_ref,
    small_ref,
    *scratch,
):
    s = types.SimpleNamespace(**dict(zip(SCRATCH, scratch)))
    gain_one, shift_one, bias_q, bias_v, bias_out, gain_two, shift_two, bias_up, bias_down = (
        ref[...].reshape(1, -1)
        for ref in (
            gain_one,
            shift_one,
            bias_q,
            bias_v,
            bias_out,
            gain_two,
            shift_two,
            bias_up,
            bias_down,
        )
    )
    sent, landed, local = scratch[len(SCRATCH) :]
    me = lax.axis_index("col")
    dp = lax.axis_index("dp")
    core = lax.rem(me, 2)
    x_bit = lax.rem(lax.div(me, 2), 2)
    y_bit = lax.div(me, 4)

    def place(r):
        step = (r & 1) * (1 - 2 * core) + ((r >> 1) & 1) * (2 - 4 * x_bit)
        return me + step + (r >> 2) * (4 - 8 * y_bit)

    def near(r):
        return (dp, place(r))

    z_pair = (dp + 1 - 2 * lax.rem(dp, 2), me)
    z_middle = (3 - dp, me)
    inner = (dp == 1) | (dp == 2)
    outer = jnp.logical_not(inner)
    barrier = pltpu.get_barrier_semaphore()
    others_z = [(lax.rem(dp + k, 4), me) for k in (1, 2, 3)]
    for device in [near(r) for r in range(1, 8)] + others_z:
        pl.semaphore_signal(barrier, inc=1, device_id=device, device_id_type=MESH)

    landings = iter(range(LANDINGS))
    ring = [None] * RING
    turns = iter(range(10**6))

    def message(source, target, device, send_at, land_at):
        return pltpu.make_async_remote_copy(
            src_ref=source,
            dst_ref=target,
            send_sem=sent.at[send_at],
            recv_sem=landed.at[land_at],
            device_id=device,
            device_id_type=MESH,
        )

    def send_all(copies, whole):
        send_at, land_at = next(turns) % RING, next(landings)
        if ring[send_at] is not None:
            ring[send_at].wait_send()
        for source, target, device in copies:
            message(source, target, device, send_at, land_at).start()
        ring[send_at] = message(whole, whole, near(1), send_at, land_at)
        return ring[send_at]

    def send(source, target, device):
        return send_all([(source, target, device)], source)

    loads = {}
    own_cols = pl.ds(pl.multiple_of(384 * me, 128), 384)
    for at, (name, source, target) in enumerate(
        (
            ("kv", w_qkv.at[:, pl.ds(768, 1536)], s.wqkv.at[:, pl.ds(768, 1536)]),
            ("q", w_qkv.at[:, pl.ds(0, 768)], s.wqkv.at[:, pl.ds(0, 768)]),
            ("down", w_down, s.wdown),
            ("out", w_out, s.wout),
            ("up", w_up, s.wup),
            ("own", w_up.at[:, own_cols], s.wup_own),
        )
    ):
        loads[name] = pltpu.make_async_copy(source, target, local.at[at])
        loads[name].start()

    class Gather:
        def __init__(self, ref):
            self.ref = ref
            self.left, self.right = pl.ds(0, 384), pl.ds(384, 384)

        def start(self):
            ref, own = self.ref, self.ref.at[0]
            pair = []
            for first, second in ((self.left, self.right), (self.right, self.left)):
                copies = [
                    (own.at[:, first], ref.at[2, :, first], near(2)),
                    (own.at[:, second], ref.at[4, :, second], near(4)),
                ]
                pair.append(send_all(copies, own))
            self.early, self.late = pair
            self.other = send(own, ref.at[1], near(1))

        def forward(self):
            ref = self.ref
            self.early.wait_recv()
            copies = [
                (ref.at[2, :, self.left], ref.at[6, :, self.left], near(4)),
                (ref.at[4, :, self.right], ref.at[6, :, self.right], near(2)),
            ]
            self.far = send_all(copies, ref.at[6])

        def to_core(self):
            ref = self.ref
            self.late.wait_recv()
            self.more = [send(ref.at[r], ref.at[r + 1], near(1)) for r in (2, 4)]

        def diagonal(self):
            self.far.wait_recv()
            self.more.append(send(self.ref.at[6], self.ref.at[7], near(1)))

        def chip(self, number):
            (self.other if number == 0 else self.more[number - 1]).wait_recv()

        def rows(self, number):
            return self.ref[2 * number : 2 * number + 2].reshape(256, 768)

    values_one = x_ref[...].astype(WIDE)
    unit_one, scale_one = norm_parts(values_one)
    normed_one = (unit_one * gain_one + shift_one).astype(LOW)
    s.n1[0] = normed_one
    s.cot[0] = cot_ref[...]
    gather_one, gather_cot, gather_two = Gather(s.n1), Gather(s.cot), Gather(s.n2)
    pl.semaphore_wait(barrier, 10)
    gather_one.start()

    def share(source, lhs, give):
        for slot, r in enumerate(SLOTS):
            ours = place(r)
            lhs[slot, :, 0:128] = source(ours)
            give[slot] = source(ours + 1 - 2 * core)
        return send(give, lhs.at[:, :, pl.ds(128, 128)], near(1))

    def turn_block(source, target, r):
        target[:, :, 128 * r : 128 * r + 128] = source[r].T.reshape(8, 96, 128)

    def form_keys(number):
        at = 256 * number
        s.keys[at : at + 256, :] = dot(gather_one.rows(number), s.wqkv[:, 768:1536]).astype(LOW)

    def form_values(number):
        at = 256 * number
        rows = dot(gather_one.rows(number), s.wqkv[:, 1536:2304]) + bias_v
        s.values[at : at + 256, :] = rows.astype(LOW)

    def active_grad(first, last):
        for j in range(first, last):
            rows = s.wdown[4 * j : 4 * j + 4].reshape(384, 768)
            s.d_act[:, 384 * j : 384 * j + 384] = dot_rows(cot_ref[...], rows)

    loads["kv"].wait()
    gather_one.chip(0)
    form_keys(0)
    form_values(0)
    loads["q"].wait()
    q = (dot(normed_one, s.wqkv[:, 0:768]) + bias_q).astype(LOW)
    q = (q.astype(WIDE) * 0.125).astype(LOW)
    s.q_low[...] = q
    row_at = lax.broadcasted_iota(jnp.int32, (128, 128), 0)
    lane_at = lax.broadcasted_iota(jnp.int32, (128, 128), 1)
    query_at = row_at + me * 128
    begin_one = lengths_ref[0, 0]
    begin_two = begin_one + lengths_ref[0, 1]
    begin_three = begin_two + lengths_ref[0, 2]
    begin = jnp.where(query_at >= begin_one, begin_one, 0)
    begin = jnp.where(query_at >= begin_two, begin_two, begin)
    begin = jnp.where(query_at >= begin_three, begin_three, begin)
    earlier = jnp.where(lane_at < row_at, 1.0, 0.0).astype(LOW)
    first_lanes = jnp.where(lane_at < 64, 1.0, 0.0)
    head_zero = (s.q_low[:, 0:128].astype(WIDE) * first_lanes).astype(LOW)

    def picks(number):
        at = 256 * number
        scores = dot_rows(head_zero, s.keys[at : at + 256, 0:128])
        key_at = jnp.concatenate(
            [lane_at + place(r) * 128 for r in (2 * number, 2 * number + 1)], axis=1
        )
        queries_at = jnp.concatenate([query_at, query_at], axis=1)
        begins = jnp.concatenate([begin, begin], axis=1)
        allowed = (key_at <= queries_at) & (key_at >= begins)
        chosen = (key_at < queries_at) & (key_at > begins)
        small_exp = jnp.exp(-jnp.abs(scores))
        soft = jnp.maximum(scores, 0.0) + jnp.log1p(small_exp)
        picked = jnp.where(chosen, soft, 0.0) * (1.0 / 1024)
        high, rest = split_low(picked)
        sums = column_sum(picked)
        s.sums[0, 2 * number : 2 * number + 1, :] = sums[:, 0:128]
        s.sums[0, 2 * number + 1 : 2 * number + 2, :] = sums[:, 128:256]
        within = dot(earlier, high) + dot(earlier, rest)
        s.forgot[:, at : at + 256] = jnp.where(allowed, within, FAR)
        sigmoid = jnp.where(scores >= 0, 1.0, small_exp) / (1.0 + small_exp)
        s.sig[:, at : at + 256] = jnp.where(chosen, sigmoid, 0.0) * (1.0 / 1024)

    def turn(source, pair):
        at = 128 * pair
        for r in range(8):
            rows = slice(128 * r, 128 * r + 128)
            s.turned[pair, :, rows] = source[rows, at : at + 128].T

    picks(0)
    turn_block(s.n1, s.n1_t, 0)
    gather_one.forward()
    s.q_turned[...] = q.T
    loads["down"].wait()
    active_grad(0, 6)
    gather_one.to_core()
    active_grad(6, 8)

    gather_one.diagonal()
    for number in (1, 2, 3):
        gather_one.chip(number)
        form_keys(number)
        picks(number)
    sum_copy = send_all(
        [(s.sums.at[0], s.sums.at[r], near(r)) for r in range(1, 8)], s.sums.at[pl.ds(1, 7)]
    )
    gather_cot.start()
    for number in (1, 2, 3):
        form_values(number)
    for pair in range(6):
        turn(s.values, pair)
    share_one = share(lambda at: s.n1_t[at, :, 0:128], s.lhs_q, s.give_q)
    sum_copy.wait_recv()

    def others(sums, later):
        rows = [jnp.zeros((1, 128), WIDE) for _ in range(8)]
        for d in range(1, 8):
            ahead = place(d) > me if later else place(d) < me
            weight = jnp.where(ahead, 1.0, 0.0)
            for r in range(8):
                rows[r] = rows[r] + weight * sums[d, (r ^ d) : (r ^ d) + 1, :]
        return rows

    for r, row in enumerate(others(s.sums, False)):
        at = 128 * r
        s.forgot_t[at : at + 128, :] = (s.forgot[:, at : at + 128] + row).T

    feature_at = lax.broadcasted_iota(jnp.int32, (128, 256), 0)
    column_at = lax.broadcasted_iota(jnp.int32, (128, 256), 1)
    own_head_t = jnp.where((feature_at < 64) == (column_at < 128), 1.0, 0.0).astype(LOW)
    long_row = lax.broadcasted_iota(jnp.int32, (256, 128), 0)
    long_lane = lax.broadcasted_iota(jnp.int32, (256, 128), 1)
    own_head = jnp.where((long_row < 128) == (long_lane < 64), 1.0, 0.0).astype(LOW)

    def both_t(values):
        return jnp.concatenate([values, values], axis=1) * own_head_t

    def both(values):
        return jnp.concatenate([values, values], axis=0) * own_head

    def attend(pair):
        at = 128 * pair
        scores = dot(s.keys[:, at : at + 128], both_t(s.q_turned[at : at + 128, :]))
        forgot = s.forgot_t[...]
        logits = scores - jnp.concatenate([forgot, forgot], axis=1)
        raised = jnp.exp(logits - jnp.max(logits, axis=0, keepdims=True))
        probs = (raised * (1.0 / jnp.sum(raised, axis=0, keepdims=True))).astype(LOW)
        s.probs[pair] = probs
        mixed = dot(s.turned[pair], probs)
        s.att_t[at : at + 64, :] = mixed[0:64, 0:128]
        s.att_t[at + 64 : at + 128, :] = mixed[64:128, 128:256]

    for pair in range(6):
        if pair == 2:
            gather_cot.forward()
        if pair == 4:
            gather_cot.to_core()
        attend(pair)

    attended_low_t = s.att_t[...].astype(LOW)
    s.att_low_t[...] = attended_low_t.reshape(8, 96, 128)
    loads["out"].wait()
    middle = values_one + dot(attended_low_t.T, s.wout[...]) + bias_out
    s.middle[...] = middle
    unit_two, scale_two = norm_parts(middle)
    s.unit_two[...] = unit_two
    normed_two = (unit_two * gain_two + shift_two).astype(LOW)
    s.n2[0] = normed_two
    gather_two.start()
    share_att = share(lambda at: s.att_low_t[at], s.lhs_out, s.give_out)
    gather_cot.diagonal()
    loads["up"].wait()
    for j in range(4):
        at = 768 * j
        hidden = dot(normed_two, s.wup[:, at : at + 768]) + bias_up[:, at : at + 768]
        active, slope = gelu_parts(hidden)
        s.act[:, at : at + 768] = active.astype(LOW)
        d_hidden = (s.d_act[:, at : at + 768] * slope).astype(LOW)
        s.d_hidden[:, at : at + 768] = d_hidden
        s.wide[2 * j : 2 * j + 1, :] = column_sum(d_hidden[:, 0:384])
        s.wide[2 * j + 1 : 2 * j + 2, :] = column_sum(d_hidden[:, 384:768])

    d_output = cot_ref[...].astype(WIDE)
    parts = []
    for j in range(3):
        parts.append(dot_rows(s.d_hidden[...], s.wup[256 * j : 256 * j + 256, :]))
    d_normed = jnp.concatenate(parts, axis=1)
    gather_two.forward()
    unit_two = s.unit_two[...]
    s.small[5:6, :] = column_sum(d_normed * unit_two)
    s.small[6:7, :] = column_sum(d_normed)
    s.small[7:8, :] = column_sum(d_output)
    d_middle = d_output + norm_back(d_normed, unit_two, scale_two, gain_two)
    s.d_mid[...] = d_middle
    s.small[4:5, :] = column_sum(d_middle)
    d_branch = d_middle.astype(LOW)
    s.db2[0:128, :] = d_branch
    share_branch = send(s.db2.at[pl.ds(0, 128)], s.db2.at[pl.ds(128, 128)], near(1))
    d_att_t = dot(s.wout[...], d_branch.T).astype(LOW)
    s.d_att_t[...] = d_att_t
    s.d_att[...] = d_att_t.T
    gather_two.to_core()

    class Unit:
        def __init__(self, rows, grads, one, two, core=None):
            self.rows, self.grads, self.one, self.two, self.core = rows, grads, one, two, core

        def across(self):
            self.copy = send(self.grads.at[1], self.core, near(1))
            self.grads = self.grads.at[0]

        def start(self):
            if self.core is not None:
                self.copy.wait_recv()
                total = self.grads[...].astype(WIDE) + self.core[...].astype(WIDE)
                self.grads[...] = total.astype(LOW)
            copies = [
                (self.grads.at[pl.ds(1, 2), :, pl.ds(0, 384)], self.one.at[0], near(2)),
                (self.grads.at[pl.ds(2, 2), :, pl.ds(384, 384)], self.one.at[1], near(4)),
            ]
            self.copy = send_all(copies, self.one)

        def pass_on(self):
            self.copy.wait_recv()
            copies = []
            for half, slot, index, r in ((0, 3, 1, 4), (1, 1, 0, 2)):
                cols = slice(384 * half, 384 * half + 384)
                total = self.grads[slot, :, cols].astype(WIDE)
                total = total + self.one[half, index].astype(WIDE)
                self.grads[slot, :, cols] = total.astype(LOW)
                source = self.grads.at[slot, :, pl.ds(384 * half, 384)]
                copies.append((source, self.two.at[half], near(r)))
            self.copy = send_all(copies, self.two)

        def finish(self, half):
            if half == 0:
                self.copy.wait_recv()
            total = self.grads[0, :, 384 * half : 384 * half + 384].astype(WIDE)
            total = total + self.one[half, half].astype(WIDE)
            return total + self.two[half].astype(WIDE)

    class Line:
        def __init__(self, blocks, places):
            self.blocks, self.places = blocks, places
            self.at = next(line_numbers)
            send_at = RING + self.at
            first, second = next(landings), next(landings)
            mine, total = s.mine.at[self.blocks], s.total.at[self.blocks]
            self.inward = message(mine, s.got_z.at[self.blocks], z_pair, send_at, first)
            self.across = message(mine, s.got_mid.at[self.blocks], z_middle, send_at, second)
            self.outward = message(total, total, z_pair, send_at, first)

        def start(self):
            pl.when(outer)(lambda: self.inward.start())

        def middle(self):
            @pl.when(inner)
            def _():
                blocks = self.blocks
                self.inward.wait_recv()
                total = s.mine[blocks].astype(WIDE) + s.got_z[blocks].astype(WIDE)
                s.mine[blocks] = total.astype(LOW)
                self.across.start()

        def back(self):
            @pl.when(inner)
            def _():
                blocks = self.blocks
                self.across.wait_recv()
                total = s.mine[blocks].astype(WIDE) + s.got_mid[blocks].astype(WIDE)
                s.total[blocks] = total.astype(LOW)
                self.across.wait_send()
                self.outward.start()

        def write(self):
            pl.when(outer)(lambda: self.outward.wait_recv())
            landing = local.at[6 + self.at]
            for source, target in self.places:
                pltpu.make_async_copy(
                    s.total.at[source], total_ref.at[target], landing
                ).start()
            self.written = pltpu.make_async_copy(
                s.total.at[self.blocks], total_ref.at[self.blocks], landing
            )

        def close(self):
            self.written.wait()
            pl.when(outer)(lambda: self.inward.wait_send())
            pl.when(inner)(lambda: self.outward.wait_send())

    line_numbers = iter(range(LINES))

    def plain(at, count):
        blocks = (pl.ds(at, count),)
        return Line(blocks, ((blocks, blocks),))

    def part(at, first):
        blocks = (at, pl.ds(first, 48))
        return Line(blocks, ((blocks, blocks),))

    def spread(r):
        return Line((pl.ds(10 + r, 2),), [(10 + i, 10 + place(i)) for i in (r, r + 1)])

    line_down = [plain(at, count) for at, count in ((0, 1), (1, 1), (2, 2), (4, 2), (6, 2))]
    line_out = plain(8, 2)
    line_up = [spread(2 * j) for j in range(4)]
    line_v, line_q = plain(22, 2), plain(18, 2)
    line_k = [plain(20, 1), part(21, 0), part(21, 48)]
    lines = line_down + [line_out] + line_up + [line_v, line_q] + line_k

    unit_out = Unit(96, s.grads_out, s.one.at[0], s.two.at[0])
    unit_q = Unit(96, s.grads_q, s.one.at[1], s.two.at[1])
    unit_k = Unit(96, s.grads_k, s.one.at[2], s.two.at[2], s.core_k)
    unit_v = Unit(96, s.grads_v, s.one.at[3], s.two.at[3], s.core_v)
    unit_n1 = Unit(128, s.d_n1, s.one_n1, s.two_n1, s.core_n1)

    def to_line(unit, at, *parts):
        for half in range(2):
            s.mine[at + half] = unit.finish(half).astype(LOW)
        for line in parts:
            line.start()

    def rows_of(source, odd):
        return jnp.concatenate([source[place(r + odd)] for r in SLOTS], axis=0)

    own_bias = jnp.zeros((1, 384), WIDE)
    for j in range(8):
        own_bias = own_bias + jnp.where(me == j, 1.0, 0.0) * bias_up[:, 384 * j : 384 * j + 384]
    loads["own"].wait()

    def own_units(number):
        gather_cot.chip(number)
        gather_two.chip(number)
        at = 256 * number
        hidden = dot(gather_two.rows(number), s.wup_own[...]) + own_bias
        active, slope = gelu_parts(hidden)
        d_active = dot_rows(gather_cot.rows(number), s.wdown[pl.ds(4 * me, 4)].reshape(384, 768))
        s.act_t[:, at : at + 256] = active.astype(LOW).T
        s.slope[at : at + 256, :] = (d_active * slope).astype(LOW)

    def out_unit():
        share_att.wait_recv()
        share_branch.wait_recv()
        grads = dot(s.lhs_out[...].reshape(384, 256), s.db2[...]).astype(LOW)
        s.grads_out[...] = grads.reshape(4, 96, 768)
        unit_out.start()

    def down_grads(half, parts):
        rows = s.act_t[192 * half : 192 * half + 192, :]
        grads = dot(rows, s.cot[...].reshape(1024, 768)).astype(LOW)
        for j in range(2):
            for i in range(2):
                block = grads[96 * j : 96 * j + 96, 384 * i : 384 * i + 384]
                s.mine[4 * half + 2 * j + i] = block
        for line in parts:
            line.start()

    def up_grads(odd):
        copies = []
        grads = dot(rows_of(s.n2_t, odd), s.slope[...]).astype(LOW).reshape(4, 96, 384)
        for slot, r in enumerate(SLOTS):
            if r + odd == 0:
                s.mine[10] = grads[0]
            else:
                s.up_give[r + odd] = grads[slot]
                copies.append((s.up_give.at[r + odd], s.mine.at[10 + r + odd], near(r + odd)))
        return copies, s.up_give.at[pl.ds(0, len(copies))]

    def logit_grads(pair):
        at = 128 * pair
        grad_t = s.d_att_t[at : at + 128, :]
        products = grad_t.astype(WIDE) * s.att_t[at : at + 128, :]
        delta = jnp.concatenate(
            [
                jnp.sum(products[0:64], axis=0, keepdims=True),
                jnp.sum(products[64:128], axis=0, keepdims=True),
            ],
            axis=1,
        )
        d_probs = dot(s.values[:, at : at + 128], both_t(grad_t))
        d_logits = s.probs[pair].astype(WIDE) * (d_probs - delta)
        both_heads = d_logits[:, 0:128] + d_logits[:, 128:256]
        if pair == 5:
            s.d_forgot_t[...] = both_heads
        else:
            s.d_forgot_t[...] += both_heads
        return d_logits

    def value_grads(pair):
        at = 128 * pair
        grads = dot(s.probs[pair], both(s.d_att[:, at : at + 128]))
        s.dkv[:, 768 + at : 896 + at] = grads.astype(LOW)

    def score_grads(pair, d_scores):
        at = 128 * pair
        turn(s.keys, pair)
        s.dkv[:, at : at + 128] = dot(d_scores, both(s.q_low[:, at : at + 128])).astype(LOW)
        grads = dot(s.turned[pair], d_scores)
        s.dq_t[at : at + 64, :] = grads[0:64, 0:128]
        s.dq_t[at + 64 : at + 128, :] = grads[64:128, 128:256]

    def attend_back(pair):
        d_logits = logit_grads(pair)
        value_grads(pair)
        score_grads(pair, d_logits.astype(LOW))

    def back_sums():
        d_logits = logit_grads(0)
        s.forgot_t[...] = d_logits[:, 0:128]
        s.second_head[...] = d_logits[:, 128:256].astype(LOW)
        for r in range(8):
            turned = s.d_forgot_t[128 * r : 128 * r + 128, :].T
            s.back_sums[0, r : r + 1, :] = column_sum(turned)
        return send_all(
            [(s.back_sums.at[0], s.back_sums.at[r], near(r)) for r in range(1, 8)],
            s.back_sums.at[pl.ds(1, 7)],
        )

    def key_unit(unit, half, odd):
        grads = s.dkv[:, 768 * half : 768 * half + 768]
        rows = rows_of(s.n1_t, odd)
        unit.grads[odd] = dot(rows, grads).astype(LOW).reshape(4, 96, 768)

    def first_pair():
        later_rows = others(s.back_sums, True)
        following = jnp.where(row_at > lane_at, 1.0, 0.0).astype(LOW)
        selected = []
        for r in range(8):
            at = 128 * r
            high, rest = split_low(s.d_forgot_t[at : at + 128, :])
            later = jnp.broadcast_to(later_rows[r], (128, 128)).T
            d_picked = -(dot(high, following) + dot(rest, following) + later)
            selected.append(s.forgot_t[at : at + 128, :] + s.sig[:, at : at + 128].T * d_picked)
        first_head = jnp.concatenate(selected, axis=0).astype(LOW)
        score_grads(0, jnp.concatenate([first_head, s.second_head[...]], axis=1))
        for j in range(6):
            at = 128 * j
            d_q = (s.dq_t[at : at + 128, :] * 0.125).astype(LOW)
            s.dq2[0:128, at : at + 128] = d_q.T
        return send(s.dq2.at[pl.ds(0, 128)], s.dq2.at[pl.ds(128, 128)], near(1))

    def query_unit():
        grads = dot(s.lhs_q[...].reshape(384, 256), s.dq2[...]).astype(LOW)
        s.grads_q[...] = grads.reshape(4, 96, 768)
        unit_q.start()

    def normed_part(j):
        cols = slice(256 * j, 256 * j + 256)
        grads = dot_rows(s.dkv[...], s.wqkv[cols, 768:2304]).astype(LOW)
        for slot, r in enumerate(SLOTS):
            for odd in range(2):
                at = 128 * (r + odd)
                s.d_n1[odd, slot, :, cols] = grads[at : at + 128]

    own_units(0)
    own_units(1)
    own_units(2)
    gather_two.diagonal()
    out_unit()
    own_units(3)
    down_grads(0, line_down[0:3])
    down_grads(1, line_down[3:5])
    for r in range(8):
        turn_block(s.n2, s.n2_t, r)
        if r:
            turn_block(s.n1, s.n1_t, r)
    up_odd = send_all(*up_grads(1))
    up_even = up_grads(0)
    attend_back(5)
    attend_back(4)
    unit_out.pass_on()
    line_down[0].middle()
    attend_back(3)
    attend_back(2)
    line_down[1].middle()
    attend_back(1)
    sum_copy = back_sums()
    up_even = send_all(*up_even)
    line_down[0].back()
    value_grads(0)
    key_unit(unit_v, 1, 1)
    line_down[2].middle()
    key_unit(unit_v, 1, 0)
    unit_v.across()
    line_down[1].back()
    to_line(unit_out, 8, line_out)
    sum_copy.wait_recv()
    share_q = first_pair()
    unit_v.start()
    line_down[3].middle()
    line_down[2].back()
    key_unit(unit_k, 0, 1)
    key_unit(unit_k, 0, 0)
    unit_k.across()
    share_one.wait_recv()
    share_q.wait_recv()
    query_unit()
    up_odd.wait_recv()
    up_even.wait_recv()
    for line in line_up:
        line.start()
    line_down[4].middle()
    line_down[3].back()
    normed_part(0)
    unit_v.pass_on()
    unit_k.start()
    line_out.middle()
    line_down[4].back()
    normed_part(1)
    normed_part(2)
    unit_n1.across()
    unit_q.pass_on()
    line_up[0].middle()
    line_out.back()
    to_line(unit_v, 22, line_v)
    mixed = jnp.zeros((128, 768), WIDE)
    for j in range(4):
        rows = s.wdown[8 * j : 8 * j + 8].reshape(768, 768)
        mixed = mixed + dot(s.act[:, 768 * j : 768 * j + 768], rows)
    s.out[...] = (s.middle[...] + mixed + bias_down).astype(LOW)
    out_copy = pltpu.make_async_copy(s.out, out_ref, local.at[6 + LINES])
    out_copy.start()
    unit_k.pass_on()
    unit_n1.start()
    line_up[1].middle()
    line_up[0].back()
    to_line(unit_q, 18, line_q)
    line_up[2].middle()
    to_line(unit_k, 20, *line_k)
    line_up[1].back()
    parts = []
    for i in range(3):
        rows = s.wqkv[256 * i : 256 * i + 256, 0:768]
        parts.append(dot_rows(s.dq2[0:128, :], rows))
    d_normed = jnp.concatenate(parts, axis=1)
    line_up[3].middle()
    line_up[2].back()
    unit_n1.pass_on()
    line_v.middle()
    line_up[3].back()
    d_normed = d_normed + jnp.concatenate([unit_n1.finish(0), unit_n1.finish(1)], axis=1)
    unit_one, scale_one = norm_parts(x_ref[...].astype(WIDE))
    s.small[0:1, :] = column_sum(d_normed * unit_one)
    s.small[1:2, :] = column_sum(d_normed)
    s.small[2:3, :] = column_sum(s.dq2[0:128, :])
    s.small[3:4, :] = column_sum(s.dkv[:, 768:1536])
    d_inputs = s.d_mid[...] + norm_back(d_normed, unit_one, scale_one, gain_one)
    s.grad[...] = d_inputs.astype(LOW)
    grad_copy = pltpu.make_async_copy(s.grad, grad_ref, local.at[7 + LINES])
    grad_copy.start()

    s.pieces[...] = jnp.zeros((8, 16, 128), WIDE)
    for j in range(8):
        s.pieces[j, 0:8, 0:96] = s.small[:, 96 * j : 96 * j + 96]
        for i in range(3):
            s.pieces[j, 8 + i : 9 + i, :] = s.wide[j : j + 1, 128 * i : 128 * i + 128]
    piece_copy = send_all(
        [(s.pieces.at[place(r)], s.pieces_got.at[r], near(r)) for r in range(1, 8)],
        s.pieces_got.at[pl.ds(1, 7)],
    )
    line_q.middle()
    line_v.back()
    line_k[0].middle()
    line_k[1].middle()
    line_k[2].middle()
    line_q.back()
    piece_copy.wait_recv()
    total = s.pieces[me]
    for r in range(1, 8):
        total = total + s.pieces_got[r]
    s.rows_z[dp] = total
    z_copy = send_all(
        [(s.rows_z.at[dp], s.rows_z.at[dp], device) for device in others_z],
        s.rows_z.at[pl.ds(0, 3)],
    )
    line_k[0].back()
    line_k[1].back()
    line_k[2].back()
    for line in line_down + [line_out] + line_up:
        line.write()
    line_v.write()
    line_q.write()
    z_copy.wait_recv()
    small_ref[...] = s.rows_z[0] + s.rows_z[1] + s.rows_z[2] + s.rows_z[3]
    for line in line_k:
        line.write()
    out_copy.wait()
    grad_copy.wait()
    for line in lines:
        line.close()
    for copy in ring:
        if copy is not None:
            copy.wait_send()


def spread_kernel(total_ref, small_ref, out_in, grad_in, out_ref, grad_ref, *outs):
    gain_one, shift_one, qkv, bias_q, bias_v, out, bias_out = outs[:7]
    gain_two, shift_two, up, bias_up, down, bias_down = outs[7:]
    out_ref[...] = out_in[...]
    grad_ref[...] = grad_in[...]
    for i in range(2):
        cols = slice(384 * i, 384 * i + 384)
        for j in range(4):
            down[96 * j : 96 * j + 96, cols] = total_ref[2 * j + i].astype(WIDE)
        out[:, cols] = total_ref[8 + i].astype(WIDE)
    for j in range(8):
        up[:, 384 * j : 384 * j + 384] = total_ref[10 + j].astype(WIDE)
    for j in range(6):
        qkv[:, 384 * j : 384 * j + 384] = total_ref[18 + j].astype(WIDE)
    rows = (gain_one, shift_one, bias_q, bias_v, bias_out, gain_two, shift_two, bias_down)
    for j, target in enumerate(rows):
        target[...] = small_ref[j, 0:96]
    for i in range(3):
        bias_up[128 * i : 128 * i + 128] = small_ref[8 + i, :]


def fused_device(
    inputs,
    gain_one,
    shift_one,
    w_qkv,
    bias_q,
    bias_v,
    w_out,
    bias_out,
    gain_two,
    shift_two,
    w_up,
    bias_up,
    w_down,
    bias_down,
    lengths,
    cotangent,
):
    vmem = pl.BlockSpec(memory_space=pltpu.VMEM)
    anywhere = pl.BlockSpec(memory_space=pl.ANY)
    vectors = [gain_one, shift_one, bias_q, bias_v, bias_out, gain_two, shift_two]
    vectors = vectors + [bias_up, bias_down]
    tokens, width = inputs.shape
    layer_out, grad_inputs, total, small = pl.pallas_call(
        layer_kernel,
        out_shape=(
            jax.ShapeDtypeStruct((tokens, width), LOW),
            jax.ShapeDtypeStruct((tokens, width), LOW),
            jax.ShapeDtypeStruct((24, 96, 384), LOW),
            jax.ShapeDtypeStruct((16, 128), WIDE),
        ),
        in_specs=[pl.BlockSpec(memory_space=pltpu.SMEM)] + [vmem] * 11 + [anywhere] * 4,
        out_specs=(anywhere, anywhere, anywhere, vmem),
        scratch_shapes=[pltpu.VMEM(shape, kind) for shape, kind in SCRATCH.values()]
        + [
            pltpu.SemaphoreType.DMA((RING + LINES,)),
            pltpu.SemaphoreType.DMA((LANDINGS,)),
            pltpu.SemaphoreType.DMA((8 + LINES,)),
        ],
        compiler_params=pltpu.CompilerParams(
            collective_id=0, has_side_effects=True, vmem_limit_bytes=VMEM_BYTES
        ),
        name="layer",
    )(lengths, inputs, cotangent, *vectors, w_qkv, w_out, w_up, w_down.reshape(32, 96, width))
    return pl.pallas_call(
        spread_kernel,
        out_shape=tuple(
            jax.ShapeDtypeStruct((tokens, width), LOW) for _ in range(2)
        )
        + tuple(
            jax.ShapeDtypeStruct(shape, WIDE)
            for shape in (
                (96,),
                (96,),
                (96, 2304),
                (96,),
                (96,),
                (96, 768),
                (96,),
                (96,),
                (96,),
                (96, 3072),
                (384,),
                (384, 768),
                (96,),
            )
        ),
        in_specs=[vmem] * 4,
        out_specs=(vmem,) * 15,
        compiler_params=pltpu.CompilerParams(vmem_limit_bytes=VMEM_BYTES),
        name="spread",
    )(total, small, layer_out, grad_inputs)


def per_device(*arguments):
    inputs, w_up = arguments[0], arguments[10]
    fits = (
        lax.axis_size("dp") == 4
        and lax.axis_size("col") == 8
        and inputs.shape == (128, 768)
        and w_up.shape == (768, 3072)
    )
    return fused_device(*arguments) if fits else general_device(*arguments)


def solution(mesh):
    return jax.shard_map(
        per_device,
        mesh=mesh,
        in_specs=(
            P(("dp", "col"), None),
            P(),
            P(),
            P(),
            P(),
            P(),
            P(),
            P(),
            P(),
            P(),
            P(),
            P(),
            P(),
            P(),
            P("dp", None),
            P(("dp", "col"), None),
        ),
        out_specs=(
            P(("dp", "col"), None),
            P(("dp", "col"), None),
            P("col"),
            P("col"),
            P("col", None),
            P("col"),
            P("col"),
            P("col", None),
            P("col"),
            P("col"),
            P("col"),
            P("col", None),
            P("col"),
            P("col", None),
            P("col"),
        ),
        check_vma=False,
    )
```

```python
import functools
import types

import jax
import jax.numpy as jnp
from jax import lax
from jax.experimental import pallas as pl
from jax.experimental.pallas import tpu as pltpu
from jax.sharding import PartitionSpec as P

H = 12
HEAD = 64


epsilon = 1e-05


def layer_norm(values, scales, offset):
    average = jnp.mean(values, axis=-1, keepdims=True)
    centered = values - average
    spread = jnp.mean(centered * centered, axis=-1, keepdims=True)
    return centered * lax.rsqrt(spread + epsilon) * scales + offset


def documents(places, row_lengths):
    finish = jnp.cumsum(row_lengths)
    begins = finish - row_lengths
    inside = (places[:, None] >= begins[None, :]) & (places[:, None] < finish[None, :])
    numbers = jnp.arange(row_lengths.shape[0], dtype=jnp.int32)
    doc_index = jnp.sum(jnp.where(inside, numbers[None, :], 0), axis=1)
    first_place = jnp.sum(jnp.where(inside, begins[None, :], 0), axis=1)
    return (doc_index, first_place == places)


def general_device(
    inputs,
    gain_one,
    shift_one,
    w_qkv,
    bias_q,
    bias_v,
    w_out,
    bias_out,
    gain_two,
    shift_two,
    w_up,
    bias_up,
    w_down,
    bias_down,
    lengths,
    cotangent,
):
    col_count = lax.axis_size("col")
    col_place = lax.axis_index("col")
    tok_rows = inputs.shape[0]
    model_width = inputs.shape[1]
    row_len = tok_rows * col_count
    block_rows = min(512, row_len)
    block_count = row_len // block_rows
    places = jnp.arange(row_len, dtype=jnp.int32)
    doc_index, first_flag = documents(places, lengths[0])
    own_first = col_place * tok_rows
    key_places = own_first + jnp.arange(tok_rows, dtype=jnp.int32)
    key_doc = lax.dynamic_slice_in_dim(doc_index, own_first, tok_rows, 0)
    key_first = lax.dynamic_slice_in_dim(first_flag, own_first, tok_rows, 0)
    floated = inputs.astype(jnp.float32)
    norm_first, first_back = jax.vjp(layer_norm, floated, gain_one, shift_one)
    normed_one = norm_first.astype(jnp.bfloat16)
    joined = jnp.dot(normed_one, w_qkv, preferred_element_type=jnp.float32)
    queries = (joined[:, :model_width] + bias_q).astype(jnp.bfloat16)
    key_rows = joined[:, model_width : 2 * model_width].astype(jnp.bfloat16)
    value_rows = (joined[:, 2 * model_width :] + bias_v).astype(jnp.bfloat16)
    key_heads = key_rows.reshape(tok_rows, H, HEAD)
    value_heads = value_rows.reshape(tok_rows, H, HEAD)
    all_queries = lax.all_gather(queries, "col", axis=0, tiled=True)

    def block_terms(source, block_index, carried):
        first_row = block_index * block_rows
        q_block = lax.dynamic_slice_in_dim(source, first_row, block_rows, 0).reshape(
            block_rows, H, HEAD
        )
        q_places = first_row + jnp.arange(block_rows, dtype=jnp.int32)
        q_doc = lax.dynamic_slice_in_dim(doc_index, first_row, block_rows, 0)
        scores = (
            jnp.einsum("khd,qhd->hkq", key_heads, q_block, preferred_element_type=jnp.float32)
            * 0.125
        )
        allowed = (key_places[:, None] <= q_places[None, :]) & (key_doc[:, None] == q_doc[None, :])
        chosen = (
            allowed
            & (key_places[:, None] < q_places[None, :])
            & jnp.logical_not(key_first)[:, None]
        )
        picked = jnp.where(chosen, jax.nn.softplus(scores[0]), 0.0) / row_len
        forgot = carried[:, None] + jnp.cumsum(picked, axis=1) - picked
        logits = jnp.where(allowed[None], scores - forgot[None], -jnp.inf)
        return (q_block, scores, chosen, picked, logits)

    def forward_block(carried, block_index):
        q_block, scores, chosen, picked, logits = block_terms(all_queries, block_index, carried)
        row_top = jnp.max(logits, axis=1)
        safe_top = jnp.where(row_top > -jnp.inf, row_top, 0.0)
        raised = jnp.exp(logits - safe_top[:, None, :])
        totals = jnp.sum(raised, axis=1)
        numerator = jnp.einsum(
            "hkq,khd->qhd",
            raised.astype(jnp.bfloat16),
            value_heads,
            preferred_element_type=jnp.float32,
        )
        return (
            carried + jnp.sum(picked, axis=1),
            (carried, row_top.T, totals.T, numerator.reshape(block_rows, model_width)),
        )

    indices = jnp.arange(block_count, dtype=jnp.int32)
    unused, (block_starts, row_tops, row_totals, numerators) = lax.scan(
        forward_block, jnp.zeros((tok_rows,), jnp.float32), indices
    )
    row_tops = row_tops.reshape(row_len, H)
    row_totals = row_totals.reshape(row_len, H)
    numerators = numerators.reshape(row_len, model_width)
    got_top, got_total, got_numer = (
        lax.all_to_all(
            row_tops[None].astype(jnp.bfloat16), "col", split_axis=1, concat_axis=0, tiled=True
        ).astype(jnp.float32),
        lax.all_to_all(
            row_totals[None].astype(jnp.bfloat16), "col", split_axis=1, concat_axis=0, tiled=True
        ).astype(jnp.float32),
        lax.all_to_all(
            numerators[None].astype(jnp.bfloat16), "col", split_axis=1, concat_axis=0, tiled=True
        ).astype(jnp.float32),
    )
    row_best = jnp.max(got_top, axis=0)
    factor = jnp.exp(got_top - row_best[None])
    totals_own = jnp.sum(factor * got_total, axis=0)
    numer_own = jnp.sum(got_numer.reshape(col_count, tok_rows, H, HEAD) * factor[..., None], axis=0)
    attended = (numer_own / totals_own[..., None]).reshape(tok_rows, model_width)
    row_lse = row_best + jnp.log(totals_own)
    attended_low = attended.astype(jnp.bfloat16)
    middle = floated + jnp.dot(attended_low, w_out, preferred_element_type=jnp.float32) + bias_out
    norm_second, second_back = jax.vjp(layer_norm, middle, gain_two, shift_two)
    normed_two = norm_second.astype(jnp.bfloat16)
    hidden = jnp.dot(normed_two, w_up, preferred_element_type=jnp.float32) + bias_up
    active_full, gelu_back = jax.vjp(jax.nn.gelu, hidden)
    active = active_full.astype(jnp.bfloat16)
    layer_out = (
        middle + jnp.dot(active, w_down, preferred_element_type=jnp.float32) + bias_down
    ).astype(jnp.bfloat16)
    d_output = cotangent.astype(jnp.float32)
    grad_w_down = jnp.einsum("tf,td->fd", active, cotangent, preferred_element_type=jnp.float32)
    grad_bias_down = jnp.sum(d_output, axis=0)
    d_active = jnp.einsum("td,fd->tf", cotangent, w_down, preferred_element_type=jnp.float32)
    d_hidden = gelu_back(d_active)[0].astype(jnp.bfloat16)
    grad_w_up = jnp.einsum("td,tf->df", normed_two, d_hidden, preferred_element_type=jnp.float32)
    grad_bias_up = jnp.sum(d_hidden.astype(jnp.float32), axis=0)
    d_normed_two = jnp.einsum("tf,df->td", d_hidden, w_up, preferred_element_type=jnp.float32)
    d_middle_norm, grad_gain_two, grad_shift_two = second_back(d_normed_two)
    d_middle = d_output + d_middle_norm
    d_branch = d_middle.astype(jnp.bfloat16)
    grad_w_out = jnp.einsum("td,te->de", attended_low, d_branch, preferred_element_type=jnp.float32)
    grad_bias_out = jnp.sum(d_middle, axis=0)
    d_attended = jnp.einsum(
        "te,de->td", d_branch, w_out, preferred_element_type=jnp.float32
    ).astype(jnp.bfloat16)
    row_delta = jnp.sum(
        (d_attended.astype(jnp.float32) * attended).reshape(tok_rows, H, HEAD), axis=2
    )
    back_queries, gathered_grad = (
        lax.all_gather(queries, "col", axis=0, tiled=True),
        lax.all_gather(d_attended, "col", axis=0, tiled=True),
    )
    all_lse, all_delta = (
        lax.all_gather(row_lse, "col", axis=0, tiled=True),
        lax.all_gather(row_delta, "col", axis=0, tiled=True),
    )

    def backward_block(carried_state, inputs_block):
        later_sum, key_grad, value_grad = carried_state
        block_index, carried = inputs_block
        q_block, scores, chosen, picked, logits = block_terms(back_queries, block_index, carried)
        first_row = block_index * block_rows
        grad_block = lax.dynamic_slice_in_dim(gathered_grad, first_row, block_rows, 0).reshape(
            block_rows, H, HEAD
        )
        lse_block = lax.dynamic_slice_in_dim(all_lse, first_row, block_rows, 0)
        delta_block = lax.dynamic_slice_in_dim(all_delta, first_row, block_rows, 0)
        weights = jnp.exp(logits - lse_block.T[:, None, :])
        value_grad = value_grad + jnp.einsum(
            "hkq,qhd->khd",
            weights.astype(jnp.bfloat16),
            grad_block,
            preferred_element_type=jnp.float32,
        )
        d_weights = jnp.einsum(
            "khd,qhd->hkq", value_heads, grad_block, preferred_element_type=jnp.float32
        )
        d_logits = weights * (d_weights - delta_block.T[:, None, :])
        d_forgot = -jnp.sum(d_logits, axis=0)
        block_sum = jnp.sum(d_forgot, axis=1)
        d_picked = later_sum[:, None] + block_sum[:, None] - jnp.cumsum(d_forgot, axis=1)
        d_select = jnp.where(chosen, jax.nn.sigmoid(scores[0]) * d_picked / row_len, 0.0)
        d_scores = d_logits.at[0].add(d_select).astype(jnp.bfloat16)
        key_grad = (
            key_grad
            + jnp.einsum("hkq,qhd->khd", d_scores, q_block, preferred_element_type=jnp.float32)
            * 0.125
        )
        query_grad = (
            jnp.einsum("hkq,khd->qhd", d_scores, key_heads, preferred_element_type=jnp.float32)
            * 0.125
        )
        return (
            (later_sum + block_sum, key_grad, value_grad),
            query_grad.reshape(block_rows, model_width),
        )

    zero_heads = jnp.zeros((tok_rows, H, HEAD), jnp.float32)
    initial = (jnp.zeros((tok_rows,), jnp.float32), zero_heads, zero_heads)
    (unused_sum, key_grad, value_grad), query_parts = lax.scan(
        backward_block, initial, (indices, block_starts), reverse=True
    )
    query_parts = query_parts.reshape(row_len, model_width)
    d_queries = lax.psum_scatter(query_parts, "col", scatter_dimension=0, tiled=True).astype(
        jnp.bfloat16
    )
    d_keys = key_grad.reshape(tok_rows, model_width).astype(jnp.bfloat16)
    d_values = value_grad.reshape(tok_rows, model_width).astype(jnp.bfloat16)
    d_joined = jnp.concatenate([d_queries, d_keys, d_values], axis=1)
    grad_w_qkv = jnp.einsum("td,te->de", normed_one, d_joined, preferred_element_type=jnp.float32)
    grad_bias_q = jnp.sum(d_queries.astype(jnp.float32), axis=0)
    grad_bias_v = jnp.sum(d_values.astype(jnp.float32), axis=0)
    d_normed_one = jnp.einsum("te,de->td", d_joined, w_qkv, preferred_element_type=jnp.float32)
    d_input_norm, grad_gain_one, grad_shift_one = first_back(d_normed_one)
    grad_inputs = (d_middle + d_input_norm).astype(jnp.bfloat16)
    (
        shard_gain_one,
        shard_shift_one,
        shard_w_qkv,
        shard_bias_q,
        shard_bias_v,
        shard_w_out,
        shard_bias_out,
        shard_gain_two,
        shard_shift_two,
        shard_w_up,
        shard_bias_up,
        shard_w_down,
        shard_bias_down,
    ) = (
        lax.psum_scatter(grad_gain_one, "col", scatter_dimension=0, tiled=True),
        lax.psum_scatter(grad_shift_one, "col", scatter_dimension=0, tiled=True),
        lax.psum_scatter(grad_w_qkv, "col", scatter_dimension=0, tiled=True),
        lax.psum_scatter(grad_bias_q, "col", scatter_dimension=0, tiled=True),
        lax.psum_scatter(grad_bias_v, "col", scatter_dimension=0, tiled=True),
        lax.psum_scatter(grad_w_out, "col", scatter_dimension=0, tiled=True),
        lax.psum_scatter(grad_bias_out, "col", scatter_dimension=0, tiled=True),
        lax.psum_scatter(grad_gain_two, "col", scatter_dimension=0, tiled=True),
        lax.psum_scatter(grad_shift_two, "col", scatter_dimension=0, tiled=True),
        lax.psum_scatter(grad_w_up, "col", scatter_dimension=0, tiled=True),
        lax.psum_scatter(grad_bias_up, "col", scatter_dimension=0, tiled=True),
        lax.psum_scatter(grad_w_down, "col", scatter_dimension=0, tiled=True),
        lax.psum_scatter(grad_bias_down, "col", scatter_dimension=0, tiled=True),
    )
    summed = (
        lax.psum(shard_gain_one.astype(jnp.bfloat16), "dp").astype(jnp.float32),
        lax.psum(shard_shift_one.astype(jnp.bfloat16), "dp").astype(jnp.float32),
        lax.psum(shard_w_qkv.astype(jnp.bfloat16), "dp").astype(jnp.float32),
        lax.psum(shard_bias_q.astype(jnp.bfloat16), "dp").astype(jnp.float32),
        lax.psum(shard_bias_v.astype(jnp.bfloat16), "dp").astype(jnp.float32),
        lax.psum(shard_w_out.astype(jnp.bfloat16), "dp").astype(jnp.float32),
        lax.psum(shard_bias_out.astype(jnp.bfloat16), "dp").astype(jnp.float32),
        lax.psum(shard_gain_two.astype(jnp.bfloat16), "dp").astype(jnp.float32),
        lax.psum(shard_shift_two.astype(jnp.bfloat16), "dp").astype(jnp.float32),
        lax.psum(shard_w_up.astype(jnp.bfloat16), "dp").astype(jnp.float32),
        lax.psum(shard_bias_up.astype(jnp.bfloat16), "dp").astype(jnp.float32),
        lax.psum(shard_w_down.astype(jnp.bfloat16), "dp").astype(jnp.float32),
        lax.psum(shard_bias_down.astype(jnp.bfloat16), "dp").astype(jnp.float32),
    )
    return (
        layer_out,
        grad_inputs,
        summed[0],
        summed[1],
        summed[2],
        summed[3],
        summed[4],
        summed[5],
        summed[6],
        summed[7],
        summed[8],
        summed[9],
        summed[10],
        summed[11],
        summed[12],
    )


MESH = pl.DeviceIdType.MESH
LOW = jnp.bfloat16
WIDE = jnp.float32
FAR = 1e30
VMEM_BYTES = 63 * 2**20


def dot(a, b):
    return jnp.dot(a, b, preferred_element_type=WIDE)


def dot_rows(a, b):
    return lax.dot_general(a, b, (((1,), (1,)), ((), ())), preferred_element_type=WIDE)


def split_low(values):
    high = values.astype(LOW)
    return high, (values - high.astype(WIDE)).astype(LOW)


def column_sum(values):
    return jnp.sum(values.astype(WIDE), axis=0, keepdims=True)


def norm_parts(values):
    average = jnp.mean(values, axis=-1, keepdims=True)
    centered = values - average
    spread = jnp.mean(centered * centered, axis=-1, keepdims=True)
    scale = lax.rsqrt(spread + epsilon)
    return centered * scale, scale


def norm_back(grad, unit, scale, gain):
    scaled = grad * gain
    first = jnp.mean(scaled, axis=-1, keepdims=True)
    second = jnp.mean(scaled * unit, axis=-1, keepdims=True)
    return scale * (scaled - first - unit * second)


def gelu_parts(hidden):
    square = hidden * hidden
    bend = jnp.tanh(0.7978845608028654 * hidden * (1.0 + 0.044715 * square))
    half = 0.5 * (1.0 + bend)
    curve = 0.7978845608028654 * (1.0 + 3 * 0.044715 * square)
    return hidden * half, half + 0.5 * hidden * (1.0 - bend * bend) * curve


SCRATCH = dict(
    wqkv=((768, 2304), LOW),
    wout=((768, 768), LOW),
    wup=((768, 3072), LOW),
    wdown=((32, 96, 768), LOW),
    wup_own=((768, 384), LOW),
    n1=((8, 128, 768), LOW),
    n1_t=((8, 96, 1024), LOW),
    n2=((8, 128, 768), LOW),
    n2_t=((8, 96, 1024), LOW),
    cot=((8, 128, 768), LOW),
    keys=((1024, 768), LOW),
    values=((1024, 768), LOW),
    turned=((6, 128, 1024), LOW),
    probs=((6, 1024, 256), LOW),
    sums=((8, 8, 128), WIDE),
    back_sums=((8, 8, 128), WIDE),
    forgot=((128, 1024), WIDE),
    forgot_t=((1024, 128), WIDE),
    sig=((128, 1024), WIDE),
    d_forgot_t=((1024, 128), WIDE),
    second_head=((1024, 128), LOW),
    q_low=((128, 768), LOW),
    q_turned=((768, 128), LOW),
    att_t=((768, 128), WIDE),
    att_low_t=((8, 96, 128), LOW),
    act=((128, 3072), LOW),
    d_act=((128, 3072), WIDE),
    d_hidden=((128, 3072), LOW),
    middle=((128, 768), WIDE),
    d_mid=((128, 768), WIDE),
    unit_two=((128, 768), WIDE),
    d_att=((128, 768), LOW),
    d_att_t=((768, 128), LOW),
    dq_t=((768, 128), WIDE),
    act_t=((384, 1024), LOW),
    slope=((1024, 384), LOW),
    db2=((256, 768), LOW),
    dq2=((256, 768), LOW),
    lhs_out=((4, 96, 256), LOW),
    lhs_q=((4, 96, 256), LOW),
    give_out=((4, 96, 128), LOW),
    give_q=((4, 96, 128), LOW),
    dkv=((1024, 1536), LOW),
    grads_out=((4, 96, 768), LOW),
    grads_q=((4, 96, 768), LOW),
    grads_k=((2, 4, 96, 768), LOW),
    grads_v=((2, 4, 96, 768), LOW),
    core_k=((4, 96, 768), LOW),
    core_v=((4, 96, 768), LOW),
    one=((4, 2, 2, 96, 384), LOW),
    two=((4, 2, 96, 384), LOW),
    d_n1=((2, 4, 128, 768), LOW),
    core_n1=((4, 128, 768), LOW),
    one_n1=((2, 2, 128, 384), LOW),
    two_n1=((2, 128, 384), LOW),
    up_give=((8, 96, 384), LOW),
    mine=((24, 96, 384), LOW),
    got_z=((24, 96, 384), LOW),
    got_mid=((24, 96, 384), LOW),
    total=((24, 96, 384), LOW),
    small=((8, 768), WIDE),
    wide=((8, 384), WIDE),
    pieces=((8, 16, 128), WIDE),
    pieces_got=((8, 16, 128), WIDE),
    rows_z=((4, 16, 128), WIDE),
    out=((128, 768), LOW),
    grad=((128, 768), LOW),
)
SLOTS = (0, 2, 6, 4)
RING = 24
LINES = 15
LANDINGS = 78


def layer_kernel(
    lengths_ref,
    x_ref,
    cot_ref,
    gain_one,
    shift_one,
    bias_q,
    bias_v,
    bias_out,
    gain_two,
    shift_two,
    bias_up,
    bias_down,
    w_qkv,
    w_out,
    w_up,
    w_down,
    out_ref,
    grad_ref,
    total_ref,
    small_ref,
    *scratch,
):
    s = types.SimpleNamespace(**dict(zip(SCRATCH, scratch)))
    gain_one, shift_one, bias_q, bias_v, bias_out, gain_two, shift_two, bias_up, bias_down = (
        ref[...].reshape(1, -1)
        for ref in (
            gain_one,
            shift_one,
            bias_q,
            bias_v,
            bias_out,
            gain_two,
            shift_two,
            bias_up,
            bias_down,
        )
    )
    sent, landed, local = scratch[len(SCRATCH) :]
    me = lax.axis_index("col")
    dp = lax.axis_index("dp")
    core = lax.rem(me, 2)
    x_bit = lax.rem(lax.div(me, 2), 2)
    y_bit = lax.div(me, 4)

    def place(r):
        step = (r & 1) * (1 - 2 * core) + ((r >> 1) & 1) * (2 - 4 * x_bit)
        return me + step + (r >> 2) * (4 - 8 * y_bit)

    def near(r):
        return (dp, place(r))

    z_pair = (dp + 1 - 2 * lax.rem(dp, 2), me)
    z_middle = (3 - dp, me)
    inner = (dp == 1) | (dp == 2)
    outer = jnp.logical_not(inner)
    barrier = pltpu.get_barrier_semaphore()
    others_z = [(lax.rem(dp + k, 4), me) for k in (1, 2, 3)]
    for device in [near(r) for r in range(1, 8)] + others_z:
        pl.semaphore_signal(barrier, inc=1, device_id=device, device_id_type=MESH)

    landings = iter(range(LANDINGS))
    ring = [None] * RING
    turns = iter(range(10**6))

    def message(source, target, device, send_at, land_at):
        return pltpu.make_async_remote_copy(
            src_ref=source,
            dst_ref=target,
            send_sem=sent.at[send_at],
            recv_sem=landed.at[land_at],
            device_id=device,
            device_id_type=MESH,
        )

    def send_all(copies, whole):
        send_at, land_at = next(turns) % RING, next(landings)
        if ring[send_at] is not None:
            ring[send_at].wait_send()
        for source, target, device in copies:
            message(source, target, device, send_at, land_at).start()
        ring[send_at] = message(whole, whole, near(1), send_at, land_at)
        return ring[send_at]

    def send(source, target, device):
        return send_all([(source, target, device)], source)

    loads = {}
    own_cols = pl.ds(pl.multiple_of(384 * me, 128), 384)
    for at, (name, source, target) in enumerate(
        (
            ("kv", w_qkv.at[:, pl.ds(768, 1536)], s.wqkv.at[:, pl.ds(768, 1536)]),
            ("q", w_qkv.at[:, pl.ds(0, 768)], s.wqkv.at[:, pl.ds(0, 768)]),
            ("down", w_down, s.wdown),
            ("out", w_out, s.wout),
            ("up", w_up, s.wup),
            ("own", w_up.at[:, own_cols], s.wup_own),
        )
    ):
        loads[name] = pltpu.make_async_copy(source, target, local.at[at])
        loads[name].start()

    class Gather:
        def __init__(self, ref):
            self.ref = ref
            self.left, self.right = pl.ds(0, 384), pl.ds(384, 384)

        def start(self):
            ref, own = self.ref, self.ref.at[0]
            pair = []
            for first, second in ((self.left, self.right), (self.right, self.left)):
                copies = [
                    (own.at[:, first], ref.at[2, :, first], near(2)),
                    (own.at[:, second], ref.at[4, :, second], near(4)),
                ]
                pair.append(send_all(copies, own))
            self.early, self.late = pair
            self.other = send(own, ref.at[1], near(1))

        def forward(self):
            ref = self.ref
            self.early.wait_recv()
            copies = [
                (ref.at[2, :, self.left], ref.at[6, :, self.left], near(4)),
                (ref.at[4, :, self.right], ref.at[6, :, self.right], near(2)),
            ]
            self.far = send_all(copies, ref.at[6])

        def to_core(self):
            ref = self.ref
            self.late.wait_recv()
            self.more = [send(ref.at[r], ref.at[r + 1], near(1)) for r in (2, 4)]

        def diagonal(self):
            self.far.wait_recv()
            self.more.append(send(self.ref.at[6], self.ref.at[7], near(1)))

        def chip(self, number):
            (self.other if number == 0 else self.more[number - 1]).wait_recv()

        def rows(self, number):
            return self.ref[2 * number : 2 * number + 2].reshape(256, 768)

    values_one = x_ref[...].astype(WIDE)
    unit_one, scale_one = norm_parts(values_one)
    normed_one = (unit_one * gain_one + shift_one).astype(LOW)
    s.n1[0] = normed_one
    s.cot[0] = cot_ref[...]
    gather_one, gather_cot, gather_two = Gather(s.n1), Gather(s.cot), Gather(s.n2)
    pl.semaphore_wait(barrier, 10)
    gather_one.start()

    def share(source, lhs, give):
        for slot, r in enumerate(SLOTS):
            ours = place(r)
            lhs[slot, :, 0:128] = source(ours)
            give[slot] = source(ours + 1 - 2 * core)
        return send(give, lhs.at[:, :, pl.ds(128, 128)], near(1))

    def turn_block(source, target, r):
        target[:, :, 128 * r : 128 * r + 128] = source[r].T.reshape(8, 96, 128)

    def form_keys(number):
        at = 256 * number
        s.keys[at : at + 256, :] = dot(gather_one.rows(number), s.wqkv[:, 768:1536]).astype(LOW)

    def form_values(number):
        at = 256 * number
        rows = dot(gather_one.rows(number), s.wqkv[:, 1536:2304]) + bias_v
        s.values[at : at + 256, :] = rows.astype(LOW)

    def active_grad(first, last):
        for j in range(first, last):
            rows = s.wdown[4 * j : 4 * j + 4].reshape(384, 768)
            s.d_act[:, 384 * j : 384 * j + 384] = dot_rows(cot_ref[...], rows)

    loads["kv"].wait()
    gather_one.chip(0)
    form_keys(0)
    form_values(0)
    loads["q"].wait()
    q = (dot(normed_one, s.wqkv[:, 0:768]) + bias_q).astype(LOW)
    q = (q.astype(WIDE) * 0.125).astype(LOW)
    s.q_low[...] = q
    row_at = lax.broadcasted_iota(jnp.int32, (128, 128), 0)
    lane_at = lax.broadcasted_iota(jnp.int32, (128, 128), 1)
    query_at = row_at + me * 128
    begin_one = lengths_ref[0, 0]
    begin_two = begin_one + lengths_ref[0, 1]
    begin_three = begin_two + lengths_ref[0, 2]
    begin = jnp.where(query_at >= begin_one, begin_one, 0)
    begin = jnp.where(query_at >= begin_two, begin_two, begin)
    begin = jnp.where(query_at >= begin_three, begin_three, begin)
    earlier = jnp.where(lane_at < row_at, 1.0, 0.0).astype(LOW)
    first_lanes = jnp.where(lane_at < 64, 1.0, 0.0)
    head_zero = (s.q_low[:, 0:128].astype(WIDE) * first_lanes).astype(LOW)

    def picks(number):
        at = 256 * number
        scores = dot_rows(head_zero, s.keys[at : at + 256, 0:128])
        key_at = jnp.concatenate(
            [lane_at + place(r) * 128 for r in (2 * number, 2 * number + 1)], axis=1
        )
        queries_at = jnp.concatenate([query_at, query_at], axis=1)
        begins = jnp.concatenate([begin, begin], axis=1)
        allowed = (key_at <= queries_at) & (key_at >= begins)
        chosen = (key_at < queries_at) & (key_at > begins)
        small_exp = jnp.exp(-jnp.abs(scores))
        soft = jnp.maximum(scores, 0.0) + jnp.log1p(small_exp)
        picked = jnp.where(chosen, soft, 0.0) * (1.0 / 1024)
        high, rest = split_low(picked)
        sums = column_sum(picked)
        s.sums[0, 2 * number : 2 * number + 1, :] = sums[:, 0:128]
        s.sums[0, 2 * number + 1 : 2 * number + 2, :] = sums[:, 128:256]
        within = dot(earlier, high) + dot(earlier, rest)
        s.forgot[:, at : at + 256] = jnp.where(allowed, within, FAR)
        sigmoid = jnp.where(scores >= 0, 1.0, small_exp) / (1.0 + small_exp)
        s.sig[:, at : at + 256] = jnp.where(chosen, sigmoid, 0.0) * (1.0 / 1024)

    def turn(source, pair):
        at = 128 * pair
        for r in range(8):
            rows = slice(128 * r, 128 * r + 128)
            s.turned[pair, :, rows] = source[rows, at : at + 128].T

    picks(0)
    turn_block(s.n1, s.n1_t, 0)
    gather_one.forward()
    s.q_turned[...] = q.T
    loads["down"].wait()
    active_grad(0, 6)
    gather_one.to_core()
    active_grad(6, 8)

    gather_one.diagonal()
    for number in (1, 2, 3):
        gather_one.chip(number)
        form_keys(number)
        picks(number)
    sum_copy = send_all(
        [(s.sums.at[0], s.sums.at[r], near(r)) for r in range(1, 8)], s.sums.at[pl.ds(1, 7)]
    )
    gather_cot.start()
    for number in (1, 2, 3):
        form_values(number)
    for pair in range(6):
        turn(s.values, pair)
    share_one = share(lambda at: s.n1_t[at, :, 0:128], s.lhs_q, s.give_q)
    sum_copy.wait_recv()

    def others(sums, later):
        rows = [jnp.zeros((1, 128), WIDE) for _ in range(8)]
        for d in range(1, 8):
            ahead = place(d) > me if later else place(d) < me
            weight = jnp.where(ahead, 1.0, 0.0)
            for r in range(8):
                rows[r] = rows[r] + weight * sums[d, (r ^ d) : (r ^ d) + 1, :]
        return rows

    for r, row in enumerate(others(s.sums, False)):
        at = 128 * r
        s.forgot_t[at : at + 128, :] = (s.forgot[:, at : at + 128] + row).T

    feature_at = lax.broadcasted_iota(jnp.int32, (128, 256), 0)
    column_at = lax.broadcasted_iota(jnp.int32, (128, 256), 1)
    own_head_t = jnp.where((feature_at < 64) == (column_at < 128), 1.0, 0.0).astype(LOW)
    long_row = lax.broadcasted_iota(jnp.int32, (256, 128), 0)
    long_lane = lax.broadcasted_iota(jnp.int32, (256, 128), 1)
    own_head = jnp.where((long_row < 128) == (long_lane < 64), 1.0, 0.0).astype(LOW)

    def both_t(values):
        return jnp.concatenate([values, values], axis=1) * own_head_t

    def both(values):
        return jnp.concatenate([values, values], axis=0) * own_head

    def attend(pair):
        at = 128 * pair
        scores = dot(s.keys[:, at : at + 128], both_t(s.q_turned[at : at + 128, :]))
        forgot = s.forgot_t[...]
        logits = scores - jnp.concatenate([forgot, forgot], axis=1)
        raised = jnp.exp(logits - jnp.max(logits, axis=0, keepdims=True))
        probs = (raised * (1.0 / jnp.sum(raised, axis=0, keepdims=True))).astype(LOW)
        s.probs[pair] = probs
        mixed = dot(s.turned[pair], probs)
        s.att_t[at : at + 64, :] = mixed[0:64, 0:128]
        s.att_t[at + 64 : at + 128, :] = mixed[64:128, 128:256]

    for pair in range(6):
        if pair == 2:
            gather_cot.forward()
        if pair == 4:
            gather_cot.to_core()
        attend(pair)

    attended_low_t = s.att_t[...].astype(LOW)
    s.att_low_t[...] = attended_low_t.reshape(8, 96, 128)
    loads["out"].wait()
    middle = values_one + dot(attended_low_t.T, s.wout[...]) + bias_out
    s.middle[...] = middle
    unit_two, scale_two = norm_parts(middle)
    s.unit_two[...] = unit_two
    normed_two = (unit_two * gain_two + shift_two).astype(LOW)
    s.n2[0] = normed_two
    gather_two.start()
    share_att = share(lambda at: s.att_low_t[at], s.lhs_out, s.give_out)
    gather_cot.diagonal()
    loads["up"].wait()
    for j in range(4):
        at = 768 * j
        hidden = dot(normed_two, s.wup[:, at : at + 768]) + bias_up[:, at : at + 768]
        active, slope = gelu_parts(hidden)
        s.act[:, at : at + 768] = active.astype(LOW)
        d_hidden = (s.d_act[:, at : at + 768] * slope).astype(LOW)
        s.d_hidden[:, at : at + 768] = d_hidden
        s.wide[2 * j : 2 * j + 1, :] = column_sum(d_hidden[:, 0:384])
        s.wide[2 * j + 1 : 2 * j + 2, :] = column_sum(d_hidden[:, 384:768])

    d_output = cot_ref[...].astype(WIDE)
    parts = []
    for j in range(3):
        parts.append(dot_rows(s.d_hidden[...], s.wup[256 * j : 256 * j + 256, :]))
    d_normed = jnp.concatenate(parts, axis=1)
    gather_two.forward()
    unit_two = s.unit_two[...]
    s.small[5:6, :] = column_sum(d_normed * unit_two)
    s.small[6:7, :] = column_sum(d_normed)
    s.small[7:8, :] = column_sum(d_output)
    d_middle = d_output + norm_back(d_normed, unit_two, scale_two, gain_two)
    s.d_mid[...] = d_middle
    s.small[4:5, :] = column_sum(d_middle)
    d_branch = d_middle.astype(LOW)
    s.db2[0:128, :] = d_branch
    share_branch = send(s.db2.at[pl.ds(0, 128)], s.db2.at[pl.ds(128, 128)], near(1))
    d_att_t = dot(s.wout[...], d_branch.T).astype(LOW)
    s.d_att_t[...] = d_att_t
    s.d_att[...] = d_att_t.T
    gather_two.to_core()

    class Unit:
        def __init__(self, rows, grads, one, two, core=None):
            self.rows, self.grads, self.one, self.two, self.core = rows, grads, one, two, core

        def across(self):
            self.copy = send(self.grads.at[1], self.core, near(1))
            self.grads = self.grads.at[0]

        def start(self):
            if self.core is not None:
                self.copy.wait_recv()
                total = self.grads[...].astype(WIDE) + self.core[...].astype(WIDE)
                self.grads[...] = total.astype(LOW)
            copies = [
                (self.grads.at[pl.ds(1, 2), :, pl.ds(0, 384)], self.one.at[0], near(2)),
                (self.grads.at[pl.ds(2, 2), :, pl.ds(384, 384)], self.one.at[1], near(4)),
            ]
            self.copy = send_all(copies, self.one)

        def pass_on(self):
            self.copy.wait_recv()
            copies = []
            for half, slot, index, r in ((0, 3, 1, 4), (1, 1, 0, 2)):
                cols = slice(384 * half, 384 * half + 384)
                total = self.grads[slot, :, cols].astype(WIDE)
                total = total + self.one[half, index].astype(WIDE)
                self.grads[slot, :, cols] = total.astype(LOW)
                source = self.grads.at[slot, :, pl.ds(384 * half, 384)]
                copies.append((source, self.two.at[half], near(r)))
            self.copy = send_all(copies, self.two)

        def finish(self, half):
            if half == 0:
                self.copy.wait_recv()
            total = self.grads[0, :, 384 * half : 384 * half + 384].astype(WIDE)
            total = total + self.one[half, half].astype(WIDE)
            return total + self.two[half].astype(WIDE)

    class Line:
        def __init__(self, blocks, places):
            self.blocks, self.places = blocks, places
            self.at = next(line_numbers)
            send_at = RING + self.at
            first, second = next(landings), next(landings)
            mine, total = s.mine.at[self.blocks], s.total.at[self.blocks]
            self.inward = message(mine, s.got_z.at[self.blocks], z_pair, send_at, first)
            self.across = message(mine, s.got_mid.at[self.blocks], z_middle, send_at, second)
            self.outward = message(total, total, z_pair, send_at, first)

        def start(self):
            pl.when(outer)(lambda: self.inward.start())

        def middle(self):
            @pl.when(inner)
            def _():
                blocks = self.blocks
                self.inward.wait_recv()
                total = s.mine[blocks].astype(WIDE) + s.got_z[blocks].astype(WIDE)
                s.mine[blocks] = total.astype(LOW)
                self.across.start()

        def back(self):
            @pl.when(inner)
            def _():
                blocks = self.blocks
                self.across.wait_recv()
                total = s.mine[blocks].astype(WIDE) + s.got_mid[blocks].astype(WIDE)
                s.total[blocks] = total.astype(LOW)
                self.across.wait_send()
                self.outward.start()

        def write(self):
            pl.when(outer)(lambda: self.outward.wait_recv())
            landing = local.at[6 + self.at]
            for source, target in self.places:
                pltpu.make_async_copy(
                    s.total.at[source], total_ref.at[target], landing
                ).start()
            self.written = pltpu.make_async_copy(
                s.total.at[self.blocks], total_ref.at[self.blocks], landing
            )

        def close(self):
            self.written.wait()
            pl.when(outer)(lambda: self.inward.wait_send())
            pl.when(inner)(lambda: self.outward.wait_send())

    line_numbers = iter(range(LINES))

    def plain(at, count):
        blocks = (pl.ds(at, count),)
        return Line(blocks, ((blocks, blocks),))

    def part(at, first):
        blocks = (at, pl.ds(first, 48))
        return Line(blocks, ((blocks, blocks),))

    def spread(r):
        return Line((pl.ds(10 + r, 2),), [(10 + i, 10 + place(i)) for i in (r, r + 1)])

    line_down = [plain(at, count) for at, count in ((0, 1), (1, 1), (2, 2), (4, 2), (6, 2))]
    line_out = plain(8, 2)
    line_up = [spread(2 * j) for j in range(4)]
    line_v, line_q = plain(22, 2), plain(18, 2)
    line_k = [plain(20, 1), part(21, 0), part(21, 48)]
    lines = line_down + [line_out] + line_up + [line_v, line_q] + line_k

    unit_out = Unit(96, s.grads_out, s.one.at[0], s.two.at[0])
    unit_q = Unit(96, s.grads_q, s.one.at[1], s.two.at[1])
    unit_k = Unit(96, s.grads_k, s.one.at[2], s.two.at[2], s.core_k)
    unit_v = Unit(96, s.grads_v, s.one.at[3], s.two.at[3], s.core_v)
    unit_n1 = Unit(128, s.d_n1, s.one_n1, s.two_n1, s.core_n1)

    def to_line(unit, at, *parts):
        for half in range(2):
            s.mine[at + half] = unit.finish(half).astype(LOW)
        for line in parts:
            line.start()

    def rows_of(source, odd):
        return jnp.concatenate([source[place(r + odd)] for r in SLOTS], axis=0)

    own_bias = jnp.zeros((1, 384), WIDE)
    for j in range(8):
        own_bias = own_bias + jnp.where(me == j, 1.0, 0.0) * bias_up[:, 384 * j : 384 * j + 384]
    loads["own"].wait()

    def own_units(number):
        gather_cot.chip(number)
        gather_two.chip(number)
        at = 256 * number
        hidden = dot(gather_two.rows(number), s.wup_own[...]) + own_bias
        active, slope = gelu_parts(hidden)
        d_active = dot_rows(gather_cot.rows(number), s.wdown[pl.ds(4 * me, 4)].reshape(384, 768))
        s.act_t[:, at : at + 256] = active.astype(LOW).T
        s.slope[at : at + 256, :] = (d_active * slope).astype(LOW)

    def out_unit():
        share_att.wait_recv()
        share_branch.wait_recv()
        grads = dot(s.lhs_out[...].reshape(384, 256), s.db2[...]).astype(LOW)
        s.grads_out[...] = grads.reshape(4, 96, 768)
        unit_out.start()

    def down_grads(half, parts):
        rows = s.act_t[192 * half : 192 * half + 192, :]
        grads = dot(rows, s.cot[...].reshape(1024, 768)).astype(LOW)
        for j in range(2):
            for i in range(2):
                block = grads[96 * j : 96 * j + 96, 384 * i : 384 * i + 384]
                s.mine[4 * half + 2 * j + i] = block
        for line in parts:
            line.start()

    def up_grads(odd):
        copies = []
        grads = dot(rows_of(s.n2_t, odd), s.slope[...]).astype(LOW).reshape(4, 96, 384)
        for slot, r in enumerate(SLOTS):
            if r + odd == 0:
                s.mine[10] = grads[0]
            else:
                s.up_give[r + odd] = grads[slot]
                copies.append((s.up_give.at[r + odd], s.mine.at[10 + r + odd], near(r + odd)))
        return copies, s.up_give.at[pl.ds(0, len(copies))]

    def logit_grads(pair):
        at = 128 * pair
        grad_t = s.d_att_t[at : at + 128, :]
        products = grad_t.astype(WIDE) * s.att_t[at : at + 128, :]
        delta = jnp.concatenate(
            [
                jnp.sum(products[0:64], axis=0, keepdims=True),
                jnp.sum(products[64:128], axis=0, keepdims=True),
            ],
            axis=1,
        )
        d_probs = dot(s.values[:, at : at + 128], both_t(grad_t))
        d_logits = s.probs[pair].astype(WIDE) * (d_probs - delta)
        both_heads = d_logits[:, 0:128] + d_logits[:, 128:256]
        if pair == 5:
            s.d_forgot_t[...] = both_heads
        else:
            s.d_forgot_t[...] += both_heads
        return d_logits

    def value_grads(pair):
        at = 128 * pair
        grads = dot(s.probs[pair], both(s.d_att[:, at : at + 128]))
        s.dkv[:, 768 + at : 896 + at] = grads.astype(LOW)

    def score_grads(pair, d_scores):
        at = 128 * pair
        turn(s.keys, pair)
        s.dkv[:, at : at + 128] = dot(d_scores, both(s.q_low[:, at : at + 128])).astype(LOW)
        grads = dot(s.turned[pair], d_scores)
        s.dq_t[at : at + 64, :] = grads[0:64, 0:128]
        s.dq_t[at + 64 : at + 128, :] = grads[64:128, 128:256]

    def attend_back(pair):
        d_logits = logit_grads(pair)
        value_grads(pair)
        score_grads(pair, d_logits.astype(LOW))

    def back_sums():
        d_logits = logit_grads(0)
        s.forgot_t[...] = d_logits[:, 0:128]
        s.second_head[...] = d_logits[:, 128:256].astype(LOW)
        for r in range(8):
            turned = s.d_forgot_t[128 * r : 128 * r + 128, :].T
            s.back_sums[0, r : r + 1, :] = column_sum(turned)
        return send_all(
            [(s.back_sums.at[0], s.back_sums.at[r], near(r)) for r in range(1, 8)],
            s.back_sums.at[pl.ds(1, 7)],
        )

    def key_unit(unit, half, odd):
        grads = s.dkv[:, 768 * half : 768 * half + 768]
        rows = rows_of(s.n1_t, odd)
        unit.grads[odd] = dot(rows, grads).astype(LOW).reshape(4, 96, 768)

    def first_pair():
        later_rows = others(s.back_sums, True)
        following = jnp.where(row_at > lane_at, 1.0, 0.0).astype(LOW)
        selected = []
        for r in range(8):
            at = 128 * r
            high, rest = split_low(s.d_forgot_t[at : at + 128, :])
            later = jnp.broadcast_to(later_rows[r], (128, 128)).T
            d_picked = -(dot(high, following) + dot(rest, following) + later)
            selected.append(s.forgot_t[at : at + 128, :] + s.sig[:, at : at + 128].T * d_picked)
        first_head = jnp.concatenate(selected, axis=0).astype(LOW)
        score_grads(0, jnp.concatenate([first_head, s.second_head[...]], axis=1))
        for j in range(6):
            at = 128 * j
            d_q = (s.dq_t[at : at + 128, :] * 0.125).astype(LOW)
            s.dq2[0:128, at : at + 128] = d_q.T
        return send(s.dq2.at[pl.ds(0, 128)], s.dq2.at[pl.ds(128, 128)], near(1))

    def query_unit():
        grads = dot(s.lhs_q[...].reshape(384, 256), s.dq2[...]).astype(LOW)
        s.grads_q[...] = grads.reshape(4, 96, 768)
        unit_q.start()

    def normed_part(j):
        cols = slice(256 * j, 256 * j + 256)
        grads = dot_rows(s.dkv[...], s.wqkv[cols, 768:2304]).astype(LOW)
        for slot, r in enumerate(SLOTS):
            for odd in range(2):
                at = 128 * (r + odd)
                s.d_n1[odd, slot, :, cols] = grads[at : at + 128]

    own_units(0)
    own_units(1)
    own_units(2)
    gather_two.diagonal()
    out_unit()
    own_units(3)
    down_grads(0, line_down[0:3])
    down_grads(1, line_down[3:5])
    for r in range(8):
        turn_block(s.n2, s.n2_t, r)
        if r:
            turn_block(s.n1, s.n1_t, r)
    up_odd = send_all(*up_grads(1))
    up_even = up_grads(0)
    attend_back(5)
    attend_back(4)
    unit_out.pass_on()
    line_down[0].middle()
    attend_back(3)
    attend_back(2)
    line_down[1].middle()
    attend_back(1)
    sum_copy = back_sums()
    up_even = send_all(*up_even)
    line_down[0].back()
    value_grads(0)
    key_unit(unit_v, 1, 1)
    line_down[2].middle()
    key_unit(unit_v, 1, 0)
    unit_v.across()
    line_down[1].back()
    to_line(unit_out, 8, line_out)
    sum_copy.wait_recv()
    share_q = first_pair()
    unit_v.start()
    line_down[3].middle()
    line_down[2].back()
    key_unit(unit_k, 0, 1)
    key_unit(unit_k, 0, 0)
    unit_k.across()
    line_down[4].middle()
    line_down[3].back()
    share_one.wait_recv()
    share_q.wait_recv()
    query_unit()
    up_odd.wait_recv()
    up_even.wait_recv()
    for line in line_up:
        line.start()
    normed_part(0)
    unit_v.pass_on()
    unit_k.start()
    line_out.middle()
    line_down[4].back()
    normed_part(1)
    normed_part(2)
    unit_n1.across()
    unit_q.pass_on()
    line_up[0].middle()
    line_out.back()
    to_line(unit_v, 22, line_v)
    mixed = jnp.zeros((128, 768), WIDE)
    for j in range(4):
        rows = s.wdown[8 * j : 8 * j + 8].reshape(768, 768)
        mixed = mixed + dot(s.act[:, 768 * j : 768 * j + 768], rows)
    s.out[...] = (s.middle[...] + mixed + bias_down).astype(LOW)
    out_copy = pltpu.make_async_copy(s.out, out_ref, local.at[6 + LINES])
    out_copy.start()
    line_up[1].middle()
    line_up[0].back()
    unit_k.pass_on()
    unit_n1.start()
    to_line(unit_q, 18, line_q)
    line_up[2].middle()
    to_line(unit_k, 20, *line_k)
    line_up[1].back()
    parts = []
    for i in range(3):
        rows = s.wqkv[256 * i : 256 * i + 256, 0:768]
        parts.append(dot_rows(s.dq2[0:128, :], rows))
    d_normed = jnp.concatenate(parts, axis=1)
    line_up[3].middle()
    line_up[2].back()
    unit_n1.pass_on()
    line_v.middle()
    line_up[3].back()
    d_normed = d_normed + jnp.concatenate([unit_n1.finish(0), unit_n1.finish(1)], axis=1)
    unit_one, scale_one = norm_parts(x_ref[...].astype(WIDE))
    s.small[0:1, :] = column_sum(d_normed * unit_one)
    s.small[1:2, :] = column_sum(d_normed)
    s.small[2:3, :] = column_sum(s.dq2[0:128, :])
    s.small[3:4, :] = column_sum(s.dkv[:, 768:1536])
    d_inputs = s.d_mid[...] + norm_back(d_normed, unit_one, scale_one, gain_one)
    s.grad[...] = d_inputs.astype(LOW)
    grad_copy = pltpu.make_async_copy(s.grad, grad_ref, local.at[7 + LINES])
    grad_copy.start()

    s.pieces[...] = jnp.zeros((8, 16, 128), WIDE)
    for j in range(8):
        s.pieces[j, 0:8, 0:96] = s.small[:, 96 * j : 96 * j + 96]
        for i in range(3):
            s.pieces[j, 8 + i : 9 + i, :] = s.wide[j : j + 1, 128 * i : 128 * i + 128]
    piece_copy = send_all(
        [(s.pieces.at[place(r)], s.pieces_got.at[r], near(r)) for r in range(1, 8)],
        s.pieces_got.at[pl.ds(1, 7)],
    )
    line_q.middle()
    line_v.back()
    line_k[0].middle()
    line_k[1].middle()
    line_k[2].middle()
    line_q.back()
    piece_copy.wait_recv()
    total = s.pieces[me]
    for r in range(1, 8):
        total = total + s.pieces_got[r]
    s.rows_z[dp] = total
    z_copy = send_all(
        [(s.rows_z.at[dp], s.rows_z.at[dp], device) for device in others_z],
        s.rows_z.at[pl.ds(0, 3)],
    )
    line_k[0].back()
    line_k[1].back()
    line_k[2].back()
    for line in line_down + [line_out] + line_up:
        line.write()
    line_v.write()
    line_q.write()
    z_copy.wait_recv()
    small_ref[...] = s.rows_z[0] + s.rows_z[1] + s.rows_z[2] + s.rows_z[3]
    for line in line_k:
        line.write()
    out_copy.wait()
    grad_copy.wait()
    for line in lines:
        line.close()
    for copy in ring:
        if copy is not None:
            copy.wait_send()


def spread_kernel(total_ref, small_ref, out_in, grad_in, out_ref, grad_ref, *outs):
    gain_one, shift_one, qkv, bias_q, bias_v, out, bias_out = outs[:7]
    gain_two, shift_two, up, bias_up, down, bias_down = outs[7:]
    out_ref[...] = out_in[...]
    grad_ref[...] = grad_in[...]
    for i in range(2):
        cols = slice(384 * i, 384 * i + 384)
        for j in range(4):
            down[96 * j : 96 * j + 96, cols] = total_ref[2 * j + i].astype(WIDE)
        out[:, cols] = total_ref[8 + i].astype(WIDE)
    for j in range(8):
        up[:, 384 * j : 384 * j + 384] = total_ref[10 + j].astype(WIDE)
    for j in range(6):
        qkv[:, 384 * j : 384 * j + 384] = total_ref[18 + j].astype(WIDE)
    rows = (gain_one, shift_one, bias_q, bias_v, bias_out, gain_two, shift_two, bias_down)
    for j, target in enumerate(rows):
        target[...] = small_ref[j, 0:96]
    for i in range(3):
        bias_up[128 * i : 128 * i + 128] = small_ref[8 + i, :]


def fused_device(
    inputs,
    gain_one,
    shift_one,
    w_qkv,
    bias_q,
    bias_v,
    w_out,
    bias_out,
    gain_two,
    shift_two,
    w_up,
    bias_up,
    w_down,
    bias_down,
    lengths,
    cotangent,
):
    vmem = pl.BlockSpec(memory_space=pltpu.VMEM)
    anywhere = pl.BlockSpec(memory_space=pl.ANY)
    vectors = [gain_one, shift_one, bias_q, bias_v, bias_out, gain_two, shift_two]
    vectors = vectors + [bias_up, bias_down]
    tokens, width = inputs.shape
    layer_out, grad_inputs, total, small = pl.pallas_call(
        layer_kernel,
        out_shape=(
            jax.ShapeDtypeStruct((tokens, width), LOW),
            jax.ShapeDtypeStruct((tokens, width), LOW),
            jax.ShapeDtypeStruct((24, 96, 384), LOW),
            jax.ShapeDtypeStruct((16, 128), WIDE),
        ),
        in_specs=[pl.BlockSpec(memory_space=pltpu.SMEM)] + [vmem] * 11 + [anywhere] * 4,
        out_specs=(anywhere, anywhere, anywhere, vmem),
        scratch_shapes=[pltpu.VMEM(shape, kind) for shape, kind in SCRATCH.values()]
        + [
            pltpu.SemaphoreType.DMA((RING + LINES,)),
            pltpu.SemaphoreType.DMA((LANDINGS,)),
            pltpu.SemaphoreType.DMA((8 + LINES,)),
        ],
        compiler_params=pltpu.CompilerParams(
            collective_id=0, has_side_effects=True, vmem_limit_bytes=VMEM_BYTES
        ),
        name="layer",
    )(lengths, inputs, cotangent, *vectors, w_qkv, w_out, w_up, w_down.reshape(32, 96, width))
    return pl.pallas_call(
        spread_kernel,
        out_shape=tuple(
            jax.ShapeDtypeStruct((tokens, width), LOW) for _ in range(2)
        )
        + tuple(
            jax.ShapeDtypeStruct(shape, WIDE)
            for shape in (
                (96,),
                (96,),
                (96, 2304),
                (96,),
                (96,),
                (96, 768),
                (96,),
                (96,),
                (96,),
                (96, 3072),
                (384,),
                (384, 768),
                (96,),
            )
        ),
        in_specs=[vmem] * 4,
        out_specs=(vmem,) * 15,
        compiler_params=pltpu.CompilerParams(vmem_limit_bytes=VMEM_BYTES),
        name="spread",
    )(total, small, layer_out, grad_inputs)


def per_device(*arguments):
    inputs, w_up = arguments[0], arguments[10]
    fits = (
        lax.axis_size("dp") == 4
        and lax.axis_size("col") == 8
        and inputs.shape == (128, 768)
        and w_up.shape == (768, 3072)
    )
    return fused_device(*arguments) if fits else general_device(*arguments)


def solution(mesh):
    return jax.shard_map(
        per_device,
        mesh=mesh,
        in_specs=(
            P(("dp", "col"), None),
            P(),
            P(),
            P(),
            P(),
            P(),
            P(),
            P(),
            P(),
            P(),
            P(),
            P(),
            P(),
            P(),
            P("dp", None),
            P(("dp", "col"), None),
        ),
        out_specs=(
            P(("dp", "col"), None),
            P(("dp", "col"), None),
            P("col"),
            P("col"),
            P("col", None),
            P("col"),
            P("col"),
            P("col", None),
            P("col"),
            P("col"),
            P("col"),
            P("col", None),
            P("col"),
            P("col", None),
            P("col"),
        ),
        check_vma=False,
    )
```
